128 devices in a mesh: seq: 8 (over z, core), tp: 16 (over x, y).
Axes of the slice: x: 4, y: 4, z: 4, core: 2. Of those that a mesh axis runs over, the one named last changes fastest.
Arguments:
- hidden: bfloat16 [1024, 4096], P('seq', 'tp'), may hold values from -20 to 20
- text_gain: bfloat16 [4096], P('tp'), may hold values from 0.2 to 4
- text_table: bfloat16 [16000, 4096], P('tp'), may hold values from -0.5 to 0.5
- proj: bfloat16 [8, 4096, 1024], P(None, 'tp'), may hold values from -0.09375 to 0.09375
- audio_table: bfloat16 [8, 2048, 1024], P(None, 'tp'), may hold values from -0.75 to 0.75
- depth_gain: bfloat16 [1024], replicated, may hold values from 0.5 to 1.5
- attn_qkv: bfloat16 [1024, 3, 1024], P(None, None, 'tp'), may hold values from -0.1875 to 0.1875
- attn_out: bfloat16 [1024, 1024], P('tp'), may hold values from -0.1875 to 0.1875
- text_ids: int32 [1024], P('seq'), may hold values from 0 to 15999
- audio_ids: int32 [1024, 8], P('seq'), may hold values from 0 to 2047
Outputs:
- losses: float32 [1024, 9], P('seq')
- grad_hidden: float32 [1024, 4096], P('seq', 'tp')
- grad_text_gain: float32 [4096], P('tp')
- grad_text_table: float32 [4096, 16000], P('seq', 'tp')
- grad_proj: float32 [8, 4096, 1024], P(None, 'tp', 'seq')
- grad_audio_table: float32 [8, 2048, 1024], P(None, 'tp', 'seq')
- grad_depth_gain: float32 [1024], replicated
- grad_attn_qkv: float32 [1024, 3, 1024], P('seq', None, 'tp')
- grad_attn_out: float32 [1024, 1024], P('tp', 'seq')
The draws below stay inside these ranges and needn't reach their ends.
All inputs are finite; a program needn't handle non-finite values.
Results may differ from the reference program's by a relative error of at most 0.022.
Values may be sent and summed in bfloat16 or wider, within the bound.
A program may use at most 128 MiB of HBM per device.

```python
import math
import jax
import jax.numpy as jnp
import numpy as np
from jax import lax

D = 4096
DD = 1024
K = 8
VA = 2048
VT = 16000
FRAME_SEQ = 128
HEAD = 64
FRAMES = 1024
N_SEQ = 8


def feature_ramp(low, high):
    position = jnp.arange(D, dtype=jnp.float32) / (D - 1)
    return low * jnp.exp(position * jnp.log(high / low))


def draw_hidden(key, part):
    key = jax.random.fold_in(key, 11)
    values = jnp.clip(jax.random.normal(key, (FRAMES, D), jnp.float32), -6.0, 6.0)
    ramp = feature_ramp(0.5, 2.0)
    return (values * ramp[None, :]).astype(jnp.bfloat16)


def draw_text_gain(key, part):
    key = jax.random.fold_in(key, 23)
    noise = 1.0 + 0.1 * jnp.clip(jax.random.normal(key, (D,), jnp.float32), -4.0, 4.0)
    ramp = feature_ramp(0.6, 1.8)
    return (noise * ramp).astype(jnp.bfloat16)


def touch_ends(entries, rng, low, top_value):
    longest = entries.shape.index(max(entries.shape))
    spots = []
    for shift in (0, 1):
        where = [jax.random.randint(jax.random.fold_in(rng, axis), (), 0, length) for axis, length in enumerate(entries.shape)]
        where[longest] = (where[longest] + shift) % entries.shape[longest]
        spots.append(tuple(where))
    return entries.at[spots[0]].set(low).at[spots[1]].set(top_value)


def levels(stream_key, extent, split, low, high):
    level = 1.0
    for axis_at, parts in split:
        heights = jax.random.uniform(jax.random.fold_in(jax.random.fold_in(stream_key, 6), axis_at), (parts,), jnp.float32, low / len(split), high / len(split))
        level = level * jnp.repeat(jnp.exp(heights), extent[axis_at] // parts).reshape((-1,) + (1,) * (len(extent) - 1 - axis_at))
    return level


def rank_table(amount, lean):
    weights = [(1 << 20) // math.isqrt(grade ** lean) + 1 for grade in range(1, amount + 1)]
    spread = 1 + sum(weights) // (1 << 30)
    return np.cumsum(np.array([max(1, weight // spread) for weight in weights]))


def ranked(rng, dims, number_of, skew):
    listing = rank_table(number_of, skew)
    pick = jax.random.randint(jax.random.fold_in(rng, 1), dims, 0, int(listing[number_of - 1]))
    standing = jnp.searchsorted(jnp.asarray(listing, jnp.int32), pick, side="right")
    return jax.random.permutation(jax.random.fold_in(rng, 2), number_of)[standing].astype(jnp.int32)


def scatter_about(rng, dims, spread, bound, cuts=(), held_as=jnp.bfloat16):
    entries = jax.random.normal(rng, dims, jnp.float32) * spread
    if len(cuts) > 0:
        entries = levels(rng, dims, cuts, -0.22, 0.18) * entries
    return jnp.clip(entries, min=-bound, max=bound).astype(held_as)


def setup_inputs(seed: int = 0) -> dict:
    key_of = jax.random.split(jax.random.key(seed), 11)
    hidden = draw_hidden(jax.random.fold_in(key_of[10], 71), 0)
    text_gain = draw_text_gain(jax.random.fold_in(key_of[10], 71), 0)
    text_table = scatter_about(key_of[2], (VT, D), (D // 32) ** -0.5, 0.5, ((0, 16),))
    proj = scatter_about(key_of[3], (K, D, DD), D ** -0.5, 0.09375, ((1, 16),))
    audio_table = scatter_about(key_of[4], (K, VA, DD), (DD // 16) ** -0.5, 0.75, ((1, 16),))
    depth_gain = jnp.clip(1.0 + 0.1 * jax.random.normal(key_of[5], (DD,), jnp.float32), 0.5, 1.5).astype(jnp.bfloat16)
    attn_qkv = scatter_about(key_of[6], (DD, 3, DD), DD ** -0.5, 0.1875, ((2, 16),))
    attn_out = scatter_about(key_of[7], (DD, DD), DD ** -0.5, 0.1875, ((0, 16),))
    text_ids = touch_ends(ranked(key_of[8], (FRAMES,), VT, 2), jax.random.fold_in(key_of[8], 3), 0, VT - 1).astype(jnp.int32)
    audio_ids = touch_ends(ranked(key_of[9], (FRAMES, K), VA, 2), jax.random.fold_in(key_of[9], 3), 0, VA - 1).astype(jnp.int32)
    return dict(hidden=hidden, text_gain=text_gain, text_table=text_table, proj=proj, audio_table=audio_table, depth_gain=depth_gain, attn_qkv=attn_qkv, attn_out=attn_out, text_ids=text_ids, audio_ids=audio_ids)


soft_cap = 12.0
epsilon = 1e-05

def capped(values):
    return soft_cap * jnp.tanh(values / soft_cap)

def cap_slope(capped_values):
    ratio = capped_values / soft_cap
    return 1.0 - ratio * ratio

def to_bfloat(values):
    return lax.optimization_barrier(values.astype(jnp.bfloat16))

def attend(triple):
    frames = triple.shape[0]
    steps = triple.shape[1]
    width = triple.shape[3]
    heads = width // HEAD
    grid = triple.astype(jnp.float32).reshape(frames, steps, 3, heads, HEAD)
    scores = jnp.einsum('fihc,fjhc->fhij', grid[:, :, 0], grid[:, :, 1]) / math.sqrt(HEAD)
    causal = jnp.arange(steps)[:, None] >= jnp.arange(steps)[None, :]
    raised = jnp.where(causal, jnp.exp(scores), 0.0)
    weights = lax.optimization_barrier((raised / lax.optimization_barrier(jnp.sum(raised, axis=3, keepdims=True))).astype(jnp.bfloat16))
    mixed = jnp.einsum('fhij,fjhc->fihc', weights.astype(jnp.float32), grid[:, :, 2])
    return mixed.reshape(frames, steps, width).astype(jnp.bfloat16)

def reference(hidden, text_gain, text_table, proj, audio_table, depth_gain, attn_qkv, attn_out, text_ids, audio_ids):
    hidden_float = hidden.astype(jnp.float32)
    row_scale = lax.rsqrt(lax.optimization_barrier(jnp.mean(hidden_float * hidden_float, axis=1, keepdims=True)) + epsilon)
    hidden_hat = hidden_float * row_scale
    normed = to_bfloat(hidden_hat * text_gain.astype(jnp.float32))
    normed_float = normed.astype(jnp.float32)
    text_logits = capped(jnp.dot(normed, text_table.T, preferred_element_type=jnp.float32))
    text_lse = soft_cap + jnp.log(lax.optimization_barrier(jnp.sum(jnp.exp(text_logits - soft_cap), axis=1)))
    text_hot = text_ids[:, None] == jnp.arange(VT)[None, :]
    text_pick = lax.optimization_barrier(jnp.sum(jnp.where(text_hot, text_logits, 0.0), axis=1))
    embed_scale = math.sqrt(DD) / 4.0
    depth_input = jnp.einsum('fd,kde->fke', normed_float, proj.astype(jnp.float32))
    looked = audio_table[jnp.arange(K)[None, :], audio_ids].astype(jnp.float32) * embed_scale
    zeros_row = jnp.zeros((FRAMES, 1, DD), jnp.float32)
    depth_input = depth_input + jnp.concatenate([zeros_row, looked[:, :-1]], axis=1)
    depth_scale = lax.rsqrt(lax.optimization_barrier(jnp.mean(depth_input * depth_input, axis=2, keepdims=True)) + epsilon)
    depth_hat = depth_input * depth_scale
    depth_normed = to_bfloat(depth_hat * depth_gain.astype(jnp.float32))
    triple = to_bfloat(jnp.einsum('fke,ecg->fkcg', depth_normed.astype(jnp.float32), attn_qkv.astype(jnp.float32)))
    attended, attend_back = jax.vjp(attend, triple)
    attended = lax.optimization_barrier(attended)
    depth_output = depth_input + jnp.einsum('fkg,ge->fke', attended.astype(jnp.float32), attn_out.astype(jnp.float32))
    output_b = to_bfloat(depth_output)
    audio_logits = capped(jnp.einsum('fke,kve->fkv', output_b.astype(jnp.float32), audio_table.astype(jnp.float32)))
    audio_lse = soft_cap + jnp.log(lax.optimization_barrier(jnp.sum(jnp.exp(audio_logits - soft_cap), axis=2)))
    audio_hot = audio_ids[:, :, None] == jnp.arange(VA)[None, None, :]
    audio_pick = lax.optimization_barrier(jnp.sum(jnp.where(audio_hot, audio_logits, 0.0), axis=2))
    losses = jnp.concatenate([(text_lse - text_pick)[:, None], audio_lse - audio_pick], axis=1)
    text_prob = jnp.exp(text_logits - text_lse[:, None])
    text_grad = to_bfloat((text_prob - text_hot.astype(jnp.float32)) * cap_slope(text_logits))
    feature_back = jnp.dot(text_grad, text_table, preferred_element_type=jnp.float32)
    grad_text_table = jnp.dot(normed.T, text_grad, preferred_element_type=jnp.float32)
    audio_prob = jnp.exp(audio_logits - audio_lse[:, :, None])
    audio_grad = to_bfloat((audio_prob - audio_hot.astype(jnp.float32)) * cap_slope(audio_logits))
    output_back = jnp.einsum('fkv,kve->fke', audio_grad.astype(jnp.float32), audio_table.astype(jnp.float32))
    output_back_b = to_bfloat(output_back)
    attended_back = jnp.einsum('fke,ge->fkg', output_back_b.astype(jnp.float32), attn_out.astype(jnp.float32)).astype(jnp.bfloat16)
    triple_back = lax.optimization_barrier(attend_back(attended_back)[0])
    normed_back = jnp.einsum('fkcg,ecg->fke', triple_back.astype(jnp.float32), attn_qkv.astype(jnp.float32))
    grad_depth_gain = lax.optimization_barrier(jnp.sum(normed_back * depth_hat, axis=(0, 1)))
    hat_back = normed_back * depth_gain.astype(jnp.float32)
    input_back = output_back + depth_scale * (hat_back - depth_hat * lax.optimization_barrier(jnp.mean(hat_back * depth_hat, axis=2, keepdims=True)))
    input_back_b = to_bfloat(input_back)
    feature_back = feature_back + jnp.einsum('fke,kde->fd', input_back_b.astype(jnp.float32), proj.astype(jnp.float32))
    gain_back = feature_back * text_gain.astype(jnp.float32)
    grad_hidden = row_scale * (gain_back - hidden_hat * lax.optimization_barrier(jnp.mean(gain_back * hidden_hat, axis=1, keepdims=True)))
    grad_text_gain = lax.optimization_barrier(jnp.sum(feature_back * hidden_hat, axis=0))
    lookup_back = jnp.concatenate([input_back[:, 1:] * embed_scale, zeros_row], axis=1)
    grad_proj = jnp.zeros((K, D, DD), jnp.float32)
    grad_audio_table = jnp.zeros((K, VA, DD), jnp.float32)
    grad_attn_qkv = jnp.zeros((DD, 3, DD), jnp.float32)
    grad_attn_out = jnp.zeros((DD, DD), jnp.float32)
    for group in range(N_SEQ):
        low = group * FRAME_SEQ
        high = low + FRAME_SEQ
        proj_term = jnp.einsum('fd,fke->kde', normed_float[low:high], input_back_b[low:high].astype(jnp.float32))
        table_term = jnp.einsum('fkv,fke->kve', audio_grad[low:high].astype(jnp.float32), output_b[low:high].astype(jnp.float32))
        table_term = table_term + jnp.einsum('fkv,fke->kve', audio_hot[low:high].astype(jnp.float32), lookup_back[low:high], precision=lax.Precision.HIGHEST)
        qkv_term = jnp.einsum('fke,fkcg->ecg', depth_normed[low:high].astype(jnp.float32), triple_back[low:high].astype(jnp.float32))
        out_term = jnp.einsum('fkg,fke->ge', attended[low:high].astype(jnp.float32), output_back_b[low:high].astype(jnp.float32))
        grad_proj = grad_proj + to_bfloat(proj_term).astype(jnp.float32)
        grad_audio_table = grad_audio_table + to_bfloat(table_term).astype(jnp.float32)
        grad_attn_qkv = grad_attn_qkv + to_bfloat(qkv_term).astype(jnp.float32)
        grad_attn_out = grad_attn_out + to_bfloat(out_term).astype(jnp.float32)
    return (losses, grad_hidden, grad_text_gain, grad_text_table, grad_proj, grad_audio_table, grad_depth_gain, grad_attn_qkv, grad_attn_out)
```

```python
import math

import jax
import jax.numpy as jnp
from jax import lax
from jax.experimental import pallas as pl
from jax.experimental.pallas import tpu as pltpu
from jax.sharding import Mesh
from jax.sharding import PartitionSpec as P

D = 4096
DD = 1024
HEAD = 64
VOCAB = 1000
MESH = pl.DeviceIdType.MESH
VMEM_LIMIT = 62 * 1024 * 1024

soft_cap = 12.0
epsilon = 1e-05
embed_scale = math.sqrt(DD) / 4.0
f32 = jnp.float32
bf16 = jnp.bfloat16

NN = (((1,), (0,)), ((), ()))
NT = (((1,), (1,)), ((), ()))
TN = (((0,), (0,)), ((), ()))


def dot(a, b, dims=NN):
    return lax.dot_general(a, b, dims, preferred_element_type=f32)


def capped(values):
    return soft_cap * jnp.tanh(values / soft_cap)


def cap_slope(capped_values):
    ratio = capped_values / soft_cap
    return 1.0 - ratio * ratio


class Place:
    def __init__(self):
        self.z = lax.axis_index("z")
        self.c = lax.axis_index("core")
        self.x = lax.axis_index("x")
        self.y = lax.axis_index("y")
        self.s = self.z * 2 + self.c
        self.t = self.x * 4 + self.y

    def ring(self, axis):
        me = {"x": self.x, "y": self.y, "z": self.z}[axis]
        return me, lax.rem(me + 1, 4), lax.rem(me + 2, 4), lax.rem(me + 3, 4)

    def xp(self, d):
        to = lax.rem(self.x + d, 4)
        return to, {"x": to}

    def yp(self, d):
        to = lax.rem(self.y + d, 4)
        return to, {"y": to}

    def sp(self, d):
        to = lax.rem(self.s + d, 8)
        return to, {"z": lax.div(to, 2), "core": lax.rem(to, 2)}

    def tp(self, d):
        to = lax.rem(self.t + d, 16)
        return to, {"x": lax.div(to, 4), "y": lax.rem(to, 4)}

    def sibling(self):
        return {"core": 1 - self.c}


class Sends:
    def __init__(self, at):
        self.at = at
        self.pending = []

    def go(self, src, dst, send, recv, device):
        pltpu.make_async_remote_copy(
            src_ref=src, dst_ref=dst, send_sem=send, recv_sem=recv, device_id=device, device_id_type=MESH
        ).start()

    def bytes_of(self, ref, sem):
        return pltpu.make_async_remote_copy(
            src_ref=ref, dst_ref=ref, send_sem=sem, recv_sem=sem,
            device_id=self.at.sibling(), device_id_type=MESH,
        )

    def sent_later(self, ref, sem):
        self.pending.append(self.bytes_of(ref, sem))

    def one(self, src, dst, sems, device):
        self.go(src, dst, sems.at[0], sems.at[1], device)
        self.sent_later(src, sems.at[0])
        return self.bytes_of(dst, sems.at[1])

    def spread(self, peer, n, src, dst, sems, slots, all_bytes=None):
        for d in range(1, n):
            to, device = peer(d)
            self.go(src(to), dst, sems.at[0], sems.at[1], device)
        if all_bytes is None:
            all_bytes = slots.at[pl.ds(0, n - 1)]
        self.sent_later(all_bytes, sems.at[0])
        return self.bytes_of(all_bytes, sems.at[1])

    def finish(self):
        for wait in self.pending:
            wait.wait_send()


class RingGather:
    def __init__(self, out, at, axis, part, slots, sems):
        self.out, self.part, self.sems, self.slots = out, part, sems, slots
        me, self.right, far, self.left = at.ring(axis)
        self.to_right, self.to_left = {axis: self.right}, {axis: self.left}
        block = part(me, None)
        out.go(block, block, sems.at[0], sems.at[1], self.to_right)
        out.go(block, block, sems.at[0], sems.at[2], self.to_left)
        out.sent_later(slots(3), sems.at[0])

    def forward(self):
        out, part, sems = self.out, self.part, self.sems
        out.bytes_of(part(self.left, None), sems.at[1]).wait_recv()
        one = part(self.left, 0)
        out.go(one, one, sems.at[0], sems.at[3], self.to_right)
        out.bytes_of(part(self.right, None), sems.at[2]).wait_recv()
        two = part(self.right, 1)
        out.go(two, two, sems.at[0], sems.at[3], self.to_left)

    def finish(self):
        self.out.bytes_of(self.slots(1), self.sems.at[3]).wait_recv()


class RingReduce:
    def __init__(self, out, at, axis, blocks, half, bufs, sems):
        self.out, self.half, self.sems, self.blocks = out, half, sems, blocks
        self.me, self.right, far, self.left = at.ring(axis)
        self.rl, self.rr, self.fa, self.fb = bufs
        self.to_right, self.to_left = {axis: self.right}, {axis: self.left}
        s = blocks
        out.go(half(s.at[far], 0), self.fa, sems.at[0], sems.at[1], self.to_right)
        out.go(half(s.at[far], 1), self.fb, sems.at[0], sems.at[2], self.to_left)
        out.go(half(s.at[self.right], 1), half(self.rl, 1), sems.at[0], sems.at[3], self.to_right)
        out.go(half(s.at[self.left], 0), half(self.rr, 0), sems.at[0], sems.at[3], self.to_left)
        out.sent_later(s.at[pl.ds(0, 3)], sems.at[0])

    def forward(self):
        s, half, out, sems = self.blocks, self.half, self.out, self.sems
        out.bytes_of(self.fa, sems.at[1]).wait_recv()
        one = half(s.at[self.right], 0)
        one[...] = (one[...].astype(f32) + self.fa[...].astype(f32)).astype(bf16)
        out.go(one, half(self.rl, 0), sems.at[0], sems.at[3], self.to_right)
        out.bytes_of(self.fb, sems.at[2]).wait_recv()
        two = half(s.at[self.left], 1)
        two[...] = (two[...].astype(f32) + self.fb[...].astype(f32)).astype(bf16)
        out.go(two, half(self.rr, 1), sems.at[0], sems.at[3], self.to_left)

    def finish(self):
        self.out.bytes_of(self.blocks.at[pl.ds(0, 2)], self.sems.at[3]).wait_recv()

    def total(self, pick=lambda ref: ref[...]):
        own = pick(self.blocks.at[self.me]).astype(f32)
        return own + pick(self.rl).astype(f32) + pick(self.rr).astype(f32)


class DirectReduce:
    def __init__(self, out, at, axis, blocks, got, sems):
        self.blocks, self.got = blocks, got
        self.me = at.ring(axis)[0]
        for d in (2, 1, 3):
            to = lax.rem(self.me + d, 4)
            out.go(blocks.at[to], got.at[d - 1], sems.at[0], sems.at[1], {axis: to})
        out.sent_later(blocks.at[pl.ds(0, 3)], sems.at[0])
        self.wait = out.bytes_of(got, sems.at[1])

    def finish(self):
        self.wait.wait_recv()

    def total(self, pick=lambda ref: ref[...]):
        own = pick(self.blocks.at[self.me]).astype(f32)
        for d in range(3):
            own = own + pick(self.got.at[d]).astype(f32)
        return own


def span(h, size):
    if h is None:
        return pl.ds(0, size)
    return pl.ds(h * (size // 2), size // 2)


def rows_half(n):
    return lambda ref, h: ref.at[pl.ds(h * n, n)]


def row_to_col(row, lanes):
    return jnp.broadcast_to(row, (lanes, row.shape[1])).T


def twice(col):
    return jnp.concatenate([col, col], axis=1)


def fold(rows, n):
    w = rows.shape[1] // n
    return jnp.concatenate([rows[:, i * w : i * w + w] for i in range(n)], axis=0).astype(bf16)


def unfold(packed, n):
    r = packed.shape[0] // n
    wide = packed.astype(f32)
    return jnp.concatenate([wide[i * r : i * r + r] for i in range(n)], axis=1)


def by_step(rows):
    return [fold(rows[4 * k : 4 * k + 4], 4) for k in range(8)]


def from_steps(ref):
    return jnp.concatenate([unfold(ref[k], 4) for k in range(8)], axis=0)


def head_masks(rows):
    lane = lax.broadcasted_iota(jnp.int32, (rows, 256), 1)
    return [(lane >= 64 * h) & (lane < 64 * h + 64) for h in range(4)]


def step_mask():
    i = lax.broadcasted_iota(jnp.int32, (128, 128), 0)
    j = lax.broadcasted_iota(jnp.int32, (128, 128), 1)
    return ((i & 3) == (j & 3)) & ((i >> 5) == (j >> 5)) & (j <= i)


def attention(qh, kk, allowed):
    scores = dot(qh, kk, NT) / math.sqrt(HEAD)
    raised = jnp.where(allowed, jnp.exp(scores), 0.0)
    return raised / jnp.sum(raised, axis=1, keepdims=True)


def ring_reduce_scratch(name, block, half):
    return [
        (name + "_s", (4,) + block, bf16),
        (name + "_rl", block, bf16),
        (name + "_rr", block, bf16),
        (name + "_fa", half, bf16),
        (name + "_fb", half, bf16),
        (name + "_m", 4, None),
    ]


def direct_scratch(name, block):
    return [(name + "_s", (4,) + block, bf16), (name + "_r", (3,) + block, bf16), (name + "_m", 2, None)]


def chain_scratch(m):
    m = str(m)
    return [
        *ring_reduce_scratch("p" + m, (4, 16, DD), (2, 16, DD)),
        *ring_reduce_scratch("q" + m, (4, 16, DD), (2, 16, DD)),
        *direct_scratch("pp" + m, (16, DD)),
        *direct_scratch("qq" + m, (16, DD)),
        ("dn_m" + m, 2, None),
        *direct_scratch("h" + m, (32, DD)),
        ("a1s" + m, (8, 16, 256), bf16), ("a1r" + m, (8, 16, 256), bf16), ("a1_m" + m, 2, None),
        ("a2s" + m, (8, 16, 256), bf16), ("a2r" + m, (8, 16, 256), bf16), ("a2_m" + m, 2, None),
        ("a3s" + m, (8, 16, 256), bf16), ("a3r" + m, (8, 16, 256), bf16), ("a3_m" + m, 2, None),
        ("ob_m" + m, 2, None), ("e" + m, (4, 8, 128), f32), ("e_m" + m, 2, None),
        *direct_scratch("v" + m, (32, DD)),
        *direct_scratch("c" + m, (32, DD)),
        ("obb_m" + m, 2, None),
    ]


SCRATCH = [
    ("tt", (VOCAB, D), bf16), ("pj", (8, 256, DD), bf16), ("au", (8, 128, DD), bf16), ("load", 3, 0),
    ("ssq", (16, 8, 128), f32), ("ssq_m", 2, None),
    ("idb", (8, 8, 128), jnp.int32), ("idb_m", 2, None), ("idr", (2, 1, 1024), jnp.int32),
    ("raw", (8, 128, DD), f32), ("look", (8, 128, DD), bf16),
    ("wb", (4, 4, 64, DD), bf16), ("wb_m", 4, None), ("wz_m", 4, None), ("wc_m", 2, None),
    ("nb", (4, 4, 128, 256), bf16), ("ny_m", 4, None), ("nx_m", 4, None),
    ("ns", (4, 2, 16, 16, 128), bf16), ("nz_m", 4, None), ("nc_m", 2, None),
    *chain_scratch(0), *chain_scratch(1),
    ("dob", (2, 2, 4, 32, DD), bf16), ("qkv", (2, 3, 128, 256), bf16),
    ("ex", (2, 4, 128, 128), f32), ("ob", (2, 4, 32, DD), bf16),
    ("gr", (2, 128, 512), bf16), ("tri", (2, 4, 128, 256), bf16),
    ("tab", (4, 128, DD), bf16), ("tab_m", 4, None),
    ("tl", (128, VOCAB), f32), ("ts", (16, 8, 128), f32), ("ts_m", 2, None), ("tgr", (128, VOCAB), bf16),
    *ring_reduce_scratch("g", (128, DD), (64, DD)),
    ("lc", (8, 2, 16, 128), f32), ("lr", (8, 2, 16, 128), f32), ("lc_m", 2, None),
    ("lx", (4, 2, 16, 128), f32), ("lx_m", 2, None), ("tlc", (128, 128), f32),
    ("nt", (256, 1024), bf16), ("tg", (4, 2, 1024, 128), bf16), ("tgz_m", 4, None), ("tgc_m", 2, None),
    *ring_reduce_scratch("t", (4, 128, 256), (2, 128, 256)),
    *ring_reduce_scratch("t2", (128, 256), (64, 256)),
    ("ndst", (8, 2, 128, 256), bf16), ("nd_m", 2, None),
    ("ib", (2, 4, 4, 32, DD), bf16), ("i0x_m", 2, None), ("i0y_m", 4, None),
    ("iax_m", 2, None), ("iay_m", 4, None), ("ibx_m", 4, None), ("iby_m", 2, None),
    ("gas", (2, 4, 4, 64, 512), bf16), ("gar", (4, 4, 64, 512), bf16), ("gar_m", 2, None),
    *ring_reduce_scratch("ga", (4, 64, 512), (2, 64, 512)),
    *direct_scratch("gz", (4, 64, 128)),
    ("sf", (2, 4, 128, 256), bf16), ("sfr", (4, 128, 256), bf16), ("sfr_m", 2, None),
    *direct_scratch("f", (128, 256)),
    ("gps", (8, 256, 128), bf16), ("gpr", (8, 256, 128), bf16), ("gp_m", 2, None),
    ("lks", (8, 128, 128), bf16), ("lkr", (8, 128, 128), bf16), ("lk_m", 2, None),
    ("gts", (8, 128, 128), bf16), ("gtr", (8, 128, 128), bf16), ("gt_m", 2, None),
    ("dgs", (8, 8, 128), f32), ("dgs_m", 2, None), ("dgt", (16, 8, 128), f32), ("dgt_m", 2, None),
    ("rd", (16, 8, 128), f32), ("rd_m", 2, None), ("tgn", (8, 8, 256), f32), ("tgn_m", 2, None),
]


def scratch_shape(entry):
    name, shape, dtype = entry
    if dtype is None or isinstance(dtype, int):
        return pltpu.SemaphoreType.DMA((shape,))
    return pltpu.VMEM(shape, dtype)


class Named:
    pass


def loop(low, high, body):
    def one(i, carry):
        body(i)
        return carry

    lax.fori_loop(low, high, one, 0)


INPUTS = ["hid", "gain", "table", "proj", "audio", "dgain", "wqkv", "wout", "tid", "ids"]
OUTPUTS = ["o_loss", "o_gh", "o_tgain", "o_gtt", "o_gp", "o_gtab", "o_dg", "o_gqkv", "o_gout"]


def kernel(*refs):
    n = Named()
    names = INPUTS + OUTPUTS + [entry[0] for entry in SCRATCH]
    for name, ref in zip(names, refs):
        setattr(n, name, ref)
    at = Place()
    out = Sends(at)

    def reduce(axis, name, half):
        bufs = [getattr(n, name + suffix) for suffix in ("_rl", "_rr", "_fa", "_fb")]
        return RingReduce(out, at, axis, getattr(n, name + "_s"), half, bufs, getattr(n, name + "_m"))

    def direct(axis, name):
        return DirectReduce(
            out, at, axis, getattr(n, name + "_s"), getattr(n, name + "_r"), getattr(n, name + "_m")
        )

    def seq_all(src, dst, sems):
        return out.spread(at.sp, 8, lambda to: src.at[to], dst.at[at.s], sems, dst)

    def seq_same(ref, sems):
        return out.spread(at.sp, 8, lambda to: ref.at[at.s], ref.at[at.s], sems, ref)

    def plane_same(ref, sems):
        return out.spread(at.tp, 16, lambda to: ref.at[at.t], ref.at[at.t], sems, ref)

    def x_same(ref, sems):
        return out.spread(at.xp, 4, lambda to: ref.at[at.x], ref.at[at.x], sems, ref)

    def y_same(ref, sems):
        return out.spread(at.yp, 4, lambda to: ref.at[at.y], ref.at[at.y], sems, ref)

    loads = [
        pltpu.make_async_copy(src, dst, n.load.at[i])
        for i, (src, dst) in enumerate([(n.proj, n.pj), (n.audio, n.au), (n.table, n.tt)])
    ]
    for copy in loads:
        copy.start()
    for c in range(3):
        n.wb[at.x, c] = n.wqkv[c]
    n.wb[at.x, 3] = n.wout[...]
    barrier = pltpu.get_barrier_semaphore()
    for d in range(1, 16):
        pl.semaphore_signal(barrier, inc=1, device_id=at.tp(d)[1], device_id_type=MESH)
    for d in range(1, 8):
        pl.semaphore_signal(barrier, inc=1, device_id=at.sp(d)[1], device_id_type=MESH)
    h = n.hid[...].astype(f32)
    gain = n.gain[...].astype(f32)[None, :]
    dgain = n.dgain[...].astype(f32)[None, :]
    ones = jnp.ones((8, 256), f32)
    n.ssq[at.t] = lax.dot_general(
        ones, h * h, NT, precision=lax.Precision.HIGHEST, preferred_element_type=f32
    )
    n.idb[at.s] = n.ids[...]
    unscaled = (h * gain).astype(bf16)
    pl.semaphore_wait(barrier, 22)

    got_ssq = plane_same(n.ssq, n.ssq_m)
    mine = pl.ds(pl.multiple_of(at.c * 32, 32), 32)
    weights = RingGather(
        out, at, "x",
        lambda i, hf: n.wb.at[i, at.z, mine] if hf is None
        else n.wb.at[i, at.z, pl.ds(pl.multiple_of(at.c * 32 + 16 * hf, 16), 16)],
        lambda k: n.wb.at[pl.ds(0, k), at.z, mine],
        n.wb_m,
    )
    got_ids = seq_same(n.idb, n.idb_m)
    loads[0].wait()

    def raw_step(k):
        n.raw[k] = dot(unscaled, n.pj[k])

    loop(0, 8, raw_step)
    loads[1].wait()
    entry = (lax.broadcasted_iota(jnp.int32, (128, 128), 1) + at.t * 128).astype(f32)
    n.look[0] = jnp.zeros((128, DD), bf16)

    def look_step(k):
        column = row_to_col(n.ids[pl.ds(k, 1), :].astype(f32), 128)
        hot = jnp.where(column == entry, 1.0, 0.0).astype(bf16)
        n.look[k + 1] = (dot(hot, n.au[k]) * embed_scale).astype(bf16)

    loop(0, 7, look_step)
    got_ssq.wait_recv()
    scale = row_to_col(lax.rsqrt(jnp.sum(n.ssq[...], axis=0)[0:1, :] / D + epsilon), 128)
    column = scale[:, 0:1]
    scale = twice(scale)
    hat = h * scale

    first = []
    for m in range(2):
        ps, qs = getattr(n, f"p{m}_s"), getattr(n, f"q{m}_s")
        part = slice(64 * m, 64 * m + 64)

        def scaled(k):
            return n.raw[k, part, :] * column[part] + n.look[k, part, :].astype(f32)

        def to_x(k):
            p = scaled(k)
            for b in range(4):
                ps[b, k] = p[16 * b : 16 * b + 16].astype(bf16)

        def to_y(k):
            p = scaled(k + 4)
            for b in range(4):
                rows = [p[16 * a + 4 * b : 16 * a + 4 * b + 4] for a in range(4)]
                qs[b, k] = jnp.concatenate(rows, axis=0).astype(bf16)

        loop(0, 4, to_x)
        red_p = reduce("x", f"p{m}", rows_half(2))
        loop(0, 4, to_y)
        first.append((red_p, reduce("y", f"q{m}", rows_half(2))))
    normed_f = hat * gain
    n.nb[at.x, at.y] = normed_f.astype(bf16)
    for b in range(16):
        n.ns[at.z, at.c, b] = fold(normed_f[8 * b : 8 * b + 8], 2)
    norm_z = RingGather(
        out, at, "z",
        lambda i, hf: n.ns.at[i, at.c, span(hf, 16)],
        lambda k: n.ns.at[pl.ds(0, k), at.c],
        n.nz_m,
    )
    norm_y = RingGather(
        out, at, "y",
        lambda i, hf: n.nb.at[at.x, i, span(hf, 128)],
        lambda k: n.nb.at[at.x, pl.ds(0, k)],
        n.ny_m,
    )

    masks = head_masks(128)
    allowed = step_mask()
    held = [Named(), Named()]

    def wcat(c):
        return jnp.concatenate([n.wb[a, c] for a in range(4)], axis=0)

    def half_of(m, name):
        return getattr(n, name + str(m))

    def chain(m):
        mine = held[m]
        red_p, red_q = first[m]
        red_p.forward()
        red_q.forward()
        yield
        for red, to, axis in ((red_p, "pp", "y"), (red_q, "qq", "x")):
            red.finish()
            total = [red.total(lambda ref: ref[k]) for k in range(4)]
            for b in range(4):
                rows = [total[k][4 * b : 4 * b + 4] for k in range(4)]
                getattr(n, f"{to}{m}_s")[b] = jnp.concatenate(rows, axis=0).astype(bf16)
            if axis == "y":
                red_pp = direct("y", f"pp{m}")
            else:
                red_qq = direct("x", f"qq{m}")
        yield
        red_pp.finish()
        red_qq.finish()
        di = jnp.concatenate([red_pp.total(), red_qq.total()], axis=0)
        mine.dscale = lax.rsqrt(jnp.mean(di * di, axis=1, keepdims=True) + epsilon)
        mine.dhat = di * mine.dscale
        n.dob[0, m, at.y] = (mine.dhat * dgain).astype(bf16)
        got = y_same(n.dob.at[0, m], half_of(m, "dn_m"))
        yield
        got.wait_recv()
        dnv = n.dob[0, m].reshape(128, DD)
        for c in range(3):
            n.qkv[m, c] = dot(dnv, wcat(c), NT).astype(bf16)
        q, k, v = n.qkv[m, 0], n.qkv[m, 1], n.qkv[m, 2]
        mixed = jnp.zeros((128, 256), f32)
        for hd in range(4):
            qh = jnp.where(masks[hd], q, jnp.zeros_like(q))
            exact = attention(qh, k, allowed)
            n.ex[m, hd] = exact
            mixed = jnp.where(masks[hd], dot(exact.astype(bf16), v), mixed)
        n.tri[m, 3] = mixed.astype(bf16)
        terms = dot(n.tri[m, 3], wcat(3))
        for b in range(4):
            getattr(n, f"h{m}_s")[b] = terms[32 * b : 32 * b + 32].astype(bf16)
        red_h = direct("y", f"h{m}")
        yield
        red_h.finish()
        src, dst = half_of(m, "a1s"), half_of(m, "a1r")
        for k, block in enumerate(by_step(di + red_h.total())):
            src[k] = block
        got = seq_all(src, dst, half_of(m, "a1_m"))
        dst[at.s] = src[at.s]
        yield
        got.wait_recv()
        n.ob[m, at.y] = from_steps(dst).astype(bf16)
        got = y_same(n.ob.at[m], half_of(m, "ob_m"))
        yield
        got.wait_recv()
        rows = n.ob[m].reshape(128, DD)
        tab = n.tab[...].reshape(512, DD)
        logits = capped(dot(rows, tab, NT))
        hot = mine.hot
        sums = jnp.sum(jnp.exp(logits - soft_cap), axis=1, keepdims=True)
        chosen = jnp.sum(jnp.where(hot, logits, 0.0), axis=1, keepdims=True)
        lane = lax.broadcasted_iota(jnp.int32, (128, 128), 1)
        packed = jnp.where(lane == 0, sums, jnp.where(lane == 1, chosen, 0.0))
        e = half_of(m, "e")
        e[at.y] = packed.T[0:8, :]
        got = y_same(e, half_of(m, "e_m"))
        yield
        got.wait_recv()
        total = jnp.sum(e[...], axis=0)
        lse_row = soft_cap + jnp.log(total[0:1, :])
        prob = jnp.exp(logits - row_to_col(lse_row, 128)[:, 0:1])
        grad = ((prob - jnp.where(hot, 1.0, 0.0)) * cap_slope(logits)).astype(bf16)
        n.gr[m] = grad
        terms = dot(grad, tab)
        for b in range(4):
            getattr(n, f"v{m}_s")[b] = terms[32 * b : 32 * b + 32].astype(bf16)
        red_v = direct("y", f"v{m}")
        loss = row_to_col(lse_row - total[1:2, :], 128)
        for g in range(8):
            rows = [loss[32 * b + 4 * g : 32 * b + 4 * g + 4] for b in range(4)]
            n.lc[g, m] = jnp.concatenate(rows, axis=0)
        yield
        red_v.finish()
        src, dst = half_of(m, "a2s"), half_of(m, "a2r")
        for k, block in enumerate(by_step(red_v.total())):
            src[k] = block
        got = seq_all(src, dst, half_of(m, "a2_m"))
        dst[at.s] = src[at.s]
        yield
        got.wait_recv()
        output_back = from_steps(dst)
        n.dob[1, m, at.y] = output_back.astype(bf16)
        got = y_same(n.dob.at[1, m], half_of(m, "obb_m"))
        yield
        got.wait_recv()
        g = dot(n.dob[1, m].reshape(128, DD), wcat(3), NT).astype(bf16)
        q, k, v = n.qkv[m, 0], n.qkv[m, 1], n.qkv[m, 2]
        dq = jnp.zeros((128, 256), f32)
        dk = jnp.zeros((128, 256), f32)
        dv = jnp.zeros((128, 256), f32)
        for hd in range(4):
            gh = jnp.where(masks[hd], g, jnp.zeros_like(g))
            exact = n.ex[m, hd]
            dw = dot(gh, v, NT).astype(bf16).astype(f32)
            ds = exact * (dw - jnp.sum(dw * exact, axis=1, keepdims=True)) / math.sqrt(HEAD)
            dv = jnp.where(masks[hd], dot(exact.T.astype(bf16), g), dv)
            dq = jnp.where(masks[hd], dot(ds.astype(bf16), k), dq)
            dk = jnp.where(masks[hd], dot(ds.T.astype(bf16), q), dk)
        n.tri[m, 0] = dq.astype(bf16)
        n.tri[m, 1] = dk.astype(bf16)
        n.tri[m, 2] = dv.astype(bf16)
        terms = dot(n.tri[m, 0], wcat(0)) + dot(n.tri[m, 1], wcat(1)) + dot(n.tri[m, 2], wcat(2))
        for b in range(4):
            getattr(n, f"c{m}_s")[b] = terms[32 * b : 32 * b + 32].astype(bf16)
        red_c = direct("y", f"c{m}")
        yield
        red_c.finish()
        nback = red_c.total()
        mine.gain_term = jnp.sum(nback * mine.dhat, axis=0, keepdims=True)
        hback = nback * dgain
        inner = jnp.mean(hback * mine.dhat, axis=1, keepdims=True)
        ib = output_back + mine.dscale * (hback - mine.dhat * inner)
        src, dst = half_of(m, "a3s"), half_of(m, "a3r")
        for k, block in enumerate(by_step(ib)):
            src[k] = block
        got = seq_all(src, dst, half_of(m, "a3_m"))
        dst[at.s] = src[at.s]
        yield
        got.wait_recv()
        n.ib[m, at.x, at.y] = from_steps(dst).astype(bf16)

        def part(axis, where, sems):
            return RingGather(out, at, axis, where, lambda k: where(pl.ds(0, k), None), sems)

        def spread(peer, mine_is, where, sems):
            src = where(mine_is)
            return out.spread(peer, 4, lambda to: src, src, sems, None, where(pl.ds(0, 3)))

        low, high = pl.ds(0, 16), pl.ds(16, 16)
        ib = n.ib.at[m]
        if m == 0:
            one = [spread(at.xp, at.x, lambda i: ib.at[i, at.y], n.i0x_m)]
        else:
            one = [
                spread(at.xp, at.x, lambda i: ib.at[i, at.y, low], n.iax_m),
                spread(at.yp, at.y, lambda i: ib.at[at.x, i, high], n.iby_m),
            ]
        yield
        one[0].wait_recv()
        if m == 0:
            two = [part("y", lambda i, hf: ib.at[:, i, :, span(hf, DD)], n.i0y_m)]
        else:
            two = [part("y", lambda i, hf: ib.at[:, i, low, span(hf, DD)], n.iay_m)]
            one[1].wait_recv()
            two.append(part("x", lambda i, hf: ib.at[i, :, high, span(hf, DD)], n.ibx_m))
        yield
        for ring in two:
            ring.forward()
        yield
        for ring in two:
            ring.finish()
        yield

    run = [chain(0), chain(1)]

    def step(m):
        next(run[m])

    def text_piece(i):
        feats = jnp.concatenate([n.nb[i // 2, 2 * (i % 2) + b] for b in range(2)], axis=1)
        part = dot(feats, n.tt[:, 512 * i : 512 * i + 512], NT)
        if i == 0:
            n.tl[...] = part
        else:
            n.tl[...] += part

    def text_back(a):
        part = dot(n.tgr[...], n.tt[:, 1024 * a : 1024 * a + 1024])
        for b in range(4):
            n.t_s[a, b] = part[:, 256 * b : 256 * b + 256].astype(bf16)

    weights.forward()
    step(0)
    step(1)
    norm_y.forward()
    weights.finish()
    weights_z = RingGather(
        out, at, "z",
        lambda i, hf: n.wb.at[span(hf, 4), i, mine],
        lambda k: n.wb.at[:, pl.ds(0, k), mine],
        n.wz_m,
    )
    step(0)
    norm_z.forward()
    norm_y.finish()
    norm_x = RingGather(
        out, at, "x", lambda i, hf: n.nb.at[i, span(hf, 4)], lambda k: n.nb.at[pl.ds(0, k)], n.nx_m
    )
    step(1)
    weights_z.forward()
    step(0)
    n.tab[at.x] = n.au[at.s]
    tab_x = RingGather(
        out, at, "x", lambda i, hf: n.tab.at[i, span(hf, 128)], lambda k: n.tab.at[pl.ds(0, k)], n.tab_m
    )
    step(1)
    norm_z.finish()
    share = n.ns.at[:, at.c]
    wait_n = out.one(share, share, n.nc_m, at.sibling())
    weights_z.finish()
    for other in (weights.right, lax.rem(at.x + 2, 4), weights.left):
        part = n.wb.at[other, :, mine]
        out.go(part, part, n.wc_m.at[0], n.wc_m.at[1], at.sibling())
    out.sent_later(n.wb.at[pl.ds(0, 3), :, mine], n.wc_m.at[0])
    wait_w = out.bytes_of(n.wb.at[pl.ds(0, 3), :, mine], n.wc_m.at[1])
    got_ids.wait_recv()
    i = lax.broadcasted_iota(jnp.int32, (128, 1024), 0)
    j = lax.broadcasted_iota(jnp.int32, (128, 1024), 1)
    same = ((i >> 6) == (j >> 9)) & (((i >> 2) & 15) == ((j >> 5) & 15)) & ((i & 3) == (j & 3))
    group = lax.broadcasted_iota(jnp.int32, (8, 1024), 0)
    j = lax.broadcasted_iota(jnp.int32, (8, 1024), 1)
    book = [at.s, jnp.maximum(at.s - 1, 0)]
    ids2 = [jnp.concatenate([n.idb[g, pl.ds(k, 1), :] for g in range(8)], axis=0) for k in book]
    spread = lax.dot_general(
        jnp.concatenate(ids2, axis=0).astype(f32), jnp.where(same, 1.0, 0.0), NN,
        precision=lax.Precision.HIGHEST, preferred_element_type=f32,
    )
    for i in range(2):
        own = jnp.where(((j >> 2) & 7) == group, spread[8 * i : 8 * i + 8], 0.0)
        n.idr[i] = jnp.sum(own, axis=0, keepdims=True).astype(jnp.int32)
    norm_x.forward()
    wait_w.wait_recv()
    step(0)
    step(1)
    wait_n.wait_recv()
    def transposed(b):
        rows = []
        for t in range(4):
            for s in range(8):
                index = 8 * lax.div(b, 4) + 2 * lax.rem(b, 4) + t // 2
                tile = unfold(n.ns[s // 2, s % 2, index], 2)
                rows.append(tile[4 * (t % 2) : 4 * (t % 2) + 4])
        cols = pl.ds(pl.multiple_of(128 * b, 128), 128)
        n.nt[:, cols] = jnp.concatenate(rows, axis=0).T.astype(bf16)

    loop(0, 8, transposed)
    step(0)
    tab_x.forward()
    step(1)
    norm_x.finish()
    loads[2].wait()
    text_piece(0)
    text_piece(1)
    step(0)
    text_piece(2)
    step(1)
    def two_blocks(to):
        return n.nb.at[lax.div(to, 2), pl.ds(2 * lax.rem(to, 2), 2)]

    n.ndst[at.s] = two_blocks(at.s)[...]
    got_nd = out.spread(at.sp, 8, two_blocks, n.ndst.at[at.s], n.nd_m, n.ndst)
    for m in range(2):
        row = n.idr[0, :, pl.ds(pl.multiple_of(at.x * 128 + 512 * m, 128), 128)]
        local = jnp.where(((row >> 7) & 3) == at.y, ((row >> 9) << 7) | (row & 127), -1)
        column = row_to_col(local.astype(f32), 128)[:, 0:1]
        held[m].hot = column == lax.broadcasted_iota(jnp.int32, (128, 512), 1).astype(f32)
    tab_x.finish()
    text_piece(3)
    step(0)
    step(1)
    text_piece(4)
    step(0)
    text_piece(5)
    step(1)
    text_piece(6)
    text_piece(7)
    step(0)
    step(1)
    tl = capped(n.tl[...])
    n.tl[...] = tl
    tid = row_to_col(n.tid[...].astype(f32), 128)[:, 0:1]
    text_hot = tid == lax.broadcasted_iota(jnp.int32, (128, VOCAB), 1).astype(f32) + (at.t * VOCAB).astype(f32)
    tsum = jnp.sum(jnp.exp(tl - soft_cap), axis=1, keepdims=True)
    tchosen = jnp.sum(jnp.where(text_hot, tl, 0.0), axis=1, keepdims=True)
    lane = lax.broadcasted_iota(jnp.int32, (128, 128), 1)
    packed = jnp.where(lane == 0, tsum, jnp.where(lane == 1, tchosen, 0.0))
    n.ts[at.t] = packed.T[0:8, :]
    got_ts = plane_same(n.ts, n.ts_m)
    step(0)
    def vocab_grad(b):
        part = n.gr[:, :, pl.ds(pl.multiple_of(128 * b, 128), 128)].reshape(256, 128)
        n.g_s[b] = dot(part.astype(f32).T.astype(bf16), n.ob[...].reshape(256, DD)).astype(bf16)

    loop(0, 4, vocab_grad)
    red_g = reduce("x", "g", rows_half(64))
    step(1)
    got_lc = seq_all(n.lc, n.lr, n.lc_m)
    n.lr[at.s] = n.lc[at.s]
    got_ts.wait_recv()
    ttotal = jnp.sum(n.ts[...], axis=0)
    tlse_row = soft_cap + jnp.log(ttotal[0:1, :])
    n.tlc[...] = row_to_col(tlse_row - ttotal[1:2, :], 128)
    tl = n.tl[...]
    tgrad = jnp.exp(tl - row_to_col(tlse_row, 128)[:, 0:1]) - jnp.where(text_hot, 1.0, 0.0)
    tgrad = tgrad * cap_slope(tl)
    n.tgr[...] = tgrad.astype(bf16)
    step(0)
    padded = jnp.concatenate([tgrad, jnp.zeros((128, 1024 - VOCAB), f32)], axis=1)
    n.tg[at.z, at.c] = padded.T.astype(bf16)
    tg_z = RingGather(
        out, at, "z",
        lambda i, hf: n.tg.at[i, at.c, span(hf, 1024)],
        lambda k: n.tg.at[pl.ds(0, k), at.c],
        n.tgz_m,
    )
    step(1)
    red_g.forward()
    text_back(0)
    step(0)
    text_back(1)
    step(1)
    text_back(2)

    def weight_grad(c):
        left, right = n.tri[:, c].reshape(256, 256), n.dob[lax.div(c, 3)].reshape(256, DD)
        g = dot(left.astype(f32).T.astype(bf16), right)
        for core in range(2):
            for zz in range(4):
                lo = 128 * (2 * zz + core)
                for a in range(4):
                    n.gas[core, a, c, :, 128 * zz : 128 * zz + 128] = g[64 * a : 64 * a + 64, lo : lo + 128].astype(bf16)

    step(0)
    text_back(3)
    red_t = reduce("x", "t", rows_half(2))
    step(1)
    red_g.finish()
    g = red_g.total()
    for b in range(8):
        n.gts[b] = g[:, 128 * b : 128 * b + 128].astype(bf16)
    n.gtr[at.s] = n.gts[at.s]
    tg_z.forward()
    step(0)
    step(1)
    got_gt = seq_all(n.gts, n.gtr, n.gt_m)
    loop(0, 4, weight_grad)
    theirs = n.gas.at[1 - at.c]
    wait_gar = out.one(theirs, n.gar, n.gar_m, at.sibling())
    step(0)
    step(1)
    red_t.forward()
    term = held[0].gain_term + held[1].gain_term
    n.dgs[at.s] = jnp.concatenate([term[:, 128 * b : 128 * b + 128] for b in range(8)], axis=0)
    got_dgs = seq_same(n.dgs, n.dgs_m)
    got_lc.wait_recv()
    lane = lax.broadcasted_iota(jnp.int32, (16, 128), 1)
    for m in range(2):
        losses = jnp.zeros((16, 128), f32)
        for k in range(8):
            losses = jnp.where(lane == 1 + k, n.lr[k, m], losses)
        n.lx[at.x, m] = losses
    got_lx = x_same(n.lx, n.lx_m)
    tg_z.finish()
    share_t = n.tg.at[:, at.c]
    wait_t = out.one(share_t, share_t, n.tgc_m, at.sibling())
    step(0)

    def features(m):
        def quarter(a):
            block = dot(n.ib[m, a].reshape(128, DD), n.pj[at.s], NT)
            for s in range(8):
                rows = [block[32 * b + 4 * s : 32 * b + 4 * s + 4] for b in range(4)]
                rows = jnp.concatenate(rows, axis=0).astype(bf16)
                n.sf[s % 2, s // 2, pl.ds(pl.multiple_of(64 * m + 16 * a, 16), 16), :] = rows

        loop(0, 4, quarter)

    def hot_before(m):
        prev = jnp.where(at.s > 0, n.idr[1, :, 512 * m : 512 * m + 512] - at.t * 128, -1)
        entry = lax.broadcasted_iota(jnp.int32, (128, 512), 0)
        return jnp.where(prev == entry, 1.0, 0.0).astype(bf16)

    features(0)
    red_t.finish()
    for b in range(4):
        n.t2_s[b] = red_t.total(lambda ref: ref[b]).astype(bf16)
    red_t2 = reduce("y", "t2", rows_half(64))
    wait_gar.wait_recv()
    for a in range(4):
        n.ga_s[a] = (n.gas[at.c, a].astype(f32) + n.gar[a].astype(f32)).astype(bf16)
    red_ga = reduce("x", "ga", rows_half(2))
    before = hot_before(0)

    def first_half(b):
        cols = pl.ds(pl.multiple_of(256 * b, 256), 256)
        rows = n.ib[0, :, :, :, cols].reshape(512, 256)
        g = dot(n.nt[:, 0:512], rows)
        n.raw[0, :, cols] = g[0:128]
        n.raw[1, :, cols] = g[128:256]
        n.raw[2, :, cols] = dot(before, rows)

    loop(0, 4, first_half)
    red_t2.forward()
    step(1)
    features(1)
    wait_sf = out.one(n.sf.at[1 - at.c], n.sfr, n.sfr_m, at.sibling())

    def proj_grad(d):
        to = lax.rem(at.z + d, 4)
        cols = pl.ds(pl.multiple_of(to * 256, 256), 256)
        held_part = jnp.concatenate([n.raw[0, :, cols], n.raw[1, :, cols]], axis=0)
        g = held_part + dot(n.nt[:, 512:1024], n.ib[1, :, :, :, cols].reshape(512, 256))
        n.gps[2 * to] = g[:, 0:128].astype(bf16)
        n.gps[2 * to + 1] = g[:, 128:256].astype(bf16)
    def send_proj(d):
        proj_grad(d)
        to = lax.rem(at.z + d, 4)
        for core in range(2):
            src = n.gps.at[2 * to + core]
            out.go(src, n.gpr.at[at.s], n.gp_m.at[0], n.gp_m.at[1], {"z": to, "core": core})

    wait_sf.wait_recv()
    for b in range(4):
        n.f_s[b] = (n.sf[at.c, b].astype(f32) + n.sfr[b].astype(f32)).astype(bf16)
    red_f = direct("z", "f")
    red_t2.finish()
    loop(1, 4, send_proj)
    proj_grad(0)
    n.gpr[at.s] = n.gps[at.s]
    theirs = 2 * at.z + 1 - at.c
    out.go(n.gps.at[theirs], n.gpr.at[at.s], n.gp_m.at[0], n.gp_m.at[1], at.sibling())
    out.sent_later(n.gps.at[pl.ds(0, 7)], n.gp_m.at[0])
    got_gp = out.bytes_of(n.gpr.at[pl.ds(0, 7)], n.gp_m.at[1])
    red_f.finish()
    fb = red_t2.total() + red_f.total()
    gback = fb * gain
    inner = jnp.sum(gback * hat, axis=1, keepdims=True)
    n.rd[at.t] = jnp.broadcast_to(inner, (128, 128)).T[0:8, :]
    got_rd = plane_same(n.rd, n.rd_m)
    n.tgn[at.s] = jnp.broadcast_to(jnp.sum(fb * hat, axis=0, keepdims=True), (8, 256))
    got_tgn = seq_same(n.tgn, n.tgn_m)
    before = hot_before(1)

    def second_half(b):
        cols = pl.ds(pl.multiple_of(256 * b, 256), 256)
        look = (n.raw[2, :, cols] + dot(before, n.ib[1, :, :, :, cols].reshape(512, 256))) * embed_scale
        n.lks[2 * b] = look[:, 0:128].astype(bf16)
        n.lks[2 * b + 1] = look[:, 128:256].astype(bf16)

    loop(0, 4, second_half)
    got_lk = seq_all(n.lks, n.lkr, n.lk_m)
    n.lkr[at.s] = n.lks[at.s]
    red_ga.forward()
    got_dgs.wait_recv()
    n.dgt[at.t] = jnp.sum(n.dgs[...], axis=0)
    got_dgt = plane_same(n.dgt, n.dgt_m)

    wait_t.wait_recv()
    got_nd.wait_recv()

    def table_grad(a):
        part = pl.ds(pl.multiple_of(256 * a, 256), 256)
        left = jnp.concatenate([n.tg[g // 2, g % 2, part, :] for g in range(8)], axis=1)
        for b in range(2):
            right = n.ndst[:, b].reshape(1024, 256)
            n.o_gtt[part, 256 * b : 256 * b + 256] = dot(left, right).astype(bf16)

    loop(0, 4, table_grad)
    red_ga.finish()
    for b in range(4):
        n.gz_s[b] = red_ga.total(lambda ref: ref[:, :, 128 * b : 128 * b + 128]).astype(bf16)
    red_gz = direct("z", "gz")
    got_rd.wait_recv()
    dots = twice(row_to_col(jnp.sum(n.rd[...], axis=0)[0:1, :], 128))
    n.o_gh[...] = scale * (gback - hat * (dots / D))
    got_tgn.wait_recv()
    n.o_tgain[...] = jnp.sum(n.tgn[...], axis=0)[0:1, :]
    got_dgt.wait_recv()
    n.o_dg[...] = jnp.sum(n.dgt[...], axis=0)
    got_lx.wait_recv()
    lane = lax.broadcasted_iota(jnp.int32, (128, 128), 1)
    losses = jnp.concatenate([n.lx[a, m] for m in range(2) for a in range(4)], axis=0)
    n.o_loss[...] = jnp.where(lane == 0, n.tlc[...], losses).T[0:9, :]
    got_gt.wait_recv()
    got_lk.wait_recv()
    for k in range(8):
        g = n.gtr[k].astype(f32)
        if k < 7:
            g = g + n.lkr[k + 1].astype(f32)
        n.o_gtab[k] = g
    got_gp.wait_recv()
    n.o_gp[...] = n.gpr[...]
    red_gz.finish()
    ga = red_gz.total()
    n.o_gqkv[...] = ga[0:3]
    n.o_gout[...] = ga[3]
    out.finish()


def write_kernel(*refs):
    count = len(refs) // 2
    for src, dst in zip(refs[:count], refs[count:]):
        dst[...] = src[...].astype(f32)


def write_outputs(results):
    shapes = [r.shape for r in results]
    shapes[3] = (VOCAB, 512)
    blocks = {1: (32, 256), 3: (256, 512), 4: (2, 256, 128), 5: (2, 128, 128)}

    def spec(i):
        block = blocks.get(i, shapes[i])
        moves = i in blocks
        return pl.BlockSpec(block, lambda g: (g if moves else 0,) + (0,) * (len(block) - 1))

    return pl.pallas_call(
        write_kernel,
        out_shape=[jax.ShapeDtypeStruct(shape, f32) for shape in shapes],
        grid=(4,),
        in_specs=[spec(i) for i in range(9)],
        out_specs=[spec(i) for i in range(9)],
        name="write",
    )(*results)


def on_device(
    hidden, text_gain, text_table, proj, audio_table, depth_gain, attn_qkv, attn_out, text_ids, audio_ids
):
    vmem = pl.BlockSpec(memory_space=pltpu.VMEM)
    hbm = pl.BlockSpec(memory_space=pl.ANY)
    outs = [
        ((9, 128), f32), ((128, 256), f32), ((1, 256), f32), ((1024, 512), bf16), ((8, 256, 128), bf16),
        ((8, 128, 128), f32), ((8, 128), f32), ((3, 64, 128), f32), ((64, 128), f32),
    ]
    results = pl.pallas_call(
        kernel,
        out_shape=[jax.ShapeDtypeStruct(shape, dtype) for shape, dtype in outs],
        in_specs=[vmem, vmem, hbm, hbm, hbm, vmem, vmem, vmem, vmem, vmem],
        out_specs=[vmem] * len(outs),
        scratch_shapes=[scratch_shape(entry) for entry in SCRATCH],
        name="head",
        compiler_params=pltpu.CompilerParams(
            collective_id=1, has_side_effects=True, vmem_limit_bytes=VMEM_LIMIT
        ),
    )(
        hidden, text_gain, text_table, proj, audio_table, depth_gain,
        jnp.transpose(attn_qkv, (1, 2, 0)), attn_out, text_ids[None, :], audio_ids.T,
    )
    losses, gh, tgain, gtt, gp, gtab, dg, gqkv, gout = write_outputs(results)
    return losses.T, gh, tgain[0], gtt.T, gp, gtab, dg.reshape(DD), jnp.transpose(gqkv, (2, 0, 1)), gout


def solution(mesh):
    fine = Mesh(mesh.devices.reshape(4, 2, 4, 4), ("z", "core", "x", "y"))
    seq = ("z", "core")
    tp = ("x", "y")
    in_specs = (
        P(seq, tp), P(tp), P(tp, None), P(None, tp, None), P(None, tp, None),
        P(), P(None, None, tp), P(tp, None), P(seq), P(seq, None),
    )
    out_specs = (
        P(seq, None), P(seq, tp), P(tp), P(seq, tp), P(None, tp, seq),
        P(None, tp, seq), P(), P(seq, None, tp), P(tp, seq),
    )
    return jax.shard_map(
        on_device, mesh=fine, in_specs=in_specs, out_specs=out_specs, check_vma=False
    )
```

```python
import math

import jax
import jax.numpy as jnp
from jax import lax
from jax.experimental import pallas as pl
from jax.experimental.pallas import tpu as pltpu
from jax.sharding import Mesh
from jax.sharding import PartitionSpec as P

D = 4096
DD = 1024
HEAD = 64
VOCAB = 1000
MESH = pl.DeviceIdType.MESH
VMEM_LIMIT = 62 * 1024 * 1024

soft_cap = 12.0
epsilon = 1e-05
embed_scale = math.sqrt(DD) / 4.0
f32 = jnp.float32
bf16 = jnp.bfloat16

NN = (((1,), (0,)), ((), ()))
NT = (((1,), (1,)), ((), ()))
TN = (((0,), (0,)), ((), ()))


def dot(a, b, dims=NN):
    return lax.dot_general(a, b, dims, preferred_element_type=f32)


def capped(values):
    return soft_cap * jnp.tanh(values / soft_cap)


def cap_slope(capped_values):
    ratio = capped_values / soft_cap
    return 1.0 - ratio * ratio


class Place:
    def __init__(self):
        self.z = lax.axis_index("z")
        self.c = lax.axis_index("core")
        self.x = lax.axis_index("x")
        self.y = lax.axis_index("y")
        self.s = self.z * 2 + self.c
        self.t = self.x * 4 + self.y

    def ring(self, axis):
        me = {"x": self.x, "y": self.y, "z": self.z}[axis]
        return me, lax.rem(me + 1, 4), lax.rem(me + 2, 4), lax.rem(me + 3, 4)

    def xp(self, d):
        to = lax.rem(self.x + d, 4)
        return to, {"x": to}

    def yp(self, d):
        to = lax.rem(self.y + d, 4)
        return to, {"y": to}

    def sp(self, d):
        to = lax.rem(self.s + d, 8)
        return to, {"z": lax.div(to, 2), "core": lax.rem(to, 2)}

    def tp(self, d):
        to = lax.rem(self.t + d, 16)
        return to, {"x": lax.div(to, 4), "y": lax.rem(to, 4)}

    def sibling(self):
        return {"core": 1 - self.c}


class Sends:
    def __init__(self, at):
        self.at = at
        self.pending = []

    def go(self, src, dst, send, recv, device):
        pltpu.make_async_remote_copy(
            src_ref=src, dst_ref=dst, send_sem=send, recv_sem=recv, device_id=device, device_id_type=MESH
        ).start()

    def bytes_of(self, ref, sem):
        return pltpu.make_async_remote_copy(
            src_ref=ref, dst_ref=ref, send_sem=sem, recv_sem=sem,
            device_id=self.at.sibling(), device_id_type=MESH,
        )

    def sent_later(self, ref, sem):
        self.pending.append(self.bytes_of(ref, sem))

    def one(self, src, dst, sems, device):
        self.go(src, dst, sems.at[0], sems.at[1], device)
        self.sent_later(src, sems.at[0])
        return self.bytes_of(dst, sems.at[1])

    def spread(self, peer, n, src, dst, sems, slots, all_bytes=None):
        for d in range(1, n):
            to, device = peer(d)
            self.go(src(to), dst, sems.at[0], sems.at[1], device)
        if all_bytes is None:
            all_bytes = slots.at[pl.ds(0, n - 1)]
        self.sent_later(all_bytes, sems.at[0])
        return self.bytes_of(all_bytes, sems.at[1])

    def finish(self):
        for wait in self.pending:
            wait.wait_send()


class RingGather:
    def __init__(self, out, at, axis, part, slots, sems):
        self.out, self.part, self.sems, self.slots = out, part, sems, slots
        me, self.right, far, self.left = at.ring(axis)
        self.to_right, self.to_left = {axis: self.right}, {axis: self.left}
        block = part(me, None)
        out.go(block, block, sems.at[0], sems.at[1], self.to_right)
        out.go(block, block, sems.at[0], sems.at[2], self.to_left)
        out.sent_later(slots(3), sems.at[0])

    def forward(self):
        out, part, sems = self.out, self.part, self.sems
        out.bytes_of(part(self.left, None), sems.at[1]).wait_recv()
        one = part(self.left, 0)
        out.go(one, one, sems.at[0], sems.at[3], self.to_right)
        out.bytes_of(part(self.right, None), sems.at[2]).wait_recv()
        two = part(self.right, 1)
        out.go(two, two, sems.at[0], sems.at[3], self.to_left)

    def finish(self):
        self.out.bytes_of(self.slots(1), self.sems.at[3]).wait_recv()


class RingReduce:
    def __init__(self, out, at, axis, blocks, half, bufs, sems):
        self.out, self.half, self.sems, self.blocks = out, half, sems, blocks
        self.me, self.right, far, self.left = at.ring(axis)
        self.rl, self.rr, self.fa, self.fb = bufs
        self.to_right, self.to_left = {axis: self.right}, {axis: self.left}
        s = blocks
        out.go(half(s.at[far], 0), self.fa, sems.at[0], sems.at[1], self.to_right)
        out.go(half(s.at[far], 1), self.fb, sems.at[0], sems.at[2], self.to_left)
        out.go(half(s.at[self.right], 1), half(self.rl, 1), sems.at[0], sems.at[3], self.to_right)
        out.go(half(s.at[self.left], 0), half(self.rr, 0), sems.at[0], sems.at[3], self.to_left)
        out.sent_later(s.at[pl.ds(0, 3)], sems.at[0])

    def forward(self):
        s, half, out, sems = self.blocks, self.half, self.out, self.sems
        out.bytes_of(self.fa, sems.at[1]).wait_recv()
        one = half(s.at[self.right], 0)
        one[...] = (one[...].astype(f32) + self.fa[...].astype(f32)).astype(bf16)
        out.go(one, half(self.rl, 0), sems.at[0], sems.at[3], self.to_right)
        out.bytes_of(self.fb, sems.at[2]).wait_recv()
        two = half(s.at[self.left], 1)
        two[...] = (two[...].astype(f32) + self.fb[...].astype(f32)).astype(bf16)
        out.go(two, half(self.rr, 1), sems.at[0], sems.at[3], self.to_left)

    def finish(self):
        self.out.bytes_of(self.blocks.at[pl.ds(0, 2)], self.sems.at[3]).wait_recv()

    def total(self, pick=lambda ref: ref[...]):
        own = pick(self.blocks.at[self.me]).astype(f32)
        return own + pick(self.rl).astype(f32) + pick(self.rr).astype(f32)


class DirectReduce:
    def __init__(self, out, at, axis, blocks, got, sems):
        self.blocks, self.got = blocks, got
        self.me = at.ring(axis)[0]
        for d in (2, 1, 3):
            to = lax.rem(self.me + d, 4)
            out.go(blocks.at[to], got.at[d - 1], sems.at[0], sems.at[1], {axis: to})
        out.sent_later(blocks.at[pl.ds(0, 3)], sems.at[0])
        self.wait = out.bytes_of(got, sems.at[1])

    def finish(self):
        self.wait.wait_recv()

    def total(self, pick=lambda ref: ref[...]):
        own = pick(self.blocks.at[self.me]).astype(f32)
        for d in range(3):
            own = own + pick(self.got.at[d]).astype(f32)
        return own


def span(h, size):
    if h is None:
        return pl.ds(0, size)
    return pl.ds(h * (size // 2), size // 2)


def rows_half(n):
    return lambda ref, h: ref.at[pl.ds(h * n, n)]


def row_to_col(row, lanes):
    return jnp.broadcast_to(row, (lanes, row.shape[1])).T


def twice(col):
    return jnp.concatenate([col, col], axis=1)


def fold(rows, n):
    w = rows.shape[1] // n
    return jnp.concatenate([rows[:, i * w : i * w + w] for i in range(n)], axis=0).astype(bf16)


def unfold(packed, n):
    r = packed.shape[0] // n
    wide = packed.astype(f32)
    return jnp.concatenate([wide[i * r : i * r + r] for i in range(n)], axis=1)


def by_step(rows):
    return [fold(rows[4 * k : 4 * k + 4], 4) for k in range(8)]


def from_steps(ref):
    return jnp.concatenate([unfold(ref[k], 4) for k in range(8)], axis=0)


def head_masks(rows):
    lane = lax.broadcasted_iota(jnp.int32, (rows, 256), 1)
    return [(lane >= 64 * h) & (lane < 64 * h + 64) for h in range(4)]


def step_mask():
    i = lax.broadcasted_iota(jnp.int32, (128, 128), 0)
    j = lax.broadcasted_iota(jnp.int32, (128, 128), 1)
    return ((i & 3) == (j & 3)) & ((i >> 5) == (j >> 5)) & (j <= i)


def attention(qh, kk, allowed):
    scores = dot(qh, kk, NT) / math.sqrt(HEAD)
    raised = jnp.where(allowed, jnp.exp(scores), 0.0)
    return raised / jnp.sum(raised, axis=1, keepdims=True)


def ring_reduce_scratch(name, block, half):
    return [
        (name + "_s", (4,) + block, bf16),
        (name + "_rl", block, bf16),
        (name + "_rr", block, bf16),
        (name + "_fa", half, bf16),
        (name + "_fb", half, bf16),
        (name + "_m", 4, None),
    ]


def direct_scratch(name, block):
    return [(name + "_s", (4,) + block, bf16), (name + "_r", (3,) + block, bf16), (name + "_m", 2, None)]


def chain_scratch(m):
    m = str(m)
    return [
        *ring_reduce_scratch("p" + m, (4, 16, DD), (2, 16, DD)),
        *ring_reduce_scratch("q" + m, (4, 16, DD), (2, 16, DD)),
        *direct_scratch("pp" + m, (16, DD)),
        *direct_scratch("qq" + m, (16, DD)),
        ("dn_m" + m, 2, None),
        *direct_scratch("h" + m, (32, DD)),
        ("a1s" + m, (8, 16, 256), bf16), ("a1r" + m, (8, 16, 256), bf16), ("a1_m" + m, 2, None),
        ("a2s" + m, (8, 16, 256), bf16), ("a2r" + m, (8, 16, 256), bf16), ("a2_m" + m, 2, None),
        ("a3s" + m, (8, 16, 256), bf16), ("a3r" + m, (8, 16, 256), bf16), ("a3_m" + m, 2, None),
        ("ob_m" + m, 2, None), ("e" + m, (4, 8, 128), f32), ("e_m" + m, 2, None),
        *direct_scratch("v" + m, (32, DD)),
        *direct_scratch("c" + m, (32, DD)),
        ("obb_m" + m, 2, None),
    ]


SCRATCH = [
    ("tt", (VOCAB, D), bf16), ("pj", (8, 256, DD), bf16), ("au", (8, 128, DD), bf16), ("load", 3, 0),
    ("ssq", (16, 8, 128), f32), ("ssq_m", 2, None),
    ("idb", (8, 8, 128), jnp.int32), ("idb_m", 2, None), ("idr", (2, 1, 1024), jnp.int32),
    ("raw", (8, 128, DD), f32), ("look", (8, 128, DD), bf16),
    ("wb", (4, 4, 64, DD), bf16), ("wb_m", 4, None), ("wz_m", 4, None), ("wc_m", 2, None),
    ("nb", (4, 4, 128, 256), bf16), ("ny_m", 4, None), ("nx_m", 4, None),
    ("ns", (4, 2, 16, 16, 128), bf16), ("nz_m", 4, None), ("nc_m", 2, None),
    *chain_scratch(0), *chain_scratch(1),
    ("dob", (2, 2, 4, 32, DD), bf16), ("qkv", (2, 3, 128, 256), bf16),
    ("ex", (2, 4, 128, 128), f32), ("ob", (2, 4, 32, DD), bf16),
    ("gr", (2, 512, 128), bf16), ("tri", (2, 4, 128, 256), bf16), ("trt", (4, 256, 256), bf16),
    ("tab", (4, 128, DD), bf16), ("tab_m", 4, None),
    ("tl", (VOCAB, 128), f32), ("ty", (4, 8, 128), f32), ("ty_m", 2, None), ("tx", (4, 8, 128), f32), ("tx_m", 2, None),
    ("tgr", (128, VOCAB), bf16), ("tlr", (1, 128), f32),
    *ring_reduce_scratch("g", (128, DD), (64, DD)),
    ("lc", (8, 2, 16, 128), f32), ("lr", (8, 2, 16, 128), f32), ("lc_m", 2, None),
    ("lx", (4, 2, 16, 128), f32), ("lx_m", 2, None),
    ("nt", (256, 1024), bf16), ("tg", (4, 2, 1024, 128), bf16), ("tgz_m", 4, None), ("tgc_m", 2, None),
    *ring_reduce_scratch("t", (4, 128, 256), (2, 128, 256)),
    *ring_reduce_scratch("t2", (128, 256), (64, 256)),
    ("ndst", (8, 2, 128, 256), bf16), ("nd_m", 2, None),
    ("ib", (2, 4, 4, 32, DD), bf16), ("i0x_m", 2, None), ("i0y_m", 4, None),
    ("iax_m", 2, None), ("iay_m", 4, None), ("ibx_m", 4, None), ("iby_m", 2, None),
    ("gas", (2, 4, 4, 64, 512), bf16), ("gar", (4, 4, 64, 512), bf16), ("gar_m", 2, None),
    *ring_reduce_scratch("ga", (4, 64, 512), (2, 64, 512)),
    *direct_scratch("gz", (4, 64, 128)),
    ("sf", (2, 4, 128, 256), bf16), ("sfr", (4, 128, 256), bf16), ("sfr_m", 2, None),
    *direct_scratch("f", (128, 256)),
    ("gas_all", (8, 384, 128), bf16), ("gar_all", (8, 384, 128), bf16), ("gall_m", 2, None),
    ("rel", (2, 2, 192, 128), bf16), ("rel_m", 3, None),
    ("gts", (8, 128, 128), bf16), ("gtr", (8, 128, 128), bf16), ("gt_m", 2, None),
    ("dgs", (8, 8, 128), f32), ("dgs_m", 2, None), ("dgy", (4, 8, 128), f32), ("dgy_m", 2, None),
    ("dgx", (4, 8, 128), f32), ("dgx_m", 2, None),
    ("rd", (16, 8, 128), f32), ("rd_m", 2, None), ("tgn", (8, 8, 256), f32), ("tgn_m", 2, None),
]


def scratch_shape(entry):
    name, shape, dtype = entry
    if dtype is None or isinstance(dtype, int):
        return pltpu.SemaphoreType.DMA((shape,))
    return pltpu.VMEM(shape, dtype)


class Named:
    pass


def loop(low, high, body):
    def one(i, carry):
        body(i)
        return carry

    lax.fori_loop(low, high, one, 0)


INPUTS = ["hid", "gain", "table", "proj", "audio", "dgain", "wqkv", "wout", "tid", "ids"]
OUTPUTS = ["o_loss", "o_gh", "o_tgain", "o_gtt", "o_gp", "o_gtab", "o_dg", "o_gqkv", "o_gout"]


def kernel(*refs):
    n = Named()
    names = INPUTS + OUTPUTS + [entry[0] for entry in SCRATCH]
    for name, ref in zip(names, refs):
        setattr(n, name, ref)
    at = Place()
    out = Sends(at)

    def reduce(axis, name, half):
        bufs = [getattr(n, name + suffix) for suffix in ("_rl", "_rr", "_fa", "_fb")]
        return RingReduce(out, at, axis, getattr(n, name + "_s"), half, bufs, getattr(n, name + "_m"))

    def direct(axis, name):
        return DirectReduce(
            out, at, axis, getattr(n, name + "_s"), getattr(n, name + "_r"), getattr(n, name + "_m")
        )

    def seq_all(src, dst, sems):
        return out.spread(at.sp, 8, lambda to: src.at[to], dst.at[at.s], sems, dst)

    def seq_same(ref, sems):
        return out.spread(at.sp, 8, lambda to: ref.at[at.s], ref.at[at.s], sems, ref)

    def plane_same(ref, sems):
        return out.spread(at.tp, 16, lambda to: ref.at[at.t], ref.at[at.t], sems, ref)

    def x_same(ref, sems):
        return out.spread(at.xp, 4, lambda to: ref.at[at.x], ref.at[at.x], sems, ref)

    def y_same(ref, sems):
        return out.spread(at.yp, 4, lambda to: ref.at[at.y], ref.at[at.y], sems, ref)

    loads = [
        pltpu.make_async_copy(src, dst, n.load.at[i])
        for i, (src, dst) in enumerate([(n.proj, n.pj), (n.audio, n.au), (n.table, n.tt)])
    ]
    for copy in loads:
        copy.start()
    for c in range(3):
        n.wb[at.x, c] = n.wqkv[c]
    n.wb[at.x, 3] = n.wout[...]
    barrier = pltpu.get_barrier_semaphore()
    for d in range(1, 16):
        pl.semaphore_signal(barrier, inc=1, device_id=at.tp(d)[1], device_id_type=MESH)
    for d in range(1, 8):
        pl.semaphore_signal(barrier, inc=1, device_id=at.sp(d)[1], device_id_type=MESH)
    h = n.hid[...].astype(f32)
    gain = n.gain[...].astype(f32)[None, :]
    dgain = n.dgain[...].astype(f32)[None, :]
    ones = jnp.ones((8, 256), f32)
    n.ssq[at.t] = lax.dot_general(
        ones, h * h, NT, precision=lax.Precision.HIGHEST, preferred_element_type=f32
    )
    n.idb[at.s] = n.ids[...]
    unscaled = (h * gain).astype(bf16)
    pl.semaphore_wait(barrier, 22)

    got_ssq = plane_same(n.ssq, n.ssq_m)
    mine = pl.ds(pl.multiple_of(at.c * 32, 32), 32)
    weights = RingGather(
        out, at, "x",
        lambda i, hf: n.wb.at[i, at.z, mine] if hf is None
        else n.wb.at[i, at.z, pl.ds(pl.multiple_of(at.c * 32 + 16 * hf, 16), 16)],
        lambda k: n.wb.at[pl.ds(0, k), at.z, mine],
        n.wb_m,
    )
    got_ids = seq_same(n.idb, n.idb_m)
    loads[0].wait()

    def raw_step(k):
        n.raw[k] = dot(unscaled, n.pj[k])

    loop(0, 8, raw_step)
    loads[1].wait()
    entry = (lax.broadcasted_iota(jnp.int32, (128, 128), 1) + at.t * 128).astype(f32)
    n.look[0] = jnp.zeros((128, DD), bf16)

    def look_step(k):
        column = row_to_col(n.ids[pl.ds(k, 1), :].astype(f32), 128)
        hot = jnp.where(column == entry, 1.0, 0.0).astype(bf16)
        n.look[k + 1] = (dot(hot, n.au[k]) * embed_scale).astype(bf16)

    loop(0, 7, look_step)
    got_ssq.wait_recv()
    scale = row_to_col(lax.rsqrt(jnp.sum(n.ssq[...], axis=0)[0:1, :] / D + epsilon), 128)
    column = scale[:, 0:1]
    scale = twice(scale)
    hat = h * scale

    first = []
    for m in range(2):
        ps, qs = getattr(n, f"p{m}_s"), getattr(n, f"q{m}_s")
        part = slice(64 * m, 64 * m + 64)

        def scaled(k):
            return n.raw[k, part, :] * column[part] + n.look[k, part, :].astype(f32)

        def to_x(k):
            p = scaled(k)
            for b in range(4):
                ps[b, k] = p[16 * b : 16 * b + 16].astype(bf16)

        def to_y(k):
            p = scaled(k + 4)
            for b in range(4):
                rows = [p[16 * a + 4 * b : 16 * a + 4 * b + 4] for a in range(4)]
                qs[b, k] = jnp.concatenate(rows, axis=0).astype(bf16)

        loop(0, 4, to_x)
        red_p = reduce("x", f"p{m}", rows_half(2))
        loop(0, 4, to_y)
        first.append((red_p, reduce("y", f"q{m}", rows_half(2))))
    normed_f = hat * gain
    n.nb[at.x, at.y] = normed_f.astype(bf16)
    for b in range(16):
        n.ns[at.z, at.c, b] = fold(normed_f[8 * b : 8 * b + 8], 2)
    norm_z = RingGather(
        out, at, "z",
        lambda i, hf: n.ns.at[i, at.c, span(hf, 16)],
        lambda k: n.ns.at[pl.ds(0, k), at.c],
        n.nz_m,
    )
    norm_y = RingGather(
        out, at, "y",
        lambda i, hf: n.nb.at[at.x, i, span(hf, 128)],
        lambda k: n.nb.at[at.x, pl.ds(0, k)],
        n.ny_m,
    )

    masks = head_masks(128)
    allowed = step_mask()
    held = [Named(), Named()]

    def wcat(c):
        return jnp.concatenate([n.wb[a, c] for a in range(4)], axis=0)

    def half_of(m, name):
        return getattr(n, name + str(m))

    def chain(m):
        mine = held[m]
        red_p, red_q = first[m]
        red_p.forward()
        red_q.forward()
        yield
        for red, to, axis in ((red_p, "pp", "y"), (red_q, "qq", "x")):
            red.finish()
            total = [red.total(lambda ref: ref[k]) for k in range(4)]
            for b in range(4):
                rows = [total[k][4 * b : 4 * b + 4] for k in range(4)]
                getattr(n, f"{to}{m}_s")[b] = jnp.concatenate(rows, axis=0).astype(bf16)
            if axis == "y":
                red_pp = direct("y", f"pp{m}")
            else:
                red_qq = direct("x", f"qq{m}")
        yield
        red_pp.finish()
        red_qq.finish()
        di = jnp.concatenate([red_pp.total(), red_qq.total()], axis=0)
        mine.dscale = lax.rsqrt(jnp.mean(di * di, axis=1, keepdims=True) + epsilon)
        mine.dhat = di * mine.dscale
        n.dob[0, m, at.y] = (mine.dhat * dgain).astype(bf16)
        got = y_same(n.dob.at[0, m], half_of(m, "dn_m"))
        yield
        got.wait_recv()
        dnv = n.dob[0, m].reshape(128, DD)
        for c in range(3):
            n.qkv[m, c] = dot(dnv, wcat(c), NT).astype(bf16)
        q, k, v = n.qkv[m, 0], n.qkv[m, 1], n.qkv[m, 2]
        mixed = jnp.zeros((128, 256), f32)
        for hd in range(4):
            qh = jnp.where(masks[hd], q, jnp.zeros_like(q))
            exact = attention(qh, k, allowed)
            n.ex[m, hd] = exact
            mixed = jnp.where(masks[hd], dot(exact.astype(bf16), v), mixed)
        n.tri[m, 3] = mixed.astype(bf16)
        terms = dot(n.tri[m, 3], wcat(3))
        for b in range(4):
            getattr(n, f"h{m}_s")[b] = terms[32 * b : 32 * b + 32].astype(bf16)
        red_h = direct("y", f"h{m}")
        yield
        red_h.finish()
        src, dst = half_of(m, "a1s"), half_of(m, "a1r")
        for k, block in enumerate(by_step(di + red_h.total())):
            src[k] = block
        got = seq_all(src, dst, half_of(m, "a1_m"))
        dst[at.s] = src[at.s]
        yield
        got.wait_recv()
        n.ob[m, at.y] = from_steps(dst).astype(bf16)
        got = y_same(n.ob.at[m], half_of(m, "ob_m"))
        yield
        got.wait_recv()
        rows = n.ob[m].reshape(128, DD)
        tab = n.tab[...].reshape(512, DD)
        logits = capped(dot(tab, rows, NT))
        hot = mine.hot == lax.broadcasted_iota(jnp.int32, (512, 128), 0)
        sums = jnp.sum(jnp.exp(logits - soft_cap), axis=0, keepdims=True)
        chosen = jnp.sum(jnp.where(hot, logits, 0.0), axis=0, keepdims=True)
        e = half_of(m, "e")
        e[at.y] = jnp.concatenate([sums, chosen, jnp.zeros((6, 128), f32)], axis=0)
        got = y_same(e, half_of(m, "e_m"))
        yield
        got.wait_recv()
        total = jnp.sum(e[...], axis=0)
        lse_row = soft_cap + jnp.log(total[0:1, :])
        grad = (jnp.exp(logits - lse_row) - jnp.where(hot, 1.0, 0.0)) * cap_slope(logits)
        n.gr[m] = grad.astype(bf16)
        terms = dot(grad.T.astype(bf16), tab)
        for b in range(4):
            getattr(n, f"v{m}_s")[b] = terms[32 * b : 32 * b + 32].astype(bf16)
        red_v = direct("y", f"v{m}")
        loss = row_to_col(lse_row - total[1:2, :], 128)
        for g in range(8):
            rows = [loss[32 * b + 4 * g : 32 * b + 4 * g + 4] for b in range(4)]
            n.lc[g, m] = jnp.concatenate(rows, axis=0)
        yield
        red_v.finish()
        src, dst = half_of(m, "a2s"), half_of(m, "a2r")
        for k, block in enumerate(by_step(red_v.total())):
            src[k] = block
        got = seq_all(src, dst, half_of(m, "a2_m"))
        dst[at.s] = src[at.s]
        yield
        got.wait_recv()
        output_back = from_steps(dst)
        n.dob[1, m, at.y] = output_back.astype(bf16)
        got = y_same(n.dob.at[1, m], half_of(m, "obb_m"))
        yield
        got.wait_recv()
        g = dot(n.dob[1, m].reshape(128, DD), wcat(3), NT).astype(bf16)
        q, k, v = n.qkv[m, 0], n.qkv[m, 1], n.qkv[m, 2]
        dq = jnp.zeros((128, 256), f32)
        dk = jnp.zeros((128, 256), f32)
        dv = jnp.zeros((128, 256), f32)
        for hd in range(4):
            gh = jnp.where(masks[hd], g, jnp.zeros_like(g))
            exact = n.ex[m, hd]
            dw = dot(gh, v, NT).astype(bf16).astype(f32)
            ds = exact * (dw - jnp.sum(dw * exact, axis=1, keepdims=True)) / math.sqrt(HEAD)
            dv = jnp.where(masks[hd], dot(exact.T.astype(bf16), g), dv)
            dq = jnp.where(masks[hd], dot(ds.astype(bf16), k), dq)
            dk = jnp.where(masks[hd], dot(ds.T.astype(bf16), q), dk)
        n.tri[m, 0] = dq.astype(bf16)
        n.tri[m, 1] = dk.astype(bf16)
        n.tri[m, 2] = dv.astype(bf16)
        terms = dot(n.tri[m, 0], wcat(0)) + dot(n.tri[m, 1], wcat(1)) + dot(n.tri[m, 2], wcat(2))
        for b in range(4):
            getattr(n, f"c{m}_s")[b] = terms[32 * b : 32 * b + 32].astype(bf16)
        red_c = direct("y", f"c{m}")
        yield
        red_c.finish()
        nback = red_c.total()
        mine.gain_term = jnp.sum(nback * mine.dhat, axis=0, keepdims=True)
        hback = nback * dgain
        inner = jnp.mean(hback * mine.dhat, axis=1, keepdims=True)
        ib = output_back + mine.dscale * (hback - mine.dhat * inner)
        src, dst = half_of(m, "a3s"), half_of(m, "a3r")
        for k, block in enumerate(by_step(ib)):
            src[k] = block
        got = seq_all(src, dst, half_of(m, "a3_m"))
        dst[at.s] = src[at.s]
        yield
        got.wait_recv()
        n.ib[m, at.x, at.y] = from_steps(dst).astype(bf16)

        def part(axis, where, sems):
            return RingGather(out, at, axis, where, lambda k: where(pl.ds(0, k), None), sems)

        def spread(peer, mine_is, where, sems):
            src = where(mine_is)
            return out.spread(peer, 4, lambda to: src, src, sems, None, where(pl.ds(0, 3)))

        low, high = pl.ds(0, 16), pl.ds(16, 16)
        ib = n.ib.at[m]
        if m == 0:
            one = [spread(at.xp, at.x, lambda i: ib.at[i, at.y], n.i0x_m)]
        else:
            one = [
                spread(at.xp, at.x, lambda i: ib.at[i, at.y, low], n.iax_m),
                spread(at.yp, at.y, lambda i: ib.at[at.x, i, high], n.iby_m),
            ]
        yield
        one[0].wait_recv()
        if m == 0:
            two = [part("y", lambda i, hf: ib.at[:, i, :, span(hf, DD)], n.i0y_m)]
        else:
            two = [part("y", lambda i, hf: ib.at[:, i, low, span(hf, DD)], n.iay_m)]
            one[1].wait_recv()
            two.append(part("x", lambda i, hf: ib.at[i, :, high, span(hf, DD)], n.ibx_m))
        yield
        for ring in two:
            ring.forward()
        yield
        for ring in two:
            ring.finish()
        yield

    run = [chain(0), chain(1)]

    def step(m):
        next(run[m])

    def text_piece(i):
        feats = jnp.concatenate([n.nb[i // 2, 2 * (i % 2) + b] for b in range(2)], axis=1)
        part = dot(n.tt[:, 512 * i : 512 * i + 512], feats, NT)
        if i == 0:
            n.tl[...] = part
        else:
            n.tl[...] += part

    def text_back(a):
        part = dot(n.tgr[...], n.tt[:, 1024 * a : 1024 * a + 1024])
        for b in range(4):
            n.t_s[a, b] = part[:, 256 * b : 256 * b + 256].astype(bf16)

    weights.forward()
    step(0)
    step(1)
    norm_y.forward()
    weights.finish()
    weights_z = RingGather(
        out, at, "z",
        lambda i, hf: n.wb.at[span(hf, 4), i, mine],
        lambda k: n.wb.at[:, pl.ds(0, k), mine],
        n.wz_m,
    )
    step(0)
    norm_z.forward()
    norm_y.finish()
    norm_x = RingGather(
        out, at, "x", lambda i, hf: n.nb.at[i, span(hf, 4)], lambda k: n.nb.at[pl.ds(0, k)], n.nx_m
    )
    step(1)
    weights_z.forward()
    step(0)
    n.tab[at.x] = n.au[at.s]
    tab_x = RingGather(
        out, at, "x", lambda i, hf: n.tab.at[i, span(hf, 128)], lambda k: n.tab.at[pl.ds(0, k)], n.tab_m
    )
    step(1)
    norm_z.finish()
    share = n.ns.at[:, at.c]
    wait_n = out.one(share, share, n.nc_m, at.sibling())
    weights_z.finish()
    for other in (weights.right, lax.rem(at.x + 2, 4), weights.left):
        part = n.wb.at[other, :, mine]
        out.go(part, part, n.wc_m.at[0], n.wc_m.at[1], at.sibling())
    out.sent_later(n.wb.at[pl.ds(0, 3), :, mine], n.wc_m.at[0])
    wait_w = out.bytes_of(n.wb.at[pl.ds(0, 3), :, mine], n.wc_m.at[1])
    got_ids.wait_recv()
    i = lax.broadcasted_iota(jnp.int32, (128, 1024), 0)
    j = lax.broadcasted_iota(jnp.int32, (128, 1024), 1)
    same = ((i >> 6) == (j >> 9)) & (((i >> 2) & 15) == ((j >> 5) & 15)) & ((i & 3) == (j & 3))
    group = lax.broadcasted_iota(jnp.int32, (8, 1024), 0)
    j = lax.broadcasted_iota(jnp.int32, (8, 1024), 1)
    book = [at.s, jnp.maximum(at.s - 1, 0)]
    ids2 = [jnp.concatenate([n.idb[g, pl.ds(k, 1), :] for g in range(8)], axis=0) for k in book]
    spread = lax.dot_general(
        jnp.concatenate(ids2, axis=0).astype(f32), jnp.where(same, 1.0, 0.0), NN,
        precision=lax.Precision.HIGHEST, preferred_element_type=f32,
    )
    for i in range(2):
        own = jnp.where(((j >> 2) & 7) == group, spread[8 * i : 8 * i + 8], 0.0)
        n.idr[i] = jnp.sum(own, axis=0, keepdims=True).astype(jnp.int32)
    norm_x.forward()
    wait_w.wait_recv()
    step(0)
    step(1)
    wait_n.wait_recv()
    def transposed(b):
        rows = []
        for t in range(4):
            for s in range(8):
                index = 8 * lax.div(b, 4) + 2 * lax.rem(b, 4) + t // 2
                tile = unfold(n.ns[s // 2, s % 2, index], 2)
                rows.append(tile[4 * (t % 2) : 4 * (t % 2) + 4])
        cols = pl.ds(pl.multiple_of(128 * b, 128), 128)
        n.nt[:, cols] = jnp.concatenate(rows, axis=0).T.astype(bf16)

    loop(0, 8, transposed)
    step(0)
    tab_x.forward()
    step(1)
    norm_x.finish()
    loads[2].wait()
    text_piece(0)
    step(0)
    text_piece(1)
    step(1)

    def two_blocks(to):
        return n.nb.at[lax.div(to, 2), pl.ds(2 * lax.rem(to, 2), 2)]

    n.ndst[at.s] = two_blocks(at.s)[...]
    got_nd = out.spread(at.sp, 8, two_blocks, n.ndst.at[at.s], n.nd_m, n.ndst)
    for m in range(2):
        row = n.idr[0, :, pl.ds(pl.multiple_of(at.x * 128 + 512 * m, 128), 128)]
        held[m].hot = jnp.where(((row >> 7) & 3) == at.y, ((row >> 9) << 7) | (row & 127), -1)
    tab_x.finish()
    text_piece(2)
    step(0)
    step(1)
    text_piece(3)
    step(0)
    text_piece(4)
    step(1)
    text_piece(5)
    step(0)
    text_piece(6)
    step(1)
    text_piece(7)
    tl = capped(n.tl[...])
    n.tl[...] = tl
    text_hot = lax.broadcasted_iota(jnp.int32, (VOCAB, 128), 0) == n.tid[...] - at.t * VOCAB
    tsum = jnp.sum(jnp.exp(tl - soft_cap), axis=0, keepdims=True)
    tchosen = jnp.sum(jnp.where(text_hot, tl, 0.0), axis=0, keepdims=True)
    n.ty[at.y] = jnp.concatenate([tsum, tchosen, jnp.zeros((6, 128), f32)], axis=0)
    got_ty = y_same(n.ty, n.ty_m)
    step(0)
    grads = jnp.concatenate([n.gr[0], n.gr[1]], axis=1)

    def vocab_grad(b):
        cols = pl.ds(pl.multiple_of(256 * b, 256), 256)
        g = dot(grads, n.ob[:, :, :, cols].reshape(256, 256))
        for a in range(4):
            n.g_s[a, :, cols] = g[128 * a : 128 * a + 128].astype(bf16)

    loop(0, 4, vocab_grad)
    red_g = reduce("x", "g", rows_half(64))
    step(1)
    got_ty.wait_recv()
    n.tx[at.x] = jnp.sum(n.ty[...], axis=0)
    got_tx = x_same(n.tx, n.tx_m)
    got_lc = seq_all(n.lc, n.lr, n.lc_m)
    n.lr[at.s] = n.lc[at.s]
    step(0)
    got_tx.wait_recv()
    ttotal = jnp.sum(n.tx[...], axis=0)
    tlse_row = soft_cap + jnp.log(ttotal[0:1, :])
    n.tlr[...] = tlse_row - ttotal[1:2, :]
    tl = n.tl[...]
    tgrad = (jnp.exp(tl - tlse_row) - jnp.where(text_hot, 1.0, 0.0)) * cap_slope(tl)
    padded = jnp.concatenate([tgrad, jnp.zeros((1024 - VOCAB, 128), f32)], axis=0)
    n.tg[at.z, at.c] = padded.astype(bf16)
    tg_z = RingGather(
        out, at, "z",
        lambda i, hf: n.tg.at[i, at.c, span(hf, 1024)],
        lambda k: n.tg.at[pl.ds(0, k), at.c],
        n.tgz_m,
    )
    n.tgr[...] = padded.T[:, 0:VOCAB].astype(bf16)
    step(1)
    red_g.forward()
    text_back(0)
    step(0)
    text_back(1)
    step(1)
    text_back(2)
    step(0)
    text_back(3)
    red_t = reduce("x", "t", rows_half(2))
    step(1)

    for c in range(4):
        n.trt[c] = n.tri[:, c].reshape(256, 256).astype(f32).T.astype(bf16)

    def weight_grad(zz):
        cols = pl.ds(pl.multiple_of(256 * zz, 256), 256)
        to = pl.ds(pl.multiple_of(128 * zz, 128), 128)
        g = dot(n.trt[0:3].reshape(768, 256), n.dob[0, :, :, :, cols].reshape(256, 256))
        last = dot(n.trt[3], n.dob[1, :, :, :, cols].reshape(256, 256))
        for core in range(2):
            for a in range(4):
                for c in range(4):
                    rows = last[64 * a : 64 * a + 64] if c == 3 else g[256 * c + 64 * a : 256 * c + 64 * a + 64]
                    n.gas[core, a, c, :, to] = rows[:, 128 * core : 128 * core + 128].astype(bf16)

    step(0)
    tg_z.forward()
    red_g.finish()
    g = red_g.total()
    for b in range(8):
        n.gts[b] = g[:, 128 * b : 128 * b + 128].astype(bf16)
    got_gt = seq_all(n.gts, n.gtr, n.gt_m)
    n.gtr[at.s] = n.gts[at.s]
    step(1)
    loop(0, 2, weight_grad)
    step(0)
    loop(2, 4, weight_grad)
    step(1)
    theirs = n.gas.at[1 - at.c]
    wait_gar = out.one(theirs, n.gar, n.gar_m, at.sibling())
    red_t.forward()
    term = held[0].gain_term + held[1].gain_term
    n.dgs[at.s] = jnp.concatenate([term[:, 128 * b : 128 * b + 128] for b in range(8)], axis=0)
    got_dgs = seq_same(n.dgs, n.dgs_m)
    got_lc.wait_recv()
    lane = lax.broadcasted_iota(jnp.int32, (16, 128), 1)
    for m in range(2):
        losses = jnp.zeros((16, 128), f32)
        for k in range(8):
            losses = jnp.where(lane == 1 + k, n.lr[k, m], losses)
        n.lx[at.x, m] = losses
    got_lx = x_same(n.lx, n.lx_m)
    tg_z.finish()
    share_t = n.tg.at[:, at.c]
    wait_t = out.one(share_t, share_t, n.tgc_m, at.sibling())
    step(0)

    def features(m):
        block = dot(n.ib[m].reshape(512, DD), n.pj[at.s], NT)
        for a in range(4):
            for s in range(8):
                lo = 128 * a + 4 * s
                rows = [block[lo + 32 * b : lo + 32 * b + 4] for b in range(4)]
                rows = jnp.concatenate(rows, axis=0).astype(bf16)
                n.sf[s % 2, s // 2, 64 * m + 16 * a : 64 * m + 16 * a + 16, :] = rows

    def hot_before(m):
        prev = jnp.where(at.s > 0, n.idr[1, :, 512 * m : 512 * m + 512] - at.t * 128, -1)
        entry = lax.broadcasted_iota(jnp.int32, (128, 512), 0)
        return jnp.where(prev == entry, 1.0, 0.0).astype(bf16)

    features(0)
    red_t.finish()
    for b in range(4):
        n.t2_s[b] = red_t.total(lambda ref: ref[b]).astype(bf16)
    red_t2 = reduce("y", "t2", rows_half(64))
    wait_gar.wait_recv()
    for a in range(4):
        n.ga_s[a] = (n.gas[at.c, a].astype(f32) + n.gar[a].astype(f32)).astype(bf16)
    red_ga = reduce("x", "ga", rows_half(2))
    left0 = jnp.concatenate([n.nt[:, 0:512], hot_before(0)], axis=0)

    def first_half(b):
        cols = pl.ds(pl.multiple_of(256 * b, 256), 256)
        g = dot(left0, n.ib[0, :, :, :, cols].reshape(512, 256))
        for i in range(3):
            n.raw[i, :, cols] = g[128 * i : 128 * i + 128]

    loop(0, 4, first_half)
    red_t2.forward()
    step(1)
    features(1)
    wait_sf = out.one(n.sf.at[1 - at.c], n.sfr, n.sfr_m, at.sibling())

    left1 = jnp.concatenate([n.nt[:, 512:1024], hot_before(1)], axis=0)

    def proj_grad(d):
        to = lax.rem(at.z + d, 4)
        cols = pl.ds(pl.multiple_of(to * 256, 256), 256)
        g = dot(left1, n.ib[1, :, :, :, cols].reshape(512, 256))
        g = g + jnp.concatenate([n.raw[i, :, cols] for i in range(3)], axis=0)
        g = jnp.concatenate([g[0:256], g[256:384] * embed_scale], axis=0)
        n.gas_all[2 * to, 0:384, :] = g[:, 0:128].astype(bf16)
        n.gas_all[2 * to + 1, 0:384, :] = g[:, 128:256].astype(bf16)

    def send_proj(d):
        proj_grad(d)
        to = lax.rem(at.z + d, 4)
        for core in range(2):
            src = n.gas_all.at[2 * to + core]
            out.go(src, n.gar_all.at[at.s], n.gall_m.at[0], n.gall_m.at[1], {"z": to, "core": core})

    right, far, left = lax.rem(at.z + 1, 4), lax.rem(at.z + 2, 4), lax.rem(at.z + 3, 4)
    low, high = pl.ds(0, 192), pl.ds(192, 192)
    proj_grad(2)
    for core in range(2):
        src = n.gas_all.at[2 * far + core]
        out.go(src.at[low], n.rel.at[0, core], n.rel_m.at[0], n.rel_m.at[1], {"z": right})
        out.go(src.at[high], n.rel.at[1, core], n.rel_m.at[0], n.rel_m.at[2], {"z": left})
    wait_sf.wait_recv()
    for b in range(4):
        n.f_s[b] = (n.sf[at.c, b].astype(f32) + n.sfr[b].astype(f32)).astype(bf16)
    red_f = direct("z", "f")
    red_t2.finish()
    send_proj(1)
    send_proj(3)
    out.bytes_of(n.rel.at[0], n.rel_m.at[1]).wait_recv()
    out.bytes_of(n.rel.at[1], n.rel_m.at[2]).wait_recv()
    for core in range(2):
        there = n.gar_all.at[2 * left + at.c, low]
        out.go(n.rel.at[0, core], there, n.gall_m.at[0], n.gall_m.at[1], {"z": right, "core": core})
        there = n.gar_all.at[2 * right + at.c, high]
        out.go(n.rel.at[1, core], there, n.gall_m.at[0], n.gall_m.at[1], {"z": left, "core": core})
    out.sent_later(n.rel, n.rel_m.at[0])
    proj_grad(0)
    n.gar_all[at.s] = n.gas_all[at.s]
    theirs = 2 * at.z + 1 - at.c
    out.go(n.gas_all.at[theirs], n.gar_all.at[at.s], n.gall_m.at[0], n.gall_m.at[1], at.sibling())
    out.sent_later(n.gas_all.at[pl.ds(0, 7)], n.gall_m.at[0])
    got_all = out.bytes_of(n.gar_all.at[pl.ds(0, 7)], n.gall_m.at[1])
    red_f.finish()
    fb = red_t2.total() + red_f.total()
    gback = fb * gain
    inner = jnp.sum(gback * hat, axis=1, keepdims=True)
    n.rd[at.t] = jnp.broadcast_to(inner, (128, 128)).T[0:8, :]
    got_rd = plane_same(n.rd, n.rd_m)
    n.tgn[at.s] = jnp.broadcast_to(jnp.sum(fb * hat, axis=0, keepdims=True), (8, 256))
    got_tgn = seq_same(n.tgn, n.tgn_m)
    red_ga.forward()
    got_dgs.wait_recv()
    n.dgy[at.y] = jnp.sum(n.dgs[...], axis=0)
    got_dgy = y_same(n.dgy, n.dgy_m)

    wait_t.wait_recv()
    got_nd.wait_recv()

    def table_grad(a):
        part = pl.ds(pl.multiple_of(512 * a, 512), 512)
        left = jnp.concatenate([n.tg[g // 2, g % 2, part, :] for g in range(8)], axis=1)
        for b in range(2):
            right = n.ndst[:, b].reshape(1024, 256)
            n.o_gtt[part, 256 * b : 256 * b + 256] = dot(left, right).astype(bf16)

    loop(0, 2, table_grad)
    got_dgy.wait_recv()
    n.dgx[at.x] = jnp.sum(n.dgy[...], axis=0)
    got_dgx = x_same(n.dgx, n.dgx_m)
    red_ga.finish()
    for b in range(4):
        n.gz_s[b] = red_ga.total(lambda ref: ref[:, :, 128 * b : 128 * b + 128]).astype(bf16)
    red_gz = direct("z", "gz")
    got_rd.wait_recv()
    dots = twice(row_to_col(jnp.sum(n.rd[...], axis=0)[0:1, :], 128))
    n.o_gh[...] = scale * (gback - hat * (dots / D))
    got_tgn.wait_recv()
    n.o_tgain[...] = jnp.sum(n.tgn[...], axis=0)[0:1, :]
    got_lx.wait_recv()
    losses = jnp.concatenate([n.lx[a, m] for m in range(2) for a in range(4)], axis=0).T
    n.o_loss[...] = jnp.concatenate([n.tlr[...], losses[1:9]], axis=0)
    got_dgx.wait_recv()
    n.o_dg[...] = jnp.sum(n.dgx[...], axis=0)
    got_gt.wait_recv()
    got_all.wait_recv()
    n.o_gp[...] = n.gar_all[:, 0:256, :]
    for k in range(8):
        g = n.gtr[k].astype(f32)
        if k < 7:
            g = g + n.gar_all[k + 1, 256:384, :].astype(f32)
        n.o_gtab[k] = g
    red_gz.finish()
    ga = red_gz.total()
    n.o_gqkv[...] = ga[0:3]
    n.o_gout[...] = ga[3]
    out.finish()


def write_kernel(*refs):
    count = len(refs) // 2
    for src, dst in zip(refs[:count], refs[count:]):
        dst[...] = src[...].astype(f32)


def write_outputs(results):
    shapes = [r.shape for r in results]
    shapes[3] = (VOCAB, 512)
    blocks = {1: (32, 256), 3: (256, 512), 4: (2, 256, 128), 5: (2, 128, 128)}

    def spec(i):
        block = blocks.get(i, shapes[i])
        moves = i in blocks
        return pl.BlockSpec(block, lambda g: (g if moves else 0,) + (0,) * (len(block) - 1))

    return pl.pallas_call(
        write_kernel,
        out_shape=[jax.ShapeDtypeStruct(shape, f32) for shape in shapes],
        grid=(4,),
        in_specs=[spec(i) for i in range(9)],
        out_specs=[spec(i) for i in range(9)],
        name="write",
    )(*results)


def on_device(
    hidden, text_gain, text_table, proj, audio_table, depth_gain, attn_qkv, attn_out, text_ids, audio_ids
):
    vmem = pl.BlockSpec(memory_space=pltpu.VMEM)
    hbm = pl.BlockSpec(memory_space=pl.ANY)
    outs = [
        ((9, 128), f32), ((128, 256), f32), ((1, 256), f32), ((1024, 512), bf16), ((8, 256, 128), bf16),
        ((8, 128, 128), f32), ((8, 128), f32), ((3, 64, 128), f32), ((64, 128), f32),
    ]
    results = pl.pallas_call(
        kernel,
        out_shape=[jax.ShapeDtypeStruct(shape, dtype) for shape, dtype in outs],
        in_specs=[vmem, vmem, hbm, hbm, hbm, vmem, vmem, vmem, vmem, vmem],
        out_specs=[vmem] * len(outs),
        scratch_shapes=[scratch_shape(entry) for entry in SCRATCH],
        name="head",
        compiler_params=pltpu.CompilerParams(
            collective_id=1, has_side_effects=True, vmem_limit_bytes=VMEM_LIMIT
        ),
    )(
        hidden, text_gain, text_table, proj, audio_table, depth_gain,
        jnp.transpose(attn_qkv, (1, 2, 0)), attn_out, text_ids[None, :], audio_ids.T,
    )
    losses, gh, tgain, gtt, gp, gtab, dg, gqkv, gout = write_outputs(results)
    return losses.T, gh, tgain[0], gtt.T, gp, gtab, dg.reshape(DD), jnp.transpose(gqkv, (2, 0, 1)), gout


def solution(mesh):
    fine = Mesh(mesh.devices.reshape(4, 2, 4, 4), ("z", "core", "x", "y"))
    seq = ("z", "core")
    tp = ("x", "y")
    in_specs = (
        P(seq, tp), P(tp), P(tp, None), P(None, tp, None), P(None, tp, None),
        P(), P(None, None, tp), P(tp, None), P(seq), P(seq, None),
    )
    out_specs = (
        P(seq, None), P(seq, tp), P(tp), P(seq, tp), P(None, tp, seq),
        P(None, tp, seq), P(), P(seq, None, tp), P(tp, seq),
    )
    return jax.shard_map(
        on_device, mesh=fine, in_specs=in_specs, out_specs=out_specs, check_vma=False
    )
```

```python
import math

import jax
import jax.numpy as jnp
from jax import lax
from jax.experimental import pallas as pl
from jax.experimental.pallas import tpu as pltpu
from jax.sharding import Mesh
from jax.sharding import PartitionSpec as P

D = 4096
DD = 1024
HEAD = 64
VOCAB = 1000
MESH = pl.DeviceIdType.MESH
VMEM_LIMIT = 62 * 1024 * 1024

soft_cap = 12.0
epsilon = 1e-05
embed_scale = math.sqrt(DD) / 4.0
f32 = jnp.float32
bf16 = jnp.bfloat16

NN = (((1,), (0,)), ((), ()))
NT = (((1,), (1,)), ((), ()))
TN = (((0,), (0,)), ((), ()))


def dot(a, b, dims=NN):
    return lax.dot_general(a, b, dims, preferred_element_type=f32)


def capped(values):
    return soft_cap * jnp.tanh(values / soft_cap)


def cap_slope(capped_values):
    ratio = capped_values / soft_cap
    return 1.0 - ratio * ratio


class Place:
    def __init__(self):
        self.z = lax.axis_index("z")
        self.c = lax.axis_index("core")
        self.x = lax.axis_index("x")
        self.y = lax.axis_index("y")
        self.s = self.z * 2 + self.c
        self.t = self.x * 4 + self.y
        z, c, x, y = self.z, self.c, self.x, self.y
        self.sibling = (z, 1 - c, x, y)
        self.known = {}
        for d in range(1, 4):
            to = lax.rem(x + d, 4)
            self.known["x", d] = (to, (z, c, to, y))
            to = lax.rem(y + d, 4)
            self.known["y", d] = (to, (z, c, x, to))
            to = lax.rem(z + d, 4)
            self.known["z", d] = (to, (to, c, x, y))
        for d in range(1, 8):
            to = lax.rem(self.s + d, 8)
            self.known["s", d] = (to, (lax.div(to, 2), lax.rem(to, 2), x, y))
        for d in range(1, 16):
            to = lax.rem(self.t + d, 16)
            self.known["t", d] = (to, (z, c, lax.div(to, 4), lax.rem(to, 4)))

    def peer(self, axis, d):
        return self.known[axis, d]

    def index(self, axis):
        return {"x": self.x, "y": self.y, "z": self.z, "s": self.s, "t": self.t}[axis]


class Sends:
    def __init__(self, at):
        self.at = at
        self.pending = []

    def go(self, src, dst, send, recv, device):
        pltpu.make_async_remote_copy(
            src_ref=src, dst_ref=dst, send_sem=send, recv_sem=recv, device_id=device, device_id_type=MESH
        ).start()

    def bytes_of(self, ref, sem):
        return pltpu.make_async_remote_copy(
            src_ref=ref, dst_ref=ref, send_sem=sem, recv_sem=sem,
            device_id=self.at.sibling, device_id_type=MESH,
        )

    def sent_later(self, ref, sem):
        self.pending.append(self.bytes_of(ref, sem))

    def one(self, src, dst, sems, device):
        self.go(src, dst, sems.at[0], sems.at[1], device)
        self.sent_later(src, sems.at[0])
        return self.bytes_of(dst, sems.at[1])

    def spread(self, axis, n, src, dst, sems, slots, all_bytes=None):
        for d in range(1, n):
            to, device = self.at.peer(axis, d)
            self.go(src(to), dst, sems.at[0], sems.at[1], device)
        if all_bytes is None:
            all_bytes = slots.at[pl.ds(0, n - 1)]
        self.sent_later(all_bytes, sems.at[0])
        return self.bytes_of(all_bytes, sems.at[1])

    def finish(self):
        for wait in self.pending:
            wait.wait_send()


class RingGather:
    def __init__(self, out, at, axis, part, slots, sems):
        self.out, self.part, self.sems, self.slots = out, part, sems, slots
        self.right, self.to_right = at.peer(axis, 1)
        self.left, self.to_left = at.peer(axis, 3)
        block = part(at.index(axis), None)
        out.go(block, block, sems.at[0], sems.at[1], self.to_right)
        out.go(block, block, sems.at[0], sems.at[2], self.to_left)
        out.sent_later(slots(3), sems.at[0])

    def forward(self):
        out, part, sems = self.out, self.part, self.sems
        out.bytes_of(part(self.left, None), sems.at[1]).wait_recv()
        one = part(self.left, 0)
        out.go(one, one, sems.at[0], sems.at[3], self.to_right)
        out.bytes_of(part(self.right, None), sems.at[2]).wait_recv()
        two = part(self.right, 1)
        out.go(two, two, sems.at[0], sems.at[3], self.to_left)

    def finish(self):
        self.out.bytes_of(self.slots(1), self.sems.at[3]).wait_recv()


class RingReduce:
    def __init__(self, out, at, axis, blocks, half, bufs, sems):
        self.out, self.half, self.sems, self.blocks = out, half, sems, blocks
        self.me, far = at.index(axis), at.peer(axis, 2)[0]
        self.right, self.to_right = at.peer(axis, 1)
        self.left, self.to_left = at.peer(axis, 3)
        self.rl, self.rr, self.fa, self.fb = bufs
        s = blocks
        out.go(half(s.at[far], 0), self.fa, sems.at[0], sems.at[1], self.to_right)
        out.go(half(s.at[far], 1), self.fb, sems.at[0], sems.at[2], self.to_left)
        out.go(half(s.at[self.right], 1), half(self.rl, 1), sems.at[0], sems.at[3], self.to_right)
        out.go(half(s.at[self.left], 0), half(self.rr, 0), sems.at[0], sems.at[3], self.to_left)
        out.sent_later(s.at[pl.ds(0, 3)], sems.at[0])

    def forward(self):
        s, half, out, sems = self.blocks, self.half, self.out, self.sems
        out.bytes_of(self.fa, sems.at[1]).wait_recv()
        one = half(s.at[self.right], 0)
        one[...] = (one[...].astype(f32) + self.fa[...].astype(f32)).astype(bf16)
        out.go(one, half(self.rl, 0), sems.at[0], sems.at[3], self.to_right)
        out.bytes_of(self.fb, sems.at[2]).wait_recv()
        two = half(s.at[self.left], 1)
        two[...] = (two[...].astype(f32) + self.fb[...].astype(f32)).astype(bf16)
        out.go(two, half(self.rr, 1), sems.at[0], sems.at[3], self.to_left)

    def finish(self):
        self.out.bytes_of(self.blocks.at[pl.ds(0, 2)], self.sems.at[3]).wait_recv()

    def total(self, pick=lambda ref: ref[...]):
        own = pick(self.blocks.at[self.me]).astype(f32)
        return own + pick(self.rl).astype(f32) + pick(self.rr).astype(f32)


class DirectReduce:
    def __init__(self, out, at, axis, blocks, got, sems):
        self.blocks, self.got = blocks, got
        self.me = at.index(axis)
        for d in (2, 1, 3):
            to, device = at.peer(axis, d)
            out.go(blocks.at[to], got.at[d - 1], sems.at[0], sems.at[1], device)
        out.sent_later(blocks.at[pl.ds(0, 3)], sems.at[0])
        self.wait = out.bytes_of(got, sems.at[1])

    def finish(self):
        self.wait.wait_recv()

    def total(self, pick=lambda ref: ref[...]):
        own = pick(self.blocks.at[self.me]).astype(f32)
        for d in range(3):
            own = own + pick(self.got.at[d]).astype(f32)
        return own


def span(h, size):
    if h is None:
        return pl.ds(0, size)
    return pl.ds(h * (size // 2), size // 2)


def rows_half(n):
    return lambda ref, h: ref.at[pl.ds(h * n, n)]


def row_to_col(row, lanes):
    return jnp.broadcast_to(row, (lanes, row.shape[1])).T


def twice(col):
    return jnp.concatenate([col, col], axis=1)


def fold(rows, n):
    w = rows.shape[1] // n
    return jnp.concatenate([rows[:, i * w : i * w + w] for i in range(n)], axis=0).astype(bf16)


def unfold(packed, n):
    r = packed.shape[0] // n
    wide = packed.astype(f32)
    return jnp.concatenate([wide[i * r : i * r + r] for i in range(n)], axis=1)


def by_step(rows):
    return [fold(rows[4 * k : 4 * k + 4], 4) for k in range(8)]


def from_steps(ref):
    return jnp.concatenate([unfold(ref[k], 4) for k in range(8)], axis=0)


def head_masks(rows):
    lane = lax.broadcasted_iota(jnp.int32, (rows, 256), 1)
    return [(lane >= 64 * h) & (lane < 64 * h + 64) for h in range(4)]


def step_mask():
    i = lax.broadcasted_iota(jnp.int32, (128, 128), 0)
    j = lax.broadcasted_iota(jnp.int32, (128, 128), 1)
    return ((i & 3) == (j & 3)) & ((i >> 5) == (j >> 5)) & (j <= i)


def attention(qh, kk, allowed):
    scores = dot(qh, kk, NT) / math.sqrt(HEAD)
    raised = jnp.where(allowed, jnp.exp(scores), 0.0)
    return raised / jnp.sum(raised, axis=1, keepdims=True)


def ring_reduce_scratch(name, block, half):
    return [
        (name + "_s", (4,) + block, bf16),
        (name + "_rl", block, bf16),
        (name + "_rr", block, bf16),
        (name + "_fa", half, bf16),
        (name + "_fb", half, bf16),
        (name + "_m", 4, None),
    ]


def direct_scratch(name, block):
    return [(name + "_s", (4,) + block, bf16), (name + "_r", (3,) + block, bf16), (name + "_m", 2, None)]


def chain_scratch(m):
    m = str(m)
    return [
        *ring_reduce_scratch("p" + m, (4, 16, DD), (2, 16, DD)),
        *ring_reduce_scratch("q" + m, (4, 16, DD), (2, 16, DD)),
        *direct_scratch("pp" + m, (16, DD)),
        *direct_scratch("qq" + m, (16, DD)),
        ("dn_m" + m, 2, None),
        *direct_scratch("h" + m, (32, DD)),
        ("a1s" + m, (8, 16, 256), bf16), ("a1r" + m, (8, 16, 256), bf16), ("a1_m" + m, 2, None),
        ("a2s" + m, (8, 16, 256), bf16), ("a2r" + m, (8, 16, 256), bf16), ("a2_m" + m, 2, None),
        ("a3s" + m, (8, 16, 256), bf16), ("a3r" + m, (8, 16, 256), bf16), ("a3_m" + m, 2, None),
        ("ob_m" + m, 2, None), ("e" + m, (4, 8, 128), f32), ("e_m" + m, 2, None),
        *direct_scratch("v" + m, (32, DD)),
        *direct_scratch("c" + m, (32, DD)),
        ("obb_m" + m, 2, None),
    ]


SCRATCH = [
    ("tt", (VOCAB, D), bf16), ("pj", (8, 256, DD), bf16), ("au", (8, 128, DD), bf16), ("load", 3, 0),
    ("ssq", (16, 8, 128), f32), ("ssq_m", 2, None),
    ("idb", (8, 8, 128), jnp.int32), ("idb_m", 2, None), ("idr", (2, 1, 1024), jnp.int32),
    ("raw", (8, 128, DD), f32), ("look", (8, 128, DD), bf16),
    ("wb", (4, 4, 64, DD), bf16), ("wb_m", 4, None), ("wz_m", 4, None), ("wc_m", 2, None),
    ("nb", (4, 4, 128, 256), bf16), ("ny_m", 4, None), ("nx_m", 4, None),
    ("ns", (4, 2, 16, 16, 128), bf16), ("nz_m", 4, None), ("nc_m", 2, None),
    *chain_scratch(0), *chain_scratch(1),
    ("dob", (2, 2, 4, 32, DD), bf16), ("qkv", (2, 3, 128, 256), bf16),
    ("ex", (2, 4, 128, 128), f32), ("ob", (2, 4, 32, DD), bf16),
    ("gr", (2, 512, 128), bf16), ("tri", (2, 4, 128, 256), bf16), ("trt", (4, 256, 256), bf16),
    ("tab", (4, 128, DD), bf16), ("tab_m", 4, None),
    ("tl", (VOCAB, 128), f32), ("ty", (4, 8, 128), f32), ("ty_m", 2, None), ("tx", (4, 8, 128), f32), ("tx_m", 2, None),
    ("tgr", (128, VOCAB), bf16), ("tlr", (1, 128), f32),
    *ring_reduce_scratch("g", (128, DD), (64, DD)),
    ("lc", (8, 2, 16, 128), f32), ("lr", (8, 2, 16, 128), f32), ("lc_m", 2, None),
    ("lx", (4, 2, 16, 128), f32), ("lx_m", 2, None),
    ("nt", (256, 1024), bf16), ("tg", (4, 2, 1024, 128), bf16), ("tgz_m", 4, None), ("tgc_m", 2, None),
    *ring_reduce_scratch("t", (4, 128, 256), (2, 128, 256)),
    *ring_reduce_scratch("t2", (128, 256), (64, 256)),
    ("ndst", (8, 2, 128, 256), bf16), ("nd_m", 2, None),
    ("ib", (2, 4, 4, 32, DD), bf16), ("i0x_m", 2, None), ("i0y_m", 4, None),
    ("iax_m", 2, None), ("iay_m", 4, None), ("ibx_m", 4, None), ("iby_m", 2, None),
    ("gas", (2, 4, 4, 64, 512), bf16), ("gar", (4, 4, 64, 512), bf16), ("gar_m", 2, None),
    *ring_reduce_scratch("ga", (4, 64, 512), (2, 64, 512)),
    *direct_scratch("gz", (4, 64, 128)),
    ("sf", (2, 4, 128, 256), bf16), ("sfr", (4, 128, 256), bf16), ("sfr_m", 2, None),
    *direct_scratch("f", (128, 256)),
    ("gas_all", (8, 384, 128), bf16), ("gar_all", (8, 384, 128), bf16), ("gall_m", 2, None),
    ("rel", (2, 2, 192, 128), bf16), ("rel_m", 3, None),
    ("gts", (8, 128, 128), bf16), ("gtr", (8, 128, 128), bf16), ("gt_m", 2, None),
    ("dgs", (8, 8, 128), f32), ("dgs_m", 2, None), ("dgy", (4, 8, 128), f32), ("dgy_m", 2, None),
    ("dgx", (4, 8, 128), f32), ("dgx_m", 2, None),
    ("rd", (16, 8, 128), f32), ("rd_m", 2, None), ("tgn", (8, 8, 256), f32), ("tgn_m", 2, None),
]


def scratch_shape(entry):
    name, shape, dtype = entry
    if dtype is None or isinstance(dtype, int):
        return pltpu.SemaphoreType.DMA((shape,))
    return pltpu.VMEM(shape, dtype)


class Named:
    pass


def loop(low, high, body):
    def one(i, carry):
        body(i)
        return carry

    lax.fori_loop(low, high, one, 0)


INPUTS = ["hid", "gain", "table", "proj", "audio", "dgain", "wqkv", "wout", "tid", "ids"]
OUTPUTS = ["o_loss", "o_gh", "o_tgain", "o_gtt", "o_gp", "o_gtab", "o_dg", "o_gqkv", "o_gout"]


def kernel(*refs):
    n = Named()
    names = INPUTS + OUTPUTS + [entry[0] for entry in SCRATCH]
    for name, ref in zip(names, refs):
        setattr(n, name, ref)
    at = Place()
    out = Sends(at)

    def reduce(axis, name, half):
        bufs = [getattr(n, name + suffix) for suffix in ("_rl", "_rr", "_fa", "_fb")]
        return RingReduce(out, at, axis, getattr(n, name + "_s"), half, bufs, getattr(n, name + "_m"))

    def direct(axis, name):
        return DirectReduce(
            out, at, axis, getattr(n, name + "_s"), getattr(n, name + "_r"), getattr(n, name + "_m")
        )

    def seq_all(src, dst, sems):
        return out.spread("s", 8, lambda to: src.at[to], dst.at[at.s], sems, dst)

    def seq_same(ref, sems):
        return out.spread("s", 8, lambda to: ref.at[at.s], ref.at[at.s], sems, ref)

    def plane_same(ref, sems):
        return out.spread("t", 16, lambda to: ref.at[at.t], ref.at[at.t], sems, ref)

    def x_same(ref, sems):
        return out.spread("x", 4, lambda to: ref.at[at.x], ref.at[at.x], sems, ref)

    def y_same(ref, sems):
        return out.spread("y", 4, lambda to: ref.at[at.y], ref.at[at.y], sems, ref)

    loads = [
        pltpu.make_async_copy(src, dst, n.load.at[i])
        for i, (src, dst) in enumerate([(n.proj, n.pj), (n.audio, n.au), (n.table, n.tt)])
    ]
    for copy in loads:
        copy.start()
    for c in range(3):
        n.wb[at.x, c] = n.wqkv[c]
    n.wb[at.x, 3] = n.wout[...]
    barrier = pltpu.get_barrier_semaphore()
    for axis, count in (("t", 16), ("s", 8)):
        for d in range(1, count):
            device = at.peer(axis, d)[1]
            pl.semaphore_signal(barrier, inc=1, device_id=device, device_id_type=MESH)
    h = n.hid[...].astype(f32)
    gain = n.gain[...].astype(f32)[None, :]
    dgain = n.dgain[...].astype(f32)[None, :]
    ones = jnp.ones((8, 256), f32)
    n.ssq[at.t] = lax.dot_general(
        ones, h * h, NT, precision=lax.Precision.HIGHEST, preferred_element_type=f32
    )
    n.idb[at.s] = n.ids[...]
    unscaled = (h * gain).astype(bf16)
    pl.semaphore_wait(barrier, 22)

    got_ssq = plane_same(n.ssq, n.ssq_m)
    mine = pl.ds(pl.multiple_of(at.c * 32, 32), 32)
    weights = RingGather(
        out, at, "x",
        lambda i, hf: n.wb.at[i, at.z, mine] if hf is None
        else n.wb.at[i, at.z, pl.ds(pl.multiple_of(at.c * 32 + 16 * hf, 16), 16)],
        lambda k: n.wb.at[pl.ds(0, k), at.z, mine],
        n.wb_m,
    )
    got_ids = seq_same(n.idb, n.idb_m)
    loads[0].wait()

    def raw_step(k):
        n.raw[k] = dot(unscaled, n.pj[k])

    loop(0, 8, raw_step)
    loads[1].wait()
    entry = (lax.broadcasted_iota(jnp.int32, (128, 128), 1) + at.t * 128).astype(f32)
    n.look[0] = jnp.zeros((128, DD), bf16)

    def look_step(k):
        column = row_to_col(n.ids[pl.ds(k, 1), :].astype(f32), 128)
        hot = jnp.where(column == entry, 1.0, 0.0).astype(bf16)
        n.look[k + 1] = (dot(hot, n.au[k]) * embed_scale).astype(bf16)

    loop(0, 7, look_step)
    got_ssq.wait_recv()
    scale = row_to_col(lax.rsqrt(jnp.sum(n.ssq[...], axis=0)[0:1, :] / D + epsilon), 128)
    column = scale[:, 0:1]
    scale = twice(scale)
    hat = h * scale

    first = []
    for m in range(2):
        ps, qs = getattr(n, f"p{m}_s"), getattr(n, f"q{m}_s")
        part = slice(64 * m, 64 * m + 64)

        def scaled(k):
            return n.raw[k, part, :] * column[part] + n.look[k, part, :].astype(f32)

        def to_x(k):
            p = scaled(k)
            for b in range(4):
                ps[b, k] = p[16 * b : 16 * b + 16].astype(bf16)

        def to_y(k):
            p = scaled(k + 4)
            for b in range(4):
                rows = [p[16 * a + 4 * b : 16 * a + 4 * b + 4] for a in range(4)]
                qs[b, k] = jnp.concatenate(rows, axis=0).astype(bf16)

        loop(0, 4, to_x)
        red_p = reduce("x", f"p{m}", rows_half(2))
        loop(0, 4, to_y)
        first.append((red_p, reduce("y", f"q{m}", rows_half(2))))
    normed_f = hat * gain
    n.nb[at.x, at.y] = normed_f.astype(bf16)
    for b in range(16):
        n.ns[at.z, at.c, b] = fold(normed_f[8 * b : 8 * b + 8], 2)
    norm_z = RingGather(
        out, at, "z",
        lambda i, hf: n.ns.at[i, at.c, span(hf, 16)],
        lambda k: n.ns.at[pl.ds(0, k), at.c],
        n.nz_m,
    )
    norm_y = RingGather(
        out, at, "y",
        lambda i, hf: n.nb.at[at.x, i, span(hf, 128)],
        lambda k: n.nb.at[at.x, pl.ds(0, k)],
        n.ny_m,
    )

    masks = head_masks(128)
    allowed = step_mask()
    held = [Named(), Named()]

    def wcat(c):
        return jnp.concatenate([n.wb[a, c] for a in range(4)], axis=0)

    def half_of(m, name):
        return getattr(n, name + str(m))

    def chain(m):
        mine = held[m]
        red_p, red_q = first[m]
        red_p.forward()
        red_q.forward()
        yield
        for red, to, axis in ((red_p, "pp", "y"), (red_q, "qq", "x")):
            red.finish()
            total = [red.total(lambda ref: ref[k]) for k in range(4)]
            for b in range(4):
                rows = [total[k][4 * b : 4 * b + 4] for k in range(4)]
                getattr(n, f"{to}{m}_s")[b] = jnp.concatenate(rows, axis=0).astype(bf16)
            if axis == "y":
                red_pp = direct("y", f"pp{m}")
            else:
                red_qq = direct("x", f"qq{m}")
        yield
        red_pp.finish()
        red_qq.finish()
        di = jnp.concatenate([red_pp.total(), red_qq.total()], axis=0)
        mine.dscale = lax.rsqrt(jnp.mean(di * di, axis=1, keepdims=True) + epsilon)
        mine.dhat = di * mine.dscale
        n.dob[0, m, at.y] = (mine.dhat * dgain).astype(bf16)
        got = y_same(n.dob.at[0, m], half_of(m, "dn_m"))
        yield
        got.wait_recv()
        dnv = n.dob[0, m].reshape(128, DD)
        for c in range(3):
            n.qkv[m, c] = dot(dnv, wcat(c), NT).astype(bf16)
        q, k, v = n.qkv[m, 0], n.qkv[m, 1], n.qkv[m, 2]
        mixed = jnp.zeros((128, 256), f32)
        for hd in range(4):
            qh = jnp.where(masks[hd], q, jnp.zeros_like(q))
            exact = attention(qh, k, allowed)
            n.ex[m, hd] = exact
            mixed = jnp.where(masks[hd], dot(exact.astype(bf16), v), mixed)
        n.tri[m, 3] = mixed.astype(bf16)
        terms = dot(n.tri[m, 3], wcat(3))
        for b in range(4):
            getattr(n, f"h{m}_s")[b] = terms[32 * b : 32 * b + 32].astype(bf16)
        red_h = direct("y", f"h{m}")
        yield
        red_h.finish()
        src, dst = half_of(m, "a1s"), half_of(m, "a1r")
        for k, block in enumerate(by_step(di + red_h.total())):
            src[k] = block
        got = seq_all(src, dst, half_of(m, "a1_m"))
        dst[at.s] = src[at.s]
        yield
        got.wait_recv()
        n.ob[m, at.y] = from_steps(dst).astype(bf16)
        got = y_same(n.ob.at[m], half_of(m, "ob_m"))
        yield
        got.wait_recv()
        rows = n.ob[m].reshape(128, DD)
        tab = n.tab[...].reshape(512, DD)
        logits = capped(dot(tab, rows, NT))
        hot = mine.hot == lax.broadcasted_iota(jnp.int32, (512, 128), 0)
        sums = jnp.sum(jnp.exp(logits - soft_cap), axis=0, keepdims=True)
        chosen = jnp.sum(jnp.where(hot, logits, 0.0), axis=0, keepdims=True)
        e = half_of(m, "e")
        e[at.y] = jnp.concatenate([sums, chosen, jnp.zeros((6, 128), f32)], axis=0)
        got = y_same(e, half_of(m, "e_m"))
        yield
        got.wait_recv()
        total = jnp.sum(e[...], axis=0)
        lse_row = soft_cap + jnp.log(total[0:1, :])
        grad = (jnp.exp(logits - lse_row) - jnp.where(hot, 1.0, 0.0)) * cap_slope(logits)
        n.gr[m] = grad.astype(bf16)
        terms = dot(grad.T.astype(bf16), tab)
        for b in range(4):
            getattr(n, f"v{m}_s")[b] = terms[32 * b : 32 * b + 32].astype(bf16)
        red_v = direct("y", f"v{m}")
        loss = row_to_col(lse_row - total[1:2, :], 128)
        for g in range(8):
            rows = [loss[32 * b + 4 * g : 32 * b + 4 * g + 4] for b in range(4)]
            n.lc[g, m] = jnp.concatenate(rows, axis=0)
        yield
        red_v.finish()
        src, dst = half_of(m, "a2s"), half_of(m, "a2r")
        for k, block in enumerate(by_step(red_v.total())):
            src[k] = block
        got = seq_all(src, dst, half_of(m, "a2_m"))
        dst[at.s] = src[at.s]
        yield
        got.wait_recv()
        output_back = from_steps(dst)
        n.dob[1, m, at.y] = output_back.astype(bf16)
        got = y_same(n.dob.at[1, m], half_of(m, "obb_m"))
        yield
        got.wait_recv()
        g = dot(n.dob[1, m].reshape(128, DD), wcat(3), NT).astype(bf16)
        q, k, v = n.qkv[m, 0], n.qkv[m, 1], n.qkv[m, 2]
        dq = jnp.zeros((128, 256), f32)
        dk = jnp.zeros((128, 256), f32)
        dv = jnp.zeros((128, 256), f32)
        for hd in range(4):
            gh = jnp.where(masks[hd], g, jnp.zeros_like(g))
            exact = n.ex[m, hd]
            dw = dot(gh, v, NT).astype(bf16).astype(f32)
            ds = exact * (dw - jnp.sum(dw * exact, axis=1, keepdims=True)) / math.sqrt(HEAD)
            dv = jnp.where(masks[hd], dot(exact.T.astype(bf16), g), dv)
            dq = jnp.where(masks[hd], dot(ds.astype(bf16), k), dq)
            dk = jnp.where(masks[hd], dot(ds.T.astype(bf16), q), dk)
        n.tri[m, 0] = dq.astype(bf16)
        n.tri[m, 1] = dk.astype(bf16)
        n.tri[m, 2] = dv.astype(bf16)
        terms = dot(n.tri[m, 0], wcat(0)) + dot(n.tri[m, 1], wcat(1)) + dot(n.tri[m, 2], wcat(2))
        for b in range(4):
            getattr(n, f"c{m}_s")[b] = terms[32 * b : 32 * b + 32].astype(bf16)
        red_c = direct("y", f"c{m}")
        yield
        red_c.finish()
        nback = red_c.total()
        mine.gain_term = jnp.sum(nback * mine.dhat, axis=0, keepdims=True)
        hback = nback * dgain
        inner = jnp.mean(hback * mine.dhat, axis=1, keepdims=True)
        ib = output_back + mine.dscale * (hback - mine.dhat * inner)
        src, dst = half_of(m, "a3s"), half_of(m, "a3r")
        for k, block in enumerate(by_step(ib)):
            src[k] = block
        got = seq_all(src, dst, half_of(m, "a3_m"))
        dst[at.s] = src[at.s]
        yield
        got.wait_recv()
        n.ib[m, at.x, at.y] = from_steps(dst).astype(bf16)

        def part(axis, where, sems):
            return RingGather(out, at, axis, where, lambda k: where(pl.ds(0, k), None), sems)

        def spread(axis, mine_is, where, sems):
            src = where(mine_is)
            return out.spread(axis, 4, lambda to: src, src, sems, None, where(pl.ds(0, 3)))

        low, high = pl.ds(0, 16), pl.ds(16, 16)
        ib = n.ib.at[m]
        if m == 0:
            one = [spread("x", at.x, lambda i: ib.at[i, at.y], n.i0x_m)]
        else:
            one = [
                spread("x", at.x, lambda i: ib.at[i, at.y, low], n.iax_m),
                spread("y", at.y, lambda i: ib.at[at.x, i, high], n.iby_m),
            ]
        yield
        one[0].wait_recv()
        if m == 0:
            two = [part("y", lambda i, hf: ib.at[:, i, :, span(hf, DD)], n.i0y_m)]
        else:
            two = [part("y", lambda i, hf: ib.at[:, i, low, span(hf, DD)], n.iay_m)]
            one[1].wait_recv()
            two.append(part("x", lambda i, hf: ib.at[i, :, high, span(hf, DD)], n.ibx_m))
        yield
        for ring in two:
            ring.forward()
        yield
        for ring in two:
            ring.finish()
        yield

    run = [chain(0), chain(1)]

    def step(m):
        next(run[m])

    def text_piece(i):
        feats = jnp.concatenate([n.nb[i // 2, 2 * (i % 2) + b] for b in range(2)], axis=1)
        part = dot(n.tt[:, 512 * i : 512 * i + 512], feats, NT)
        if i == 0:
            n.tl[...] = part
        else:
            n.tl[...] += part

    def text_back(a):
        part = dot(n.tgr[...], n.tt[:, 1024 * a : 1024 * a + 1024])
        for b in range(4):
            n.t_s[a, b] = part[:, 256 * b : 256 * b + 256].astype(bf16)

    weights.forward()
    step(0)
    step(1)
    norm_y.forward()
    weights.finish()
    weights_z = RingGather(
        out, at, "z",
        lambda i, hf: n.wb.at[span(hf, 4), i, mine],
        lambda k: n.wb.at[:, pl.ds(0, k), mine],
        n.wz_m,
    )
    step(0)
    norm_z.forward()
    norm_y.finish()
    norm_x = RingGather(
        out, at, "x", lambda i, hf: n.nb.at[i, span(hf, 4)], lambda k: n.nb.at[pl.ds(0, k)], n.nx_m
    )
    step(1)
    weights_z.forward()
    step(0)
    n.tab[at.x] = n.au[at.s]
    tab_x = RingGather(
        out, at, "x", lambda i, hf: n.tab.at[i, span(hf, 128)], lambda k: n.tab.at[pl.ds(0, k)], n.tab_m
    )
    step(1)
    norm_z.finish()
    share = n.ns.at[:, at.c]
    wait_n = out.one(share, share, n.nc_m, at.sibling)
    weights_z.finish()
    for other in (weights.right, at.peer("x", 2)[0], weights.left):
        part = n.wb.at[other, :, mine]
        out.go(part, part, n.wc_m.at[0], n.wc_m.at[1], at.sibling)
    out.sent_later(n.wb.at[pl.ds(0, 3), :, mine], n.wc_m.at[0])
    wait_w = out.bytes_of(n.wb.at[pl.ds(0, 3), :, mine], n.wc_m.at[1])
    got_ids.wait_recv()
    i = lax.broadcasted_iota(jnp.int32, (128, 1024), 0)
    j = lax.broadcasted_iota(jnp.int32, (128, 1024), 1)
    same = ((i >> 6) == (j >> 9)) & (((i >> 2) & 15) == ((j >> 5) & 15)) & ((i & 3) == (j & 3))
    group = lax.broadcasted_iota(jnp.int32, (8, 1024), 0)
    j = lax.broadcasted_iota(jnp.int32, (8, 1024), 1)
    book = [at.s, jnp.maximum(at.s - 1, 0)]
    ids2 = [jnp.concatenate([n.idb[g, pl.ds(k, 1), :] for g in range(8)], axis=0) for k in book]
    spread = lax.dot_general(
        jnp.concatenate(ids2, axis=0).astype(f32), jnp.where(same, 1.0, 0.0), NN,
        precision=lax.Precision.HIGHEST, preferred_element_type=f32,
    )
    for i in range(2):
        own = jnp.where(((j >> 2) & 7) == group, spread[8 * i : 8 * i + 8], 0.0)
        n.idr[i] = jnp.sum(own, axis=0, keepdims=True).astype(jnp.int32)
    norm_x.forward()
    wait_w.wait_recv()
    step(0)
    step(1)
    wait_n.wait_recv()
    def transposed(b):
        rows = []
        for t in range(4):
            for s in range(8):
                index = 8 * lax.div(b, 4) + 2 * lax.rem(b, 4) + t // 2
                tile = unfold(n.ns[s // 2, s % 2, index], 2)
                rows.append(tile[4 * (t % 2) : 4 * (t % 2) + 4])
        cols = pl.ds(pl.multiple_of(128 * b, 128), 128)
        n.nt[:, cols] = jnp.concatenate(rows, axis=0).T.astype(bf16)

    loop(0, 8, transposed)
    step(0)
    tab_x.forward()
    step(1)
    norm_x.finish()
    loads[2].wait()
    text_piece(0)
    step(0)
    text_piece(1)
    step(1)

    def two_blocks(to):
        return n.nb.at[lax.div(to, 2), pl.ds(2 * lax.rem(to, 2), 2)]

    n.ndst[at.s] = two_blocks(at.s)[...]
    got_nd = out.spread("s", 8, two_blocks, n.ndst.at[at.s], n.nd_m, n.ndst)
    for m in range(2):
        row = n.idr[0, :, pl.ds(pl.multiple_of(at.x * 128 + 512 * m, 128), 128)]
        held[m].hot = jnp.where(((row >> 7) & 3) == at.y, ((row >> 9) << 7) | (row & 127), -1)
    tab_x.finish()
    text_piece(2)
    step(0)
    step(1)
    text_piece(3)
    step(0)
    text_piece(4)
    step(1)
    text_piece(5)
    step(0)
    text_piece(6)
    step(1)
    text_piece(7)
    tl = capped(n.tl[...])
    n.tl[...] = tl
    text_hot = lax.broadcasted_iota(jnp.int32, (VOCAB, 128), 0) == n.tid[...] - at.t * VOCAB
    tsum = jnp.sum(jnp.exp(tl - soft_cap), axis=0, keepdims=True)
    tchosen = jnp.sum(jnp.where(text_hot, tl, 0.0), axis=0, keepdims=True)
    n.ty[at.y] = jnp.concatenate([tsum, tchosen, jnp.zeros((6, 128), f32)], axis=0)
    got_ty = y_same(n.ty, n.ty_m)
    step(0)
    grads = jnp.concatenate([n.gr[0], n.gr[1]], axis=1)

    def vocab_grad(b):
        cols = pl.ds(pl.multiple_of(256 * b, 256), 256)
        g = dot(grads, n.ob[:, :, :, cols].reshape(256, 256))
        for a in range(4):
            n.g_s[a, :, cols] = g[128 * a : 128 * a + 128].astype(bf16)

    loop(0, 4, vocab_grad)
    red_g = reduce("x", "g", rows_half(64))
    step(1)
    got_ty.wait_recv()
    n.tx[at.x] = jnp.sum(n.ty[...], axis=0)
    got_tx = x_same(n.tx, n.tx_m)
    got_lc = seq_all(n.lc, n.lr, n.lc_m)
    n.lr[at.s] = n.lc[at.s]
    step(0)
    got_tx.wait_recv()
    ttotal = jnp.sum(n.tx[...], axis=0)
    tlse_row = soft_cap + jnp.log(ttotal[0:1, :])
    n.tlr[...] = tlse_row - ttotal[1:2, :]
    tl = n.tl[...]
    tgrad = (jnp.exp(tl - tlse_row) - jnp.where(text_hot, 1.0, 0.0)) * cap_slope(tl)
    padded = jnp.concatenate([tgrad, jnp.zeros((1024 - VOCAB, 128), f32)], axis=0)
    n.tg[at.z, at.c] = padded.astype(bf16)
    tg_z = RingGather(
        out, at, "z",
        lambda i, hf: n.tg.at[i, at.c, span(hf, 1024)],
        lambda k: n.tg.at[pl.ds(0, k), at.c],
        n.tgz_m,
    )
    n.tgr[...] = padded.T[:, 0:VOCAB].astype(bf16)
    step(1)
    red_g.forward()
    text_back(0)
    step(0)
    text_back(1)
    step(1)
    text_back(2)
    step(0)
    text_back(3)
    red_t = reduce("x", "t", rows_half(2))
    step(1)

    for c in range(4):
        n.trt[c] = n.tri[:, c].reshape(256, 256).astype(f32).T.astype(bf16)

    def weight_grad(zz):
        cols = pl.ds(pl.multiple_of(256 * zz, 256), 256)
        to = pl.ds(pl.multiple_of(128 * zz, 128), 128)
        g = dot(n.trt[0:3].reshape(768, 256), n.dob[0, :, :, :, cols].reshape(256, 256))
        last = dot(n.trt[3], n.dob[1, :, :, :, cols].reshape(256, 256))
        for core in range(2):
            for a in range(4):
                for c in range(4):
                    rows = last[64 * a : 64 * a + 64] if c == 3 else g[256 * c + 64 * a : 256 * c + 64 * a + 64]
                    n.gas[core, a, c, :, to] = rows[:, 128 * core : 128 * core + 128].astype(bf16)

    step(0)
    tg_z.forward()
    red_g.finish()
    g = red_g.total()
    for b in range(8):
        n.gts[b] = g[:, 128 * b : 128 * b + 128].astype(bf16)
    got_gt = seq_all(n.gts, n.gtr, n.gt_m)
    n.gtr[at.s] = n.gts[at.s]
    step(1)
    loop(0, 2, weight_grad)
    step(0)
    loop(2, 4, weight_grad)
    step(1)
    theirs = n.gas.at[1 - at.c]
    wait_gar = out.one(theirs, n.gar, n.gar_m, at.sibling)
    red_t.forward()
    term = held[0].gain_term + held[1].gain_term
    n.dgs[at.s] = jnp.concatenate([term[:, 128 * b : 128 * b + 128] for b in range(8)], axis=0)
    got_dgs = seq_same(n.dgs, n.dgs_m)
    got_lc.wait_recv()
    lane = lax.broadcasted_iota(jnp.int32, (16, 128), 1)
    for m in range(2):
        losses = jnp.zeros((16, 128), f32)
        for k in range(8):
            losses = jnp.where(lane == 1 + k, n.lr[k, m], losses)
        n.lx[at.x, m] = losses
    got_lx = x_same(n.lx, n.lx_m)
    tg_z.finish()
    share_t = n.tg.at[:, at.c]
    wait_t = out.one(share_t, share_t, n.tgc_m, at.sibling)
    step(0)

    def features(m):
        block = dot(n.ib[m].reshape(512, DD), n.pj[at.s], NT)
        for a in range(4):
            for s in range(8):
                lo = 128 * a + 4 * s
                rows = [block[lo + 32 * b : lo + 32 * b + 4] for b in range(4)]
                rows = jnp.concatenate(rows, axis=0).astype(bf16)
                n.sf[s % 2, s // 2, 64 * m + 16 * a : 64 * m + 16 * a + 16, :] = rows

    def hot_before(m):
        prev = jnp.where(at.s > 0, n.idr[1, :, 512 * m : 512 * m + 512] - at.t * 128, -1)
        entry = lax.broadcasted_iota(jnp.int32, (128, 512), 0)
        return jnp.where(prev == entry, 1.0, 0.0).astype(bf16)

    features(0)
    red_t.finish()
    for b in range(4):
        n.t2_s[b] = red_t.total(lambda ref: ref[b]).astype(bf16)
    red_t2 = reduce("y", "t2", rows_half(64))
    wait_gar.wait_recv()
    for a in range(4):
        n.ga_s[a] = (n.gas[at.c, a].astype(f32) + n.gar[a].astype(f32)).astype(bf16)
    red_ga = reduce("x", "ga", rows_half(2))
    left0 = jnp.concatenate([n.nt[:, 0:512], hot_before(0)], axis=0)

    def first_half(b):
        cols = pl.ds(pl.multiple_of(256 * b, 256), 256)
        g = dot(left0, n.ib[0, :, :, :, cols].reshape(512, 256))
        for i in range(3):
            n.raw[i, :, cols] = g[128 * i : 128 * i + 128]

    loop(0, 4, first_half)
    red_t2.forward()
    step(1)
    features(1)
    wait_sf = out.one(n.sf.at[1 - at.c], n.sfr, n.sfr_m, at.sibling)

    left1 = jnp.concatenate([n.nt[:, 512:1024], hot_before(1)], axis=0)

    def proj_grad(d):
        to = lax.rem(at.z + d, 4)
        cols = pl.ds(pl.multiple_of(to * 256, 256), 256)
        g = dot(left1, n.ib[1, :, :, :, cols].reshape(512, 256))
        g = g + jnp.concatenate([n.raw[i, :, cols] for i in range(3)], axis=0)
        g = jnp.concatenate([g[0:256], g[256:384] * embed_scale], axis=0)
        n.gas_all[2 * to, 0:384, :] = g[:, 0:128].astype(bf16)
        n.gas_all[2 * to + 1, 0:384, :] = g[:, 128:256].astype(bf16)

    def send_proj(d):
        proj_grad(d)
        to = lax.rem(at.z + d, 4)
        for core in range(2):
            src = n.gas_all.at[2 * to + core]
            out.go(src, n.gar_all.at[at.s], n.gall_m.at[0], n.gall_m.at[1], (to, core, at.x, at.y))

    (right, to_right), (far, _), (left, to_left) = [at.peer("z", d) for d in (1, 2, 3)]
    low, high = pl.ds(0, 192), pl.ds(192, 192)
    proj_grad(2)
    for core in range(2):
        src = n.gas_all.at[2 * far + core]
        out.go(src.at[low], n.rel.at[0, core], n.rel_m.at[0], n.rel_m.at[1], to_right)
        out.go(src.at[high], n.rel.at[1, core], n.rel_m.at[0], n.rel_m.at[2], to_left)
    wait_sf.wait_recv()
    for b in range(4):
        n.f_s[b] = (n.sf[at.c, b].astype(f32) + n.sfr[b].astype(f32)).astype(bf16)
    red_f = direct("z", "f")
    red_t2.finish()
    send_proj(1)
    send_proj(3)
    out.bytes_of(n.rel.at[0], n.rel_m.at[1]).wait_recv()
    out.bytes_of(n.rel.at[1], n.rel_m.at[2]).wait_recv()
    for core in range(2):
        there = n.gar_all.at[2 * left + at.c, low]
        out.go(n.rel.at[0, core], there, n.gall_m.at[0], n.gall_m.at[1], (right, core, at.x, at.y))
        there = n.gar_all.at[2 * right + at.c, high]
        out.go(n.rel.at[1, core], there, n.gall_m.at[0], n.gall_m.at[1], (left, core, at.x, at.y))
    out.sent_later(n.rel, n.rel_m.at[0])
    proj_grad(0)
    n.gar_all[at.s] = n.gas_all[at.s]
    theirs = 2 * at.z + 1 - at.c
    out.go(n.gas_all.at[theirs], n.gar_all.at[at.s], n.gall_m.at[0], n.gall_m.at[1], at.sibling)
    out.sent_later(n.gas_all.at[pl.ds(0, 7)], n.gall_m.at[0])
    got_all = out.bytes_of(n.gar_all.at[pl.ds(0, 7)], n.gall_m.at[1])
    red_f.finish()
    fb = red_t2.total() + red_f.total()
    gback = fb * gain
    inner = jnp.sum(gback * hat, axis=1, keepdims=True)
    n.rd[at.t] = jnp.broadcast_to(inner, (128, 128)).T[0:8, :]
    got_rd = plane_same(n.rd, n.rd_m)
    n.tgn[at.s] = jnp.broadcast_to(jnp.sum(fb * hat, axis=0, keepdims=True), (8, 256))
    got_tgn = seq_same(n.tgn, n.tgn_m)
    red_ga.forward()
    got_dgs.wait_recv()
    n.dgy[at.y] = jnp.sum(n.dgs[...], axis=0)
    got_dgy = y_same(n.dgy, n.dgy_m)

    wait_t.wait_recv()
    got_nd.wait_recv()

    def table_grad(a):
        part = pl.ds(pl.multiple_of(512 * a, 512), 512)
        left = jnp.concatenate([n.tg[g // 2, g % 2, part, :] for g in range(8)], axis=1)
        for b in range(2):
            right = n.ndst[:, b].reshape(1024, 256)
            n.o_gtt[part, 256 * b : 256 * b + 256] = dot(left, right).astype(bf16)

    loop(0, 2, table_grad)
    got_dgy.wait_recv()
    n.dgx[at.x] = jnp.sum(n.dgy[...], axis=0)
    got_dgx = x_same(n.dgx, n.dgx_m)
    red_ga.finish()
    for b in range(4):
        n.gz_s[b] = red_ga.total(lambda ref: ref[:, :, 128 * b : 128 * b + 128]).astype(bf16)
    red_gz = direct("z", "gz")
    got_rd.wait_recv()
    dots = twice(row_to_col(jnp.sum(n.rd[...], axis=0)[0:1, :], 128))
    n.o_gh[...] = scale * (gback - hat * (dots / D))
    got_tgn.wait_recv()
    n.o_tgain[...] = jnp.sum(n.tgn[...], axis=0)[0:1, :]
    got_lx.wait_recv()
    losses = jnp.concatenate([n.lx[a, m] for m in range(2) for a in range(4)], axis=0).T
    n.o_loss[...] = jnp.concatenate([n.tlr[...], losses[1:9]], axis=0)
    got_dgx.wait_recv()
    n.o_dg[...] = jnp.sum(n.dgx[...], axis=0)
    got_gt.wait_recv()
    got_all.wait_recv()
    n.o_gp[...] = n.gar_all[:, 0:256, :]
    for k in range(8):
        g = n.gtr[k].astype(f32)
        if k < 7:
            g = g + n.gar_all[k + 1, 256:384, :].astype(f32)
        n.o_gtab[k] = g
    red_gz.finish()
    ga = red_gz.total()
    n.o_gqkv[...] = ga[0:3]
    n.o_gout[...] = ga[3]
    out.finish()


def write_kernel(*refs):
    count = len(refs) // 2
    for src, dst in zip(refs[:count], refs[count:]):
        dst[...] = src[...].astype(f32)


def write_outputs(results):
    shapes = [r.shape for r in results]
    shapes[3] = (VOCAB, 512)
    blocks = {1: (64, 256), 3: (512, 512), 4: (4, 256, 128), 5: (4, 128, 128)}

    def spec(i):
        block = blocks.get(i, shapes[i])
        moves = i in blocks
        return pl.BlockSpec(block, lambda g: (g if moves else 0,) + (0,) * (len(block) - 1))

    return pl.pallas_call(
        write_kernel,
        out_shape=[jax.ShapeDtypeStruct(shape, f32) for shape in shapes],
        grid=(2,),
        in_specs=[spec(i) for i in range(9)],
        out_specs=[spec(i) for i in range(9)],
        name="write",
    )(*results)


def on_device(
    hidden, text_gain, text_table, proj, audio_table, depth_gain, attn_qkv, attn_out, text_ids, audio_ids
):
    vmem = pl.BlockSpec(memory_space=pltpu.VMEM)
    hbm = pl.BlockSpec(memory_space=pl.ANY)
    outs = [
        ((9, 128), f32), ((128, 256), f32), ((1, 256), f32), ((1024, 512), bf16), ((8, 256, 128), bf16),
        ((8, 128, 128), f32), ((8, 128), f32), ((3, 64, 128), f32), ((64, 128), f32),
    ]
    results = pl.pallas_call(
        kernel,
        out_shape=[jax.ShapeDtypeStruct(shape, dtype) for shape, dtype in outs],
        in_specs=[vmem, vmem, hbm, hbm, hbm, vmem, vmem, vmem, vmem, vmem],
        out_specs=[vmem] * len(outs),
        scratch_shapes=[scratch_shape(entry) for entry in SCRATCH],
        name="head",
        compiler_params=pltpu.CompilerParams(
            collective_id=1, has_side_effects=True, vmem_limit_bytes=VMEM_LIMIT
        ),
    )(
        hidden, text_gain, text_table, proj, audio_table, depth_gain,
        jnp.transpose(attn_qkv, (1, 2, 0)), attn_out, text_ids[None, :], audio_ids.T,
    )
    losses, gh, tgain, gtt, gp, gtab, dg, gqkv, gout = write_outputs(results)
    return losses.T, gh, tgain[0], gtt.T, gp, gtab, dg.reshape(DD), jnp.transpose(gqkv, (2, 0, 1)), gout


def solution(mesh):
    fine = Mesh(mesh.devices.reshape(4, 2, 4, 4), ("z", "core", "x", "y"))
    seq = ("z", "core")
    tp = ("x", "y")
    in_specs = (
        P(seq, tp), P(tp), P(tp, None), P(None, tp, None), P(None, tp, None),
        P(), P(None, None, tp), P(tp, None), P(seq), P(seq, None),
    )
    out_specs = (
        P(seq, None), P(seq, tp), P(tp), P(seq, tp), P(None, tp, seq),
        P(None, tp, seq), P(), P(seq, None, tp), P(tp, seq),
    )
    return jax.shard_map(
        on_device, mesh=fine, in_specs=in_specs, out_specs=out_specs, check_vma=False
    )
```

```python
import math

import jax
import jax.numpy as jnp
from jax import lax
from jax.experimental import pallas as pl
from jax.experimental.pallas import tpu as pltpu
from jax.sharding import Mesh
from jax.sharding import PartitionSpec as P

D = 4096
DD = 1024
HEAD = 64
VOCAB = 1000
MESH = pl.DeviceIdType.MESH
VMEM_LIMIT = 62 * 1024 * 1024

soft_cap = 12.0
epsilon = 1e-05
embed_scale = math.sqrt(DD) / 4.0
f32 = jnp.float32
bf16 = jnp.bfloat16

NN = (((1,), (0,)), ((), ()))
NT = (((1,), (1,)), ((), ()))
TN = (((0,), (0,)), ((), ()))


def dot(a, b, dims=NN):
    return lax.dot_general(a, b, dims, preferred_element_type=f32)


def capped(values):
    return soft_cap * jnp.tanh(values / soft_cap)


def cap_slope(capped_values):
    ratio = capped_values / soft_cap
    return 1.0 - ratio * ratio


class Place:
    def __init__(self):
        self.z = lax.axis_index("z")
        self.c = lax.axis_index("core")
        self.x = lax.axis_index("x")
        self.y = lax.axis_index("y")
        self.s = self.z * 2 + self.c
        self.t = self.x * 4 + self.y
        z, c, x, y = self.z, self.c, self.x, self.y
        self.sibling = (z, 1 - c, x, y)
        self.known = {}
        for d in range(1, 4):
            to = lax.rem(x + d, 4)
            self.known["x", d] = (to, (z, c, to, y))
            to = lax.rem(y + d, 4)
            self.known["y", d] = (to, (z, c, x, to))
            to = lax.rem(z + d, 4)
            self.known["z", d] = (to, (to, c, x, y))
        for d in range(1, 8):
            to = lax.rem(self.s + d, 8)
            self.known["s", d] = (to, (lax.div(to, 2), lax.rem(to, 2), x, y))
        for d in range(1, 16):
            to = lax.rem(self.t + d, 16)
            self.known["t", d] = (to, (z, c, lax.div(to, 4), lax.rem(to, 4)))

    def peer(self, axis, d):
        return self.known[axis, d]

    def index(self, axis):
        return {"x": self.x, "y": self.y, "z": self.z, "s": self.s, "t": self.t}[axis]


class Sends:
    def __init__(self, at):
        self.at = at
        self.pending = []

    def go(self, src, dst, send, recv, device):
        pltpu.make_async_remote_copy(
            src_ref=src, dst_ref=dst, send_sem=send, recv_sem=recv, device_id=device, device_id_type=MESH
        ).start()

    def bytes_of(self, ref, sem):
        return pltpu.make_async_remote_copy(
            src_ref=ref, dst_ref=ref, send_sem=sem, recv_sem=sem,
            device_id=self.at.sibling, device_id_type=MESH,
        )

    def sent_later(self, ref, sem):
        self.pending.append(self.bytes_of(ref, sem))

    def one(self, src, dst, sems, device):
        self.go(src, dst, sems.at[0], sems.at[1], device)
        self.sent_later(src, sems.at[0])
        return self.bytes_of(dst, sems.at[1])

    def spread(self, axis, n, src, dst, sems, slots, all_bytes=None):
        order = {4: (2, 1, 3), 8: (4, 3, 5, 2, 6, 1, 7)}.get(n, range(1, n))
        for d in order:
            to, device = self.at.peer(axis, d)
            self.go(src(to), dst, sems.at[0], sems.at[1], device)
        if all_bytes is None:
            all_bytes = slots.at[pl.ds(0, n - 1)]
        self.sent_later(all_bytes, sems.at[0])
        return self.bytes_of(all_bytes, sems.at[1])

    def finish(self):
        for wait in self.pending:
            wait.wait_send()


class RingGather:
    def __init__(self, out, at, axis, part, slots, sems):
        self.out, self.part, self.sems, self.slots = out, part, sems, slots
        self.right, self.to_right = at.peer(axis, 1)
        self.left, self.to_left = at.peer(axis, 3)
        block = part(at.index(axis), None)
        out.go(block, block, sems.at[0], sems.at[1], self.to_right)
        out.go(block, block, sems.at[0], sems.at[2], self.to_left)
        out.sent_later(slots(3), sems.at[0])

    def forward(self):
        out, part, sems = self.out, self.part, self.sems
        out.bytes_of(part(self.left, None), sems.at[1]).wait_recv()
        one = part(self.left, 0)
        out.go(one, one, sems.at[0], sems.at[3], self.to_right)
        out.bytes_of(part(self.right, None), sems.at[2]).wait_recv()
        two = part(self.right, 1)
        out.go(two, two, sems.at[0], sems.at[3], self.to_left)

    def finish(self):
        self.out.bytes_of(self.slots(1), self.sems.at[3]).wait_recv()


class RingReduce:
    def __init__(self, out, at, axis, blocks, half, bufs, sems):
        self.out, self.half, self.sems, self.blocks = out, half, sems, blocks
        self.me, far = at.index(axis), at.peer(axis, 2)[0]
        self.right, self.to_right = at.peer(axis, 1)
        self.left, self.to_left = at.peer(axis, 3)
        self.rl, self.rr, self.fa, self.fb = bufs
        s = blocks
        out.go(half(s.at[far], 0), self.fa, sems.at[0], sems.at[1], self.to_right)
        out.go(half(s.at[far], 1), self.fb, sems.at[0], sems.at[2], self.to_left)
        out.go(half(s.at[self.right], 1), half(self.rl, 1), sems.at[0], sems.at[3], self.to_right)
        out.go(half(s.at[self.left], 0), half(self.rr, 0), sems.at[0], sems.at[3], self.to_left)
        out.sent_later(s.at[pl.ds(0, 3)], sems.at[0])

    def forward(self):
        s, half, out, sems = self.blocks, self.half, self.out, self.sems
        out.bytes_of(self.fa, sems.at[1]).wait_recv()
        one = half(s.at[self.right], 0)
        one[...] = (one[...].astype(f32) + self.fa[...].astype(f32)).astype(bf16)
        out.go(one, half(self.rl, 0), sems.at[0], sems.at[3], self.to_right)
        out.bytes_of(self.fb, sems.at[2]).wait_recv()
        two = half(s.at[self.left], 1)
        two[...] = (two[...].astype(f32) + self.fb[...].astype(f32)).astype(bf16)
        out.go(two, half(self.rr, 1), sems.at[0], sems.at[3], self.to_left)

    def finish(self):
        self.out.bytes_of(self.blocks.at[pl.ds(0, 2)], self.sems.at[3]).wait_recv()

    def total(self, pick=lambda ref: ref[...]):
        own = pick(self.blocks.at[self.me]).astype(f32)
        return own + pick(self.rl).astype(f32) + pick(self.rr).astype(f32)


class DirectReduce:
    def __init__(self, out, at, axis, blocks, got, sems):
        self.blocks, self.got = blocks, got
        self.me = at.index(axis)
        for d in (2, 1, 3):
            to, device = at.peer(axis, d)
            out.go(blocks.at[to], got.at[d - 1], sems.at[0], sems.at[1], device)
        out.sent_later(blocks.at[pl.ds(0, 3)], sems.at[0])
        self.wait = out.bytes_of(got, sems.at[1])

    def finish(self):
        self.wait.wait_recv()

    def total(self, pick=lambda ref: ref[...]):
        own = pick(self.blocks.at[self.me]).astype(f32)
        for d in range(3):
            own = own + pick(self.got.at[d]).astype(f32)
        return own


def span(h, size):
    if h is None:
        return pl.ds(0, size)
    return pl.ds(h * (size // 2), size // 2)


def rows_half(n):
    return lambda ref, h: ref.at[pl.ds(h * n, n)]


def row_to_col(row, lanes):
    return jnp.broadcast_to(row, (lanes, row.shape[1])).T


def twice(col):
    return jnp.concatenate([col, col], axis=1)


def fold(rows, n):
    w = rows.shape[1] // n
    return jnp.concatenate([rows[:, i * w : i * w + w] for i in range(n)], axis=0).astype(bf16)


def unfold(packed, n):
    r = packed.shape[0] // n
    wide = packed.astype(f32)
    return jnp.concatenate([wide[i * r : i * r + r] for i in range(n)], axis=1)


def by_step(rows):
    return [fold(rows[4 * k : 4 * k + 4], 4) for k in range(8)]


def from_steps(ref):
    return jnp.concatenate([unfold(ref[k], 4) for k in range(8)], axis=0)


def head_masks(rows):
    lane = lax.broadcasted_iota(jnp.int32, (rows, 256), 1)
    return [(lane >= 64 * h) & (lane < 64 * h + 64) for h in range(4)]


def step_mask():
    i = lax.broadcasted_iota(jnp.int32, (128, 128), 0)
    j = lax.broadcasted_iota(jnp.int32, (128, 128), 1)
    return ((i & 3) == (j & 3)) & ((i >> 5) == (j >> 5)) & (j <= i)


def attention(qh, kk, allowed):
    scores = dot(qh, kk, NT) / math.sqrt(HEAD)
    raised = jnp.where(allowed, jnp.exp(scores), 0.0)
    return raised / jnp.sum(raised, axis=1, keepdims=True)


def ring_reduce_scratch(name, block, half):
    return [
        (name + "_s", (4,) + block, bf16),
        (name + "_rl", block, bf16),
        (name + "_rr", block, bf16),
        (name + "_fa", half, bf16),
        (name + "_fb", half, bf16),
        (name + "_m", 4, None),
    ]


def direct_scratch(name, block):
    return [(name + "_s", (4,) + block, bf16), (name + "_r", (3,) + block, bf16), (name + "_m", 2, None)]


def chain_scratch(m):
    m = str(m)
    return [
        *ring_reduce_scratch("p" + m, (4, 16, DD), (2, 16, DD)),
        *ring_reduce_scratch("q" + m, (4, 16, DD), (2, 16, DD)),
        *direct_scratch("pp" + m, (16, DD)),
        *direct_scratch("qq" + m, (16, DD)),
        ("dn_m" + m, 2, None),
        *direct_scratch("h" + m, (32, DD)),
        ("a1s" + m, (8, 16, 256), bf16), ("a1r" + m, (8, 16, 256), bf16), ("a1_m" + m, 2, None),
        ("a2s" + m, (8, 16, 256), bf16), ("a2r" + m, (8, 16, 256), bf16), ("a2_m" + m, 2, None),
        ("a3s" + m, (8, 16, 256), bf16), ("a3r" + m, (8, 16, 256), bf16), ("a3_m" + m, 2, None),
        ("ob_m" + m, 2, None), ("e" + m, (4, 8, 128), f32), ("e_m" + m, 2, None),
        *direct_scratch("v" + m, (32, DD)),
        *direct_scratch("c" + m, (32, DD)),
        ("obb_m" + m, 2, None),
    ]


SCRATCH = [
    ("tt", (VOCAB, D), bf16), ("pj", (8, 256, DD), bf16), ("au", (8, 128, DD), bf16), ("load", 3, 0),
    ("ssq", (16, 8, 128), f32), ("ssq_m", 2, None),
    ("idb", (8, 8, 128), jnp.int32), ("idb_m", 2, None), ("idr", (2, 1, 1024), jnp.int32),
    ("raw", (8, 128, DD), f32), ("look", (8, 128, DD), bf16),
    ("wb", (4, 4, 64, DD), bf16), ("wb_m", 4, None), ("wz_m", 4, None), ("wc_m", 2, None),
    ("nb", (4, 4, 128, 256), bf16), ("ny_m", 4, None), ("nx_m", 4, None),
    ("ns", (4, 2, 16, 16, 128), bf16), ("nz_m", 4, None), ("nc_m", 2, None),
    *chain_scratch(0), *chain_scratch(1),
    ("dob", (2, 2, 4, 32, DD), bf16), ("qkv", (2, 3, 128, 256), bf16),
    ("ex", (2, 4, 128, 128), f32), ("ob", (2, 4, 32, DD), bf16),
    ("gr", (2, 512, 128), bf16), ("tri", (2, 4, 128, 256), bf16), ("trt", (4, 256, 256), bf16),
    ("tab", (4, 128, DD), bf16), ("tab_m", 4, None),
    ("tl", (VOCAB, 128), f32), ("ty", (4, 8, 128), f32), ("ty_m", 2, None), ("tx", (4, 8, 128), f32), ("tx_m", 2, None),
    ("tgr", (128, VOCAB), bf16), ("tlr", (1, 128), f32),
    *ring_reduce_scratch("g", (128, DD), (64, DD)),
    ("lc", (8, 2, 16, 128), f32), ("lr", (8, 2, 16, 128), f32), ("lc_m", 2, None),
    ("lx", (4, 2, 16, 128), f32), ("lx_m", 2, None),
    ("nt", (256, 1024), bf16), ("tg", (4, 2, 1024, 128), bf16), ("tgz_m", 4, None), ("tgc_m", 2, None),
    *ring_reduce_scratch("t", (4, 128, 256), (2, 128, 256)),
    *ring_reduce_scratch("t2", (128, 256), (64, 256)),
    ("ndst", (8, 2, 128, 256), bf16), ("nd_m", 2, None),
    ("ib", (2, 4, 4, 32, DD), bf16), ("i0x_m", 2, None), ("i0y_m", 4, None),
    ("iax_m", 2, None), ("iay_m", 4, None), ("ibx_m", 4, None), ("iby_m", 2, None),
    ("gas", (2, 4, 4, 64, 512), bf16), ("gar", (4, 4, 64, 512), bf16), ("gar_m", 2, None),
    *ring_reduce_scratch("ga", (4, 64, 512), (2, 64, 512)),
    *direct_scratch("gz", (4, 64, 128)),
    ("sf", (2, 4, 128, 256), bf16), ("sfr", (4, 128, 256), bf16), ("sfr_m", 2, None),
    *direct_scratch("f", (128, 256)),
    ("gas_all", (8, 384, 128), bf16), ("gar_all", (8, 384, 128), bf16), ("gall_m", 2, None),
    ("rel", (2, 2, 192, 128), bf16), ("rel_m", 3, None),
    ("gts", (8, 128, 128), bf16), ("gtr", (8, 128, 128), bf16), ("gt_m", 2, None),
    ("dgs", (8, 8, 128), f32), ("dgs_m", 2, None), ("dgy", (4, 8, 128), f32), ("dgy_m", 2, None),
    ("dgx", (4, 8, 128), f32), ("dgx_m", 2, None),
    ("rd", (16, 8, 128), f32), ("rd_m", 2, None), ("tgn", (8, 8, 256), f32), ("tgn_m", 2, None),
]


def scratch_shape(entry):
    name, shape, dtype = entry
    if dtype is None or isinstance(dtype, int):
        return pltpu.SemaphoreType.DMA((shape,))
    return pltpu.VMEM(shape, dtype)


class Named:
    pass


def loop(low, high, body):
    def one(i, carry):
        body(i)
        return carry

    lax.fori_loop(low, high, one, 0)


INPUTS = ["hid", "gain", "table", "proj", "audio", "dgain", "wqkv", "wout", "tid", "ids"]
OUTPUTS = ["o_loss", "o_gh", "o_tgain", "o_gtt", "o_gp", "o_gtab", "o_dg", "o_gqkv", "o_gout"]


def kernel(*refs):
    n = Named()
    names = INPUTS + OUTPUTS + [entry[0] for entry in SCRATCH]
    for name, ref in zip(names, refs):
        setattr(n, name, ref)
    at = Place()
    out = Sends(at)

    def reduce(axis, name, half):
        bufs = [getattr(n, name + suffix) for suffix in ("_rl", "_rr", "_fa", "_fb")]
        return RingReduce(out, at, axis, getattr(n, name + "_s"), half, bufs, getattr(n, name + "_m"))

    def direct(axis, name):
        return DirectReduce(
            out, at, axis, getattr(n, name + "_s"), getattr(n, name + "_r"), getattr(n, name + "_m")
        )

    def seq_all(src, dst, sems):
        return out.spread("s", 8, lambda to: src.at[to], dst.at[at.s], sems, dst)

    def seq_same(ref, sems):
        return out.spread("s", 8, lambda to: ref.at[at.s], ref.at[at.s], sems, ref)

    def plane_same(ref, sems):
        return out.spread("t", 16, lambda to: ref.at[at.t], ref.at[at.t], sems, ref)

    def x_same(ref, sems):
        return out.spread("x", 4, lambda to: ref.at[at.x], ref.at[at.x], sems, ref)

    def y_same(ref, sems):
        return out.spread("y", 4, lambda to: ref.at[at.y], ref.at[at.y], sems, ref)

    loads = [
        pltpu.make_async_copy(src, dst, n.load.at[i])
        for i, (src, dst) in enumerate([(n.proj, n.pj), (n.audio, n.au), (n.table, n.tt)])
    ]
    for copy in loads:
        copy.start()
    for c in range(3):
        n.wb[at.x, c] = n.wqkv[c]
    n.wb[at.x, 3] = n.wout[...]
    barrier = pltpu.get_barrier_semaphore()
    for axis, count in (("t", 16), ("s", 8)):
        for d in range(1, count):
            device = at.peer(axis, d)[1]
            pl.semaphore_signal(barrier, inc=1, device_id=device, device_id_type=MESH)
    h = n.hid[...].astype(f32)
    gain = n.gain[...].astype(f32)[None, :]
    dgain = n.dgain[...].astype(f32)[None, :]
    ones = jnp.ones((8, 256), f32)
    n.ssq[at.t] = lax.dot_general(
        ones, h * h, NT, precision=lax.Precision.HIGHEST, preferred_element_type=f32
    )
    n.idb[at.s] = n.ids[...]
    unscaled = (h * gain).astype(bf16)
    pl.semaphore_wait(barrier, 22)

    got_ssq = plane_same(n.ssq, n.ssq_m)
    mine = pl.ds(pl.multiple_of(at.c * 32, 32), 32)
    weights = RingGather(
        out, at, "x",
        lambda i, hf: n.wb.at[i, at.z, mine] if hf is None
        else n.wb.at[i, at.z, pl.ds(pl.multiple_of(at.c * 32 + 16 * hf, 16), 16)],
        lambda k: n.wb.at[pl.ds(0, k), at.z, mine],
        n.wb_m,
    )
    got_ids = seq_same(n.idb, n.idb_m)
    loads[0].wait()

    def raw_step(k):
        n.raw[k] = dot(unscaled, n.pj[k])

    loop(0, 8, raw_step)
    loads[1].wait()
    entry = (lax.broadcasted_iota(jnp.int32, (128, 128), 1) + at.t * 128).astype(f32)
    n.look[0] = jnp.zeros((128, DD), bf16)

    def look_step(k):
        column = row_to_col(n.ids[pl.ds(k, 1), :].astype(f32), 128)
        hot = jnp.where(column == entry, 1.0, 0.0).astype(bf16)
        n.look[k + 1] = (dot(hot, n.au[k]) * embed_scale).astype(bf16)

    loop(0, 7, look_step)
    got_ssq.wait_recv()
    scale = row_to_col(lax.rsqrt(jnp.sum(n.ssq[...], axis=0)[0:1, :] / D + epsilon), 128)
    column = scale[:, 0:1]
    scale = twice(scale)
    hat = h * scale

    first = []
    for m in range(2):
        ps, qs = getattr(n, f"p{m}_s"), getattr(n, f"q{m}_s")
        part = slice(64 * m, 64 * m + 64)

        def scaled(k):
            return n.raw[k, part, :] * column[part] + n.look[k, part, :].astype(f32)

        def to_x(k):
            p = scaled(k)
            for b in range(4):
                ps[b, k] = p[16 * b : 16 * b + 16].astype(bf16)

        def to_y(k):
            p = scaled(k + 4)
            for b in range(4):
                rows = [p[16 * a + 4 * b : 16 * a + 4 * b + 4] for a in range(4)]
                qs[b, k] = jnp.concatenate(rows, axis=0).astype(bf16)

        loop(0, 4, to_x)
        red_p = reduce("x", f"p{m}", rows_half(2))
        loop(0, 4, to_y)
        first.append((red_p, reduce("y", f"q{m}", rows_half(2))))
    normed_f = hat * gain
    n.nb[at.x, at.y] = normed_f.astype(bf16)
    for b in range(16):
        n.ns[at.z, at.c, b] = fold(normed_f[8 * b : 8 * b + 8], 2)
    norm_z = RingGather(
        out, at, "z",
        lambda i, hf: n.ns.at[i, at.c, span(hf, 16)],
        lambda k: n.ns.at[pl.ds(0, k), at.c],
        n.nz_m,
    )
    norm_y = RingGather(
        out, at, "y",
        lambda i, hf: n.nb.at[at.x, i, span(hf, 128)],
        lambda k: n.nb.at[at.x, pl.ds(0, k)],
        n.ny_m,
    )

    masks = head_masks(128)
    allowed = step_mask()
    held = [Named(), Named()]

    def wcat(c):
        return jnp.concatenate([n.wb[a, c] for a in range(4)], axis=0)

    def half_of(m, name):
        return getattr(n, name + str(m))

    def chain(m):
        mine = held[m]
        red_p, red_q = first[m]
        red_p.forward()
        red_q.forward()
        yield
        for red, to, axis in ((red_p, "pp", "y"), (red_q, "qq", "x")):
            red.finish()
            total = [red.total(lambda ref: ref[k]) for k in range(4)]
            for b in range(4):
                rows = [total[k][4 * b : 4 * b + 4] for k in range(4)]
                getattr(n, f"{to}{m}_s")[b] = jnp.concatenate(rows, axis=0).astype(bf16)
            if axis == "y":
                red_pp = direct("y", f"pp{m}")
            else:
                red_qq = direct("x", f"qq{m}")
        yield
        red_pp.finish()
        red_qq.finish()
        di = jnp.concatenate([red_pp.total(), red_qq.total()], axis=0)
        mine.dscale = lax.rsqrt(jnp.mean(di * di, axis=1, keepdims=True) + epsilon)
        mine.dhat = di * mine.dscale
        n.dob[0, m, at.y] = (mine.dhat * dgain).astype(bf16)
        got = y_same(n.dob.at[0, m], half_of(m, "dn_m"))
        yield
        got.wait_recv()
        dnv = n.dob[0, m].reshape(128, DD)
        for c in range(3):
            n.qkv[m, c] = dot(dnv, wcat(c), NT).astype(bf16)
        q, k, v = n.qkv[m, 0], n.qkv[m, 1], n.qkv[m, 2]
        mixed = jnp.zeros((128, 256), f32)
        for hd in range(4):
            qh = jnp.where(masks[hd], q, jnp.zeros_like(q))
            exact = attention(qh, k, allowed)
            n.ex[m, hd] = exact
            mixed = jnp.where(masks[hd], dot(exact.astype(bf16), v), mixed)
        n.tri[m, 3] = mixed.astype(bf16)
        terms = dot(n.tri[m, 3], wcat(3))
        for b in range(4):
            getattr(n, f"h{m}_s")[b] = terms[32 * b : 32 * b + 32].astype(bf16)
        red_h = direct("y", f"h{m}")
        yield
        red_h.finish()
        src, dst = half_of(m, "a1s"), half_of(m, "a1r")
        for k, block in enumerate(by_step(di + red_h.total())):
            src[k] = block
        got = seq_all(src, dst, half_of(m, "a1_m"))
        dst[at.s] = src[at.s]
        yield
        got.wait_recv()
        n.ob[m, at.y] = from_steps(dst).astype(bf16)
        got = y_same(n.ob.at[m], half_of(m, "ob_m"))
        yield
        got.wait_recv()
        rows = n.ob[m].reshape(128, DD)
        tab = n.tab[...].reshape(512, DD)
        logits = capped(dot(tab, rows, NT))
        hot = mine.hot == lax.broadcasted_iota(jnp.int32, (512, 128), 0)
        sums = jnp.sum(jnp.exp(logits - soft_cap), axis=0, keepdims=True)
        chosen = jnp.sum(jnp.where(hot, logits, 0.0), axis=0, keepdims=True)
        e = half_of(m, "e")
        e[at.y] = jnp.concatenate([sums, chosen, jnp.zeros((6, 128), f32)], axis=0)
        got = y_same(e, half_of(m, "e_m"))
        yield
        got.wait_recv()
        total = jnp.sum(e[...], axis=0)
        lse_row = soft_cap + jnp.log(total[0:1, :])
        grad = (jnp.exp(logits - lse_row) - jnp.where(hot, 1.0, 0.0)) * cap_slope(logits)
        n.gr[m] = grad.astype(bf16)
        terms = dot(grad.T.astype(bf16), tab)
        for b in range(4):
            getattr(n, f"v{m}_s")[b] = terms[32 * b : 32 * b + 32].astype(bf16)
        red_v = direct("y", f"v{m}")
        loss = row_to_col(lse_row - total[1:2, :], 128)
        for g in range(8):
            rows = [loss[32 * b + 4 * g : 32 * b + 4 * g + 4] for b in range(4)]
            n.lc[g, m] = jnp.concatenate(rows, axis=0)
        yield
        red_v.finish()
        src, dst = half_of(m, "a2s"), half_of(m, "a2r")
        for k, block in enumerate(by_step(red_v.total())):
            src[k] = block
        got = seq_all(src, dst, half_of(m, "a2_m"))
        dst[at.s] = src[at.s]
        yield
        got.wait_recv()
        output_back = from_steps(dst)
        n.dob[1, m, at.y] = output_back.astype(bf16)
        got = y_same(n.dob.at[1, m], half_of(m, "obb_m"))
        yield
        got.wait_recv()
        g = dot(n.dob[1, m].reshape(128, DD), wcat(3), NT).astype(bf16)
        q, k, v = n.qkv[m, 0], n.qkv[m, 1], n.qkv[m, 2]
        dq = jnp.zeros((128, 256), f32)
        dk = jnp.zeros((128, 256), f32)
        dv = jnp.zeros((128, 256), f32)
        for hd in range(4):
            gh = jnp.where(masks[hd], g, jnp.zeros_like(g))
            exact = n.ex[m, hd]
            dw = dot(gh, v, NT).astype(bf16).astype(f32)
            ds = exact * (dw - jnp.sum(dw * exact, axis=1, keepdims=True)) / math.sqrt(HEAD)
            dv = jnp.where(masks[hd], dot(exact.T.astype(bf16), g), dv)
            dq = jnp.where(masks[hd], dot(ds.astype(bf16), k), dq)
            dk = jnp.where(masks[hd], dot(ds.T.astype(bf16), q), dk)
        n.tri[m, 0] = dq.astype(bf16)
        n.tri[m, 1] = dk.astype(bf16)
        n.tri[m, 2] = dv.astype(bf16)
        terms = dot(n.tri[m, 0], wcat(0)) + dot(n.tri[m, 1], wcat(1)) + dot(n.tri[m, 2], wcat(2))
        for b in range(4):
            getattr(n, f"c{m}_s")[b] = terms[32 * b : 32 * b + 32].astype(bf16)
        red_c = direct("y", f"c{m}")
        yield
        red_c.finish()
        nback = red_c.total()
        mine.gain_term = jnp.sum(nback * mine.dhat, axis=0, keepdims=True)
        hback = nback * dgain
        inner = jnp.mean(hback * mine.dhat, axis=1, keepdims=True)
        ib = output_back + mine.dscale * (hback - mine.dhat * inner)
        src, dst = half_of(m, "a3s"), half_of(m, "a3r")
        for k, block in enumerate(by_step(ib)):
            src[k] = block
        got = seq_all(src, dst, half_of(m, "a3_m"))
        dst[at.s] = src[at.s]
        yield
        got.wait_recv()
        n.ib[m, at.x, at.y] = from_steps(dst).astype(bf16)

        def part(axis, where, sems):
            return RingGather(out, at, axis, where, lambda k: where(pl.ds(0, k), None), sems)

        def spread(axis, mine_is, where, sems):
            src = where(mine_is)
            return out.spread(axis, 4, lambda to: src, src, sems, None, where(pl.ds(0, 3)))

        low, high = pl.ds(0, 16), pl.ds(16, 16)
        ib = n.ib.at[m]
        if m == 0:
            one = [spread("x", at.x, lambda i: ib.at[i, at.y], n.i0x_m)]
        else:
            one = [
                spread("x", at.x, lambda i: ib.at[i, at.y, low], n.iax_m),
                spread("y", at.y, lambda i: ib.at[at.x, i, high], n.iby_m),
            ]
        yield
        one[0].wait_recv()
        if m == 0:
            two = [part("y", lambda i, hf: ib.at[:, i, :, span(hf, DD)], n.i0y_m)]
        else:
            two = [part("y", lambda i, hf: ib.at[:, i, low, span(hf, DD)], n.iay_m)]
            one[1].wait_recv()
            two.append(part("x", lambda i, hf: ib.at[i, :, high, span(hf, DD)], n.ibx_m))
        yield
        for ring in two:
            ring.forward()
        yield
        for ring in two:
            ring.finish()
        yield

    run = [chain(0), chain(1)]

    def step(m):
        next(run[m])

    def text_piece(i):
        feats = jnp.concatenate([n.nb[i // 2, 2 * (i % 2) + b] for b in range(2)], axis=1)
        part = dot(n.tt[:, 512 * i : 512 * i + 512], feats, NT)
        if i == 0:
            n.tl[...] = part
        else:
            n.tl[...] += part

    def text_back(a):
        part = dot(n.tgr[...], n.tt[:, 1024 * a : 1024 * a + 1024])
        for b in range(4):
            n.t_s[a, b] = part[:, 256 * b : 256 * b + 256].astype(bf16)

    weights.forward()
    step(0)
    step(1)
    norm_y.forward()
    weights.finish()
    weights_z = RingGather(
        out, at, "z",
        lambda i, hf: n.wb.at[span(hf, 4), i, mine],
        lambda k: n.wb.at[:, pl.ds(0, k), mine],
        n.wz_m,
    )
    step(0)
    norm_z.forward()
    norm_y.finish()
    norm_x = RingGather(
        out, at, "x", lambda i, hf: n.nb.at[i, span(hf, 4)], lambda k: n.nb.at[pl.ds(0, k)], n.nx_m
    )
    step(1)
    weights_z.forward()
    step(0)
    n.tab[at.x] = n.au[at.s]
    tab_x = RingGather(
        out, at, "x", lambda i, hf: n.tab.at[i, span(hf, 128)], lambda k: n.tab.at[pl.ds(0, k)], n.tab_m
    )
    step(1)
    norm_z.finish()
    share = n.ns.at[:, at.c]
    wait_n = out.one(share, share, n.nc_m, at.sibling)
    weights_z.finish()
    for other in (weights.right, at.peer("x", 2)[0], weights.left):
        part = n.wb.at[other, :, mine]
        out.go(part, part, n.wc_m.at[0], n.wc_m.at[1], at.sibling)
    out.sent_later(n.wb.at[pl.ds(0, 3), :, mine], n.wc_m.at[0])
    wait_w = out.bytes_of(n.wb.at[pl.ds(0, 3), :, mine], n.wc_m.at[1])
    got_ids.wait_recv()
    i = lax.broadcasted_iota(jnp.int32, (128, 1024), 0)
    j = lax.broadcasted_iota(jnp.int32, (128, 1024), 1)
    same = ((i >> 6) == (j >> 9)) & (((i >> 2) & 15) == ((j >> 5) & 15)) & ((i & 3) == (j & 3))
    group = lax.broadcasted_iota(jnp.int32, (8, 1024), 0)
    j = lax.broadcasted_iota(jnp.int32, (8, 1024), 1)
    book = [at.s, jnp.maximum(at.s - 1, 0)]
    ids2 = [jnp.concatenate([n.idb[g, pl.ds(k, 1), :] for g in range(8)], axis=0) for k in book]
    spread = lax.dot_general(
        jnp.concatenate(ids2, axis=0).astype(f32), jnp.where(same, 1.0, 0.0), NN,
        precision=lax.Precision.HIGHEST, preferred_element_type=f32,
    )
    for i in range(2):
        own = jnp.where(((j >> 2) & 7) == group, spread[8 * i : 8 * i + 8], 0.0)
        n.idr[i] = jnp.sum(own, axis=0, keepdims=True).astype(jnp.int32)
    norm_x.forward()
    wait_w.wait_recv()
    step(0)
    step(1)
    wait_n.wait_recv()
    def transposed(b):
        rows = []
        for t in range(4):
            for s in range(8):
                index = 8 * lax.div(b, 4) + 2 * lax.rem(b, 4) + t // 2
                tile = unfold(n.ns[s // 2, s % 2, index], 2)
                rows.append(tile[4 * (t % 2) : 4 * (t % 2) + 4])
        cols = pl.ds(pl.multiple_of(128 * b, 128), 128)
        n.nt[:, cols] = jnp.concatenate(rows, axis=0).T.astype(bf16)

    loop(0, 8, transposed)
    step(0)
    tab_x.forward()
    step(1)
    norm_x.finish()
    loads[2].wait()
    text_piece(0)
    text_piece(1)
    step(0)
    text_piece(2)
    step(1)

    def two_blocks(to):
        return n.nb.at[lax.div(to, 2), pl.ds(2 * lax.rem(to, 2), 2)]

    n.ndst[at.s] = two_blocks(at.s)[...]
    got_nd = out.spread("s", 8, two_blocks, n.ndst.at[at.s], n.nd_m, n.ndst)
    for m in range(2):
        row = n.idr[0, :, pl.ds(pl.multiple_of(at.x * 128 + 512 * m, 128), 128)]
        held[m].hot = jnp.where(((row >> 7) & 3) == at.y, ((row >> 9) << 7) | (row & 127), -1)
    text_piece(3)
    tab_x.finish()
    step(0)
    text_piece(4)
    step(1)
    text_piece(5)
    step(0)
    step(1)
    text_piece(6)
    text_piece(7)
    tl = capped(n.tl[...])
    n.tl[...] = tl
    text_hot = lax.broadcasted_iota(jnp.int32, (VOCAB, 128), 0) == n.tid[...] - at.t * VOCAB
    tsum = jnp.sum(jnp.exp(tl - soft_cap), axis=0, keepdims=True)
    tchosen = jnp.sum(jnp.where(text_hot, tl, 0.0), axis=0, keepdims=True)
    n.ty[at.y] = jnp.concatenate([tsum, tchosen, jnp.zeros((6, 128), f32)], axis=0)
    got_ty = y_same(n.ty, n.ty_m)
    step(0)
    step(1)
    grads = jnp.concatenate([n.gr[0], n.gr[1]], axis=1)

    def vocab_grad(b):
        cols = pl.ds(pl.multiple_of(256 * b, 256), 256)
        g = dot(grads, n.ob[:, :, :, cols].reshape(256, 256))
        for a in range(4):
            n.g_s[a, :, cols] = g[128 * a : 128 * a + 128].astype(bf16)

    loop(0, 4, vocab_grad)
    red_g = reduce("x", "g", rows_half(64))
    got_ty.wait_recv()
    n.tx[at.x] = jnp.sum(n.ty[...], axis=0)
    got_tx = x_same(n.tx, n.tx_m)
    step(0)
    step(1)
    got_lc = seq_all(n.lc, n.lr, n.lc_m)
    n.lr[at.s] = n.lc[at.s]
    got_tx.wait_recv()
    ttotal = jnp.sum(n.tx[...], axis=0)
    tlse_row = soft_cap + jnp.log(ttotal[0:1, :])
    n.tlr[...] = tlse_row - ttotal[1:2, :]
    tl = n.tl[...]
    tgrad = (jnp.exp(tl - tlse_row) - jnp.where(text_hot, 1.0, 0.0)) * cap_slope(tl)
    padded = jnp.concatenate([tgrad, jnp.zeros((1024 - VOCAB, 128), f32)], axis=0)
    n.tg[at.z, at.c] = padded.astype(bf16)
    tg_z = RingGather(
        out, at, "z",
        lambda i, hf: n.tg.at[i, at.c, span(hf, 1024)],
        lambda k: n.tg.at[pl.ds(0, k), at.c],
        n.tgz_m,
    )
    n.tgr[...] = padded.T[:, 0:VOCAB].astype(bf16)
    step(0)
    text_back(0)
    step(1)
    red_g.forward()
    text_back(1)
    step(0)
    text_back(2)
    step(1)
    text_back(3)
    red_t = reduce("x", "t", rows_half(2))
    step(0)
    step(1)

    for c in range(4):
        n.trt[c] = n.tri[:, c].reshape(256, 256).astype(f32).T.astype(bf16)

    def weight_grad(zz):
        cols = pl.ds(pl.multiple_of(256 * zz, 256), 256)
        to = pl.ds(pl.multiple_of(128 * zz, 128), 128)
        g = dot(n.trt[0:3].reshape(768, 256), n.dob[0, :, :, :, cols].reshape(256, 256))
        last = dot(n.trt[3], n.dob[1, :, :, :, cols].reshape(256, 256))
        for core in range(2):
            for a in range(4):
                for c in range(4):
                    rows = last[64 * a : 64 * a + 64] if c == 3 else g[256 * c + 64 * a : 256 * c + 64 * a + 64]
                    n.gas[core, a, c, :, to] = rows[:, 128 * core : 128 * core + 128].astype(bf16)

    step(0)
    tg_z.forward()
    red_g.finish()
    g = red_g.total()
    for b in range(8):
        n.gts[b] = g[:, 128 * b : 128 * b + 128].astype(bf16)
    got_gt = seq_all(n.gts, n.gtr, n.gt_m)
    n.gtr[at.s] = n.gts[at.s]
    step(1)
    loop(0, 2, weight_grad)
    step(0)
    loop(2, 4, weight_grad)
    step(1)
    theirs = n.gas.at[1 - at.c]
    wait_gar = out.one(theirs, n.gar, n.gar_m, at.sibling)
    red_t.forward()
    term = held[0].gain_term + held[1].gain_term
    n.dgs[at.s] = jnp.concatenate([term[:, 128 * b : 128 * b + 128] for b in range(8)], axis=0)
    got_dgs = seq_same(n.dgs, n.dgs_m)
    got_lc.wait_recv()
    lane = lax.broadcasted_iota(jnp.int32, (16, 128), 1)
    for m in range(2):
        losses = jnp.zeros((16, 128), f32)
        for k in range(8):
            losses = jnp.where(lane == 1 + k, n.lr[k, m], losses)
        n.lx[at.x, m] = losses
    got_lx = x_same(n.lx, n.lx_m)
    tg_z.finish()
    share_t = n.tg.at[:, at.c]
    wait_t = out.one(share_t, share_t, n.tgc_m, at.sibling)
    step(0)

    def features(m):
        block = dot(n.ib[m].reshape(512, DD), n.pj[at.s], NT)
        for a in range(4):
            for s in range(8):
                lo = 128 * a + 4 * s
                rows = [block[lo + 32 * b : lo + 32 * b + 4] for b in range(4)]
                rows = jnp.concatenate(rows, axis=0).astype(bf16)
                n.sf[s % 2, s // 2, 64 * m + 16 * a : 64 * m + 16 * a + 16, :] = rows

    def hot_before(m):
        prev = jnp.where(at.s > 0, n.idr[1, :, 512 * m : 512 * m + 512] - at.t * 128, -1)
        entry = lax.broadcasted_iota(jnp.int32, (128, 512), 0)
        return jnp.where(prev == entry, 1.0, 0.0).astype(bf16)

    features(0)
    red_t.finish()
    for b in range(4):
        n.t2_s[b] = red_t.total(lambda ref: ref[b]).astype(bf16)
    red_t2 = reduce("y", "t2", rows_half(64))
    wait_gar.wait_recv()
    for a in range(4):
        n.ga_s[a] = (n.gas[at.c, a].astype(f32) + n.gar[a].astype(f32)).astype(bf16)
    red_ga = reduce("x", "ga", rows_half(2))
    left0 = jnp.concatenate([n.nt[:, 0:512], hot_before(0)], axis=0)

    def first_half(b):
        cols = pl.ds(pl.multiple_of(256 * b, 256), 256)
        g = dot(left0, n.ib[0, :, :, :, cols].reshape(512, 256))
        for i in range(3):
            n.raw[i, :, cols] = g[128 * i : 128 * i + 128]

    loop(0, 4, first_half)
    red_t2.forward()
    step(1)
    features(1)
    wait_sf = out.one(n.sf.at[1 - at.c], n.sfr, n.sfr_m, at.sibling)

    left1 = jnp.concatenate([n.nt[:, 512:1024], hot_before(1)], axis=0)

    def proj_grad(d):
        to = lax.rem(at.z + d, 4)
        cols = pl.ds(pl.multiple_of(to * 256, 256), 256)
        g = dot(left1, n.ib[1, :, :, :, cols].reshape(512, 256))
        g = g + jnp.concatenate([n.raw[i, :, cols] for i in range(3)], axis=0)
        g = jnp.concatenate([g[0:256], g[256:384] * embed_scale], axis=0)
        n.gas_all[2 * to, 0:384, :] = g[:, 0:128].astype(bf16)
        n.gas_all[2 * to + 1, 0:384, :] = g[:, 128:256].astype(bf16)

    def send_proj(d):
        proj_grad(d)
        to = lax.rem(at.z + d, 4)
        for core in range(2):
            src = n.gas_all.at[2 * to + core]
            out.go(src, n.gar_all.at[at.s], n.gall_m.at[0], n.gall_m.at[1], (to, core, at.x, at.y))

    (right, to_right), (far, _), (left, to_left) = [at.peer("z", d) for d in (1, 2, 3)]
    low, high = pl.ds(0, 192), pl.ds(192, 192)
    proj_grad(2)
    wait_sf.wait_recv()
    for b in range(4):
        n.f_s[b] = (n.sf[at.c, b].astype(f32) + n.sfr[b].astype(f32)).astype(bf16)
    red_f = direct("z", "f")
    for core in range(2):
        src = n.gas_all.at[2 * far + core]
        out.go(src.at[low], n.rel.at[0, core], n.rel_m.at[0], n.rel_m.at[1], to_right)
        out.go(src.at[high], n.rel.at[1, core], n.rel_m.at[0], n.rel_m.at[2], to_left)
    red_t2.finish()
    send_proj(1)
    send_proj(3)
    out.bytes_of(n.rel.at[0], n.rel_m.at[1]).wait_recv()
    out.bytes_of(n.rel.at[1], n.rel_m.at[2]).wait_recv()
    for core in range(2):
        there = n.gar_all.at[2 * left + at.c, low]
        out.go(n.rel.at[0, core], there, n.gall_m.at[0], n.gall_m.at[1], (right, core, at.x, at.y))
        there = n.gar_all.at[2 * right + at.c, high]
        out.go(n.rel.at[1, core], there, n.gall_m.at[0], n.gall_m.at[1], (left, core, at.x, at.y))
    out.sent_later(n.rel, n.rel_m.at[0])
    proj_grad(0)
    n.gar_all[at.s] = n.gas_all[at.s]
    theirs = 2 * at.z + 1 - at.c
    out.go(n.gas_all.at[theirs], n.gar_all.at[at.s], n.gall_m.at[0], n.gall_m.at[1], at.sibling)
    out.sent_later(n.gas_all.at[pl.ds(0, 7)], n.gall_m.at[0])
    got_all = out.bytes_of(n.gar_all.at[pl.ds(0, 7)], n.gall_m.at[1])
    red_f.finish()
    fb = red_t2.total() + red_f.total()
    gback = fb * gain
    inner = jnp.sum(gback * hat, axis=1, keepdims=True)
    n.rd[at.t] = jnp.broadcast_to(inner, (128, 128)).T[0:8, :]
    got_rd = plane_same(n.rd, n.rd_m)
    n.tgn[at.s] = jnp.broadcast_to(jnp.sum(fb * hat, axis=0, keepdims=True), (8, 256))
    got_tgn = seq_same(n.tgn, n.tgn_m)
    red_ga.forward()
    got_dgs.wait_recv()
    n.dgy[at.y] = jnp.sum(n.dgs[...], axis=0)
    got_dgy = y_same(n.dgy, n.dgy_m)

    wait_t.wait_recv()
    got_nd.wait_recv()

    def table_grad(a):
        part = pl.ds(pl.multiple_of(512 * a, 512), 512)
        left = jnp.concatenate([n.tg[g // 2, g % 2, part, :] for g in range(8)], axis=1)
        for b in range(2):
            right = n.ndst[:, b].reshape(1024, 256)
            n.o_gtt[part, 256 * b : 256 * b + 256] = dot(left, right).astype(bf16)

    loop(0, 2, table_grad)
    got_dgy.wait_recv()
    n.dgx[at.x] = jnp.sum(n.dgy[...], axis=0)
    got_dgx = x_same(n.dgx, n.dgx_m)
    red_ga.finish()
    for b in range(4):
        n.gz_s[b] = red_ga.total(lambda ref: ref[:, :, 128 * b : 128 * b + 128]).astype(bf16)
    red_gz = direct("z", "gz")
    got_rd.wait_recv()
    dots = twice(row_to_col(jnp.sum(n.rd[...], axis=0)[0:1, :], 128))
    n.o_gh[...] = scale * (gback - hat * (dots / D))
    got_tgn.wait_recv()
    n.o_tgain[...] = jnp.sum(n.tgn[...], axis=0)[0:1, :]
    got_lx.wait_recv()
    losses = jnp.concatenate([n.lx[a, m] for m in range(2) for a in range(4)], axis=0).T
    n.o_loss[...] = jnp.concatenate([n.tlr[...], losses[1:9]], axis=0)
    got_dgx.wait_recv()
    n.o_dg[...] = jnp.sum(n.dgx[...], axis=0)
    got_gt.wait_recv()
    got_all.wait_recv()
    n.o_gp[...] = n.gar_all[:, 0:256, :]
    for k in range(8):
        g = n.gtr[k].astype(f32)
        if k < 7:
            g = g + n.gar_all[k + 1, 256:384, :].astype(f32)
        n.o_gtab[k] = g
    red_gz.finish()
    ga = red_gz.total()
    n.o_gqkv[...] = ga[0:3]
    n.o_gout[...] = ga[3]
    out.finish()


def write_kernel(*refs):
    count = len(refs) // 2
    for src, dst in zip(refs[:count], refs[count:]):
        dst[...] = src[...].astype(f32)


def write_outputs(results):
    shapes = [r.shape for r in results]
    shapes[3] = (VOCAB, 512)
    blocks = {1: (64, 256), 3: (512, 512), 4: (4, 256, 128), 5: (4, 128, 128)}

    def spec(i):
        block = blocks.get(i, shapes[i])
        moves = i in blocks
        return pl.BlockSpec(block, lambda g: (g if moves else 0,) + (0,) * (len(block) - 1))

    return pl.pallas_call(
        write_kernel,
        out_shape=[jax.ShapeDtypeStruct(shape, f32) for shape in shapes],
        grid=(2,),
        in_specs=[spec(i) for i in range(9)],
        out_specs=[spec(i) for i in range(9)],
        name="write",
    )(*results)


def on_device(
    hidden, text_gain, text_table, proj, audio_table, depth_gain, attn_qkv, attn_out, text_ids, audio_ids
):
    vmem = pl.BlockSpec(memory_space=pltpu.VMEM)
    hbm = pl.BlockSpec(memory_space=pl.ANY)
    outs = [
        ((9, 128), f32), ((128, 256), f32), ((1, 256), f32), ((1024, 512), bf16), ((8, 256, 128), bf16),
        ((8, 128, 128), f32), ((8, 128), f32), ((3, 64, 128), f32), ((64, 128), f32),
    ]
    results = pl.pallas_call(
        kernel,
        out_shape=[jax.ShapeDtypeStruct(shape, dtype) for shape, dtype in outs],
        in_specs=[vmem, vmem, hbm, hbm, hbm, vmem, vmem, vmem, vmem, vmem],
        out_specs=[vmem] * len(outs),
        scratch_shapes=[scratch_shape(entry) for entry in SCRATCH],
        name="head",
        compiler_params=pltpu.CompilerParams(
            collective_id=1, has_side_effects=True, vmem_limit_bytes=VMEM_LIMIT
        ),
    )(
        hidden, text_gain, text_table, proj, audio_table, depth_gain,
        jnp.transpose(attn_qkv, (1, 2, 0)), attn_out, text_ids[None, :], audio_ids.T,
    )
    losses, gh, tgain, gtt, gp, gtab, dg, gqkv, gout = write_outputs(results)
    return losses.T, gh, tgain[0], gtt.T, gp, gtab, dg.reshape(DD), jnp.transpose(gqkv, (2, 0, 1)), gout


def solution(mesh):
    fine = Mesh(mesh.devices.reshape(4, 2, 4, 4), ("z", "core", "x", "y"))
    seq = ("z", "core")
    tp = ("x", "y")
    in_specs = (
        P(seq, tp), P(tp), P(tp, None), P(None, tp, None), P(None, tp, None),
        P(), P(None, None, tp), P(tp, None), P(seq), P(seq, None),
    )
    out_specs = (
        P(seq, None), P(seq, tp), P(tp), P(seq, tp), P(None, tp, seq),
        P(None, tp, seq), P(), P(seq, None, tp), P(tp, seq),
    )
    return jax.shard_map(
        on_device, mesh=fine, in_specs=in_specs, out_specs=out_specs, check_vma=False
    )
```

```python
import math

import jax
import jax.numpy as jnp
from jax import lax
from jax.experimental import pallas as pl
from jax.experimental.pallas import tpu as pltpu
from jax.sharding import Mesh
from jax.sharding import PartitionSpec as P

D = 4096
DD = 1024
HEAD = 64
VOCAB = 1000
MESH = pl.DeviceIdType.MESH
VMEM_LIMIT = 62 * 1024 * 1024

soft_cap = 12.0
epsilon = 1e-05
embed_scale = math.sqrt(DD) / 4.0
f32 = jnp.float32
bf16 = jnp.bfloat16

NN = (((1,), (0,)), ((), ()))
NT = (((1,), (1,)), ((), ()))
TN = (((0,), (0,)), ((), ()))


def dot(a, b, dims=NN):
    return lax.dot_general(a, b, dims, preferred_element_type=f32)


def capped(values):
    return soft_cap * jnp.tanh(values / soft_cap)


def cap_slope(capped_values):
    ratio = capped_values / soft_cap
    return 1.0 - ratio * ratio


class Place:
    def __init__(self):
        self.z = lax.axis_index("z")
        self.c = lax.axis_index("core")
        self.x = lax.axis_index("x")
        self.y = lax.axis_index("y")
        self.s = self.z * 2 + self.c
        self.t = self.x * 4 + self.y
        z, c, x, y = self.z, self.c, self.x, self.y
        self.sibling = (z, 1 - c, x, y)
        self.known = {}
        for d in range(1, 4):
            to = lax.rem(x + d, 4)
            self.known["x", d] = (to, (z, c, to, y))
            to = lax.rem(y + d, 4)
            self.known["y", d] = (to, (z, c, x, to))
            to = lax.rem(z + d, 4)
            self.known["z", d] = (to, (to, c, x, y))
        for d in range(1, 8):
            to = lax.rem(self.s + d, 8)
            self.known["s", d] = (to, (lax.div(to, 2), lax.rem(to, 2), x, y))
        for d in range(1, 16):
            to = lax.rem(self.t + d, 16)
            self.known["t", d] = (to, (z, c, lax.div(to, 4), lax.rem(to, 4)))

    def peer(self, axis, d):
        return self.known[axis, d]

    def index(self, axis):
        return {"x": self.x, "y": self.y, "z": self.z, "s": self.s, "t": self.t}[axis]


class Sends:
    def __init__(self, at):
        self.at = at
        self.pending = []

    def go(self, src, dst, send, recv, device):
        pltpu.make_async_remote_copy(
            src_ref=src, dst_ref=dst, send_sem=send, recv_sem=recv, device_id=device, device_id_type=MESH
        ).start()

    def bytes_of(self, ref, sem):
        return pltpu.make_async_remote_copy(
            src_ref=ref, dst_ref=ref, send_sem=sem, recv_sem=sem,
            device_id=self.at.sibling, device_id_type=MESH,
        )

    def sent_later(self, ref, sem):
        self.pending.append(self.bytes_of(ref, sem))

    def one(self, src, dst, sems, device):
        self.go(src, dst, sems.at[0], sems.at[1], device)
        self.sent_later(src, sems.at[0])
        return self.bytes_of(dst, sems.at[1])

    def spread(self, axis, n, src, dst, sems, slots, all_bytes=None):
        for d in range(1, n):
            to, device = self.at.peer(axis, d)
            self.go(src(to), dst, sems.at[0], sems.at[1], device)
        if all_bytes is None:
            all_bytes = slots.at[pl.ds(0, n - 1)]
        self.sent_later(all_bytes, sems.at[0])
        return self.bytes_of(all_bytes, sems.at[1])

    def finish(self):
        for wait in self.pending:
            wait.wait_send()


class RingGather:
    def __init__(self, out, at, axis, part, slots, sems):
        self.out, self.part, self.sems, self.slots = out, part, sems, slots
        self.right, self.to_right = at.peer(axis, 1)
        self.left, self.to_left = at.peer(axis, 3)
        block = part(at.index(axis), None)
        out.go(block, block, sems.at[0], sems.at[1], self.to_right)
        out.go(block, block, sems.at[0], sems.at[2], self.to_left)
        out.sent_later(slots(3), sems.at[0])

    def forward(self):
        out, part, sems = self.out, self.part, self.sems
        out.bytes_of(part(self.left, None), sems.at[1]).wait_recv()
        one = part(self.left, 0)
        out.go(one, one, sems.at[0], sems.at[3], self.to_right)
        out.bytes_of(part(self.right, None), sems.at[2]).wait_recv()
        two = part(self.right, 1)
        out.go(two, two, sems.at[0], sems.at[3], self.to_left)

    def finish(self):
        self.out.bytes_of(self.slots(1), self.sems.at[3]).wait_recv()


class RingReduce:
    def __init__(self, out, at, axis, blocks, half, bufs, sems):
        self.out, self.half, self.sems, self.blocks = out, half, sems, blocks
        self.me, far = at.index(axis), at.peer(axis, 2)[0]
        self.right, self.to_right = at.peer(axis, 1)
        self.left, self.to_left = at.peer(axis, 3)
        self.rl, self.rr, self.fa, self.fb = bufs
        s = blocks
        out.go(half(s.at[far], 0), self.fa, sems.at[0], sems.at[1], self.to_right)
        out.go(half(s.at[far], 1), self.fb, sems.at[0], sems.at[2], self.to_left)
        out.go(half(s.at[self.right], 1), half(self.rl, 1), sems.at[0], sems.at[3], self.to_right)
        out.go(half(s.at[self.left], 0), half(self.rr, 0), sems.at[0], sems.at[3], self.to_left)
        out.sent_later(s.at[pl.ds(0, 3)], sems.at[0])

    def forward(self):
        s, half, out, sems = self.blocks, self.half, self.out, self.sems
        out.bytes_of(self.fa, sems.at[1]).wait_recv()
        one = half(s.at[self.right], 0)
        one[...] = (one[...].astype(f32) + self.fa[...].astype(f32)).astype(bf16)
        out.go(one, half(self.rl, 0), sems.at[0], sems.at[3], self.to_right)
        out.bytes_of(self.fb, sems.at[2]).wait_recv()
        two = half(s.at[self.left], 1)
        two[...] = (two[...].astype(f32) + self.fb[...].astype(f32)).astype(bf16)
        out.go(two, half(self.rr, 1), sems.at[0], sems.at[3], self.to_left)

    def finish(self):
        self.out.bytes_of(self.blocks.at[pl.ds(0, 2)], self.sems.at[3]).wait_recv()

    def total(self, pick=lambda ref: ref[...]):
        own = pick(self.blocks.at[self.me]).astype(f32)
        return own + pick(self.rl).astype(f32) + pick(self.rr).astype(f32)


class DirectReduce:
    def __init__(self, out, at, axis, blocks, got, sems):
        self.blocks, self.got = blocks, got
        self.me = at.index(axis)
        for d in (2, 1, 3):
            to, device = at.peer(axis, d)
            out.go(blocks.at[to], got.at[d - 1], sems.at[0], sems.at[1], device)
        out.sent_later(blocks.at[pl.ds(0, 3)], sems.at[0])
        self.wait = out.bytes_of(got, sems.at[1])

    def finish(self):
        self.wait.wait_recv()

    def total(self, pick=lambda ref: ref[...]):
        own = pick(self.blocks.at[self.me]).astype(f32)
        for d in range(3):
            own = own + pick(self.got.at[d]).astype(f32)
        return own


def span(h, size):
    if h is None:
        return pl.ds(0, size)
    return pl.ds(h * (size // 2), size // 2)


def rows_half(n):
    return lambda ref, h: ref.at[pl.ds(h * n, n)]


def row_to_col(row, lanes):
    return jnp.broadcast_to(row, (lanes, row.shape[1])).T


def twice(col):
    return jnp.concatenate([col, col], axis=1)


def fold(rows, n):
    w = rows.shape[1] // n
    return jnp.concatenate([rows[:, i * w : i * w + w] for i in range(n)], axis=0).astype(bf16)


def unfold(packed, n):
    r = packed.shape[0] // n
    wide = packed.astype(f32)
    return jnp.concatenate([wide[i * r : i * r + r] for i in range(n)], axis=1)


def by_step(rows):
    return [fold(rows[4 * k : 4 * k + 4], 4) for k in range(8)]


def from_steps(ref):
    return jnp.concatenate([unfold(ref[k], 4) for k in range(8)], axis=0)


def head_masks(rows):
    lane = lax.broadcasted_iota(jnp.int32, (rows, 256), 1)
    return [(lane >= 64 * h) & (lane < 64 * h + 64) for h in range(4)]


def step_mask():
    i = lax.broadcasted_iota(jnp.int32, (128, 128), 0)
    j = lax.broadcasted_iota(jnp.int32, (128, 128), 1)
    return ((i & 3) == (j & 3)) & ((i >> 5) == (j >> 5)) & (j <= i)


def attention(qh, kk, allowed):
    scores = dot(qh, kk, NT) / math.sqrt(HEAD)
    raised = jnp.where(allowed, jnp.exp(scores), 0.0)
    return raised / jnp.sum(raised, axis=1, keepdims=True)


def ring_reduce_scratch(name, block, half):
    return [
        (name + "_s", (4,) + block, bf16),
        (name + "_rl", block, bf16),
        (name + "_rr", block, bf16),
        (name + "_fa", half, bf16),
        (name + "_fb", half, bf16),
        (name + "_m", 4, None),
    ]


def direct_scratch(name, block):
    return [(name + "_s", (4,) + block, bf16), (name + "_r", (3,) + block, bf16), (name + "_m", 2, None)]


def chain_scratch(m):
    m = str(m)
    return [
        *ring_reduce_scratch("p" + m, (4, 16, DD), (2, 16, DD)),
        *ring_reduce_scratch("q" + m, (4, 16, DD), (2, 16, DD)),
        *direct_scratch("pp" + m, (16, DD)),
        *direct_scratch("qq" + m, (16, DD)),
        ("dn_m" + m, 2, None),
        *direct_scratch("h" + m, (32, DD)),
        ("a1s" + m, (8, 16, 256), bf16), ("a1r" + m, (8, 16, 256), bf16), ("a1_m" + m, 2, None),
        ("a2s" + m, (8, 16, 256), bf16), ("a2r" + m, (8, 16, 256), bf16), ("a2_m" + m, 2, None),
        ("a3s" + m, (8, 16, 256), bf16), ("a3r" + m, (8, 16, 256), bf16), ("a3_m" + m, 2, None),
        ("ob_m" + m, 2, None), ("e" + m, (4, 8, 128), f32), ("e_m" + m, 2, None),
        *direct_scratch("v" + m, (32, DD)),
        *direct_scratch("c" + m, (32, DD)),
        ("obb_m" + m, 2, None),
    ]


SCRATCH = [
    ("tt", (VOCAB, D), bf16), ("pj", (8, 256, DD), bf16), ("au", (8, 128, DD), bf16), ("load", 3, 0),
    ("ssq", (16, 8, 128), f32), ("ssq_m", 2, None),
    ("idb", (8, 8, 128), jnp.int32), ("idb_m", 2, None), ("idr", (2, 1, 1024), jnp.int32),
    ("raw", (8, 128, DD), f32), ("look", (8, 128, DD), bf16),
    ("wb", (4, 4, 64, DD), bf16), ("wb_m", 4, None), ("wz_m", 4, None), ("wc_m", 2, None),
    ("nb", (4, 4, 128, 256), bf16), ("ny_m", 4, None), ("nx_m", 4, None),
    ("ns", (4, 2, 16, 16, 128), bf16), ("nz_m", 4, None), ("nc_m", 2, None),
    *chain_scratch(0), *chain_scratch(1),
    ("dob", (2, 2, 4, 32, DD), bf16), ("qkv", (2, 3, 128, 256), bf16),
    ("ex", (2, 4, 128, 128), f32), ("ob", (2, 4, 32, DD), bf16),
    ("gr", (2, 512, 128), bf16), ("tri", (2, 4, 128, 256), bf16), ("trt", (4, 256, 256), bf16),
    ("tab", (4, 128, DD), bf16), ("tab_m", 4, None),
    ("tl", (VOCAB, 128), f32), ("ty", (4, 8, 128), f32), ("ty_m", 2, None), ("tx", (4, 8, 128), f32), ("tx_m", 2, None),
    ("tgr", (128, VOCAB), bf16), ("tlr", (1, 128), f32),
    *ring_reduce_scratch("g", (128, DD), (64, DD)),
    ("lc", (8, 2, 16, 128), f32), ("lr", (8, 2, 16, 128), f32), ("lc_m", 2, None),
    ("lx", (4, 2, 16, 128), f32), ("lx_m", 2, None),
    ("nt", (256, 1024), bf16), ("tg", (4, 2, 1024, 128), bf16), ("tgz_m", 4, None), ("tgc_m", 2, None),
    *ring_reduce_scratch("t", (4, 128, 256), (2, 128, 256)),
    *ring_reduce_scratch("t2", (128, 256), (64, 256)),
    ("ndst", (8, 2, 128, 256), bf16), ("nd_m", 2, None),
    ("ib", (2, 4, 4, 32, DD), bf16), ("i0x_m", 2, None), ("i0y_m", 4, None),
    ("iax_m", 2, None), ("iay_m", 4, None), ("ibx_m", 4, None), ("iby_m", 2, None),
    ("gas", (2, 4, 4, 64, 512), bf16), ("gar", (4, 4, 64, 512), bf16), ("gar_m", 2, None),
    *ring_reduce_scratch("ga", (4, 64, 512), (2, 64, 512)),
    *direct_scratch("gz", (4, 64, 128)),
    ("sf", (2, 4, 128, 256), bf16), ("sfr", (4, 128, 256), bf16), ("sfr_m", 2, None),
    *direct_scratch("f", (128, 256)),
    ("gas_all", (8, 384, 128), bf16), ("gar_all", (8, 384, 128), bf16), ("gall_m", 2, None),
    ("rel", (2, 2, 192, 128), bf16), ("rel_m", 3, None),
    ("gts", (8, 128, 128), bf16), ("gtr", (8, 128, 128), bf16), ("gt_m", 2, None),
    ("dgs", (8, 8, 128), f32), ("dgs_m", 2, None), ("dgy", (4, 8, 128), f32), ("dgy_m", 2, None),
    ("dgx", (4, 8, 128), f32), ("dgx_m", 2, None),
    ("rd", (16, 8, 128), f32), ("rd_m", 2, None), ("tgn", (8, 8, 256), f32), ("tgn_m", 2, None),
]


def scratch_shape(entry):
    name, shape, dtype = entry
    if dtype is None or isinstance(dtype, int):
        return pltpu.SemaphoreType.DMA((shape,))
    return pltpu.VMEM(shape, dtype)


class Named:
    pass


def loop(low, high, body):
    def one(i, carry):
        body(i)
        return carry

    lax.fori_loop(low, high, one, 0)


INPUTS = ["hid", "gain", "table", "proj", "audio", "dgain", "wqkv", "wout", "tid", "ids"]
OUTPUTS = ["o_loss", "o_gh", "o_tgain", "o_gtt", "o_gp", "o_gtab", "o_dg", "o_gqkv", "o_gout"]


def kernel(*refs):
    n = Named()
    names = INPUTS + OUTPUTS + [entry[0] for entry in SCRATCH]
    for name, ref in zip(names, refs):
        setattr(n, name, ref)
    at = Place()
    out = Sends(at)

    def reduce(axis, name, half):
        bufs = [getattr(n, name + suffix) for suffix in ("_rl", "_rr", "_fa", "_fb")]
        return RingReduce(out, at, axis, getattr(n, name + "_s"), half, bufs, getattr(n, name + "_m"))

    def direct(axis, name):
        return DirectReduce(
            out, at, axis, getattr(n, name + "_s"), getattr(n, name + "_r"), getattr(n, name + "_m")
        )

    def seq_all(src, dst, sems):
        return out.spread("s", 8, lambda to: src.at[to], dst.at[at.s], sems, dst)

    def seq_same(ref, sems):
        return out.spread("s", 8, lambda to: ref.at[at.s], ref.at[at.s], sems, ref)

    def plane_same(ref, sems):
        return out.spread("t", 16, lambda to: ref.at[at.t], ref.at[at.t], sems, ref)

    def x_same(ref, sems):
        return out.spread("x", 4, lambda to: ref.at[at.x], ref.at[at.x], sems, ref)

    def y_same(ref, sems):
        return out.spread("y", 4, lambda to: ref.at[at.y], ref.at[at.y], sems, ref)

    loads = [
        pltpu.make_async_copy(src, dst, n.load.at[i])
        for i, (src, dst) in enumerate([(n.audio, n.au), (n.proj, n.pj), (n.table, n.tt)])
    ]
    for copy in loads:
        copy.start()
    for c in range(3):
        n.wb[at.x, c] = n.wqkv[c]
    n.wb[at.x, 3] = n.wout[...]
    barrier = pltpu.get_barrier_semaphore()
    for axis, count in (("t", 16), ("s", 8)):
        for d in range(1, count):
            device = at.peer(axis, d)[1]
            pl.semaphore_signal(barrier, inc=1, device_id=device, device_id_type=MESH)
    h = n.hid[...].astype(f32)
    gain = n.gain[...].astype(f32)[None, :]
    dgain = n.dgain[...].astype(f32)[None, :]
    ones = jnp.ones((8, 256), f32)
    n.ssq[at.t] = lax.dot_general(
        ones, h * h, NT, precision=lax.Precision.HIGHEST, preferred_element_type=f32
    )
    n.idb[at.s] = n.ids[...]
    unscaled = (h * gain).astype(bf16)
    loads[0].wait()
    entry = (lax.broadcasted_iota(jnp.int32, (128, 128), 1) + at.t * 128).astype(f32)
    n.look[0] = jnp.zeros((128, DD), bf16)

    def look_step(k):
        column = row_to_col(n.ids[pl.ds(k, 1), :].astype(f32), 128)
        hot = jnp.where(column == entry, 1.0, 0.0).astype(bf16)
        n.look[k + 1] = (dot(hot, n.au[k]) * embed_scale).astype(bf16)

    loop(0, 7, look_step)
    pl.semaphore_wait(barrier, 22)

    got_ssq = plane_same(n.ssq, n.ssq_m)
    mine = pl.ds(pl.multiple_of(at.c * 32, 32), 32)
    weights = RingGather(
        out, at, "x",
        lambda i, hf: n.wb.at[i, at.z, mine] if hf is None
        else n.wb.at[i, at.z, pl.ds(pl.multiple_of(at.c * 32 + 16 * hf, 16), 16)],
        lambda k: n.wb.at[pl.ds(0, k), at.z, mine],
        n.wb_m,
    )
    got_ids = seq_same(n.idb, n.idb_m)
    loads[1].wait()

    def raw_step(k):
        n.raw[k] = dot(unscaled, n.pj[k])

    loop(0, 8, raw_step)
    got_ssq.wait_recv()
    scale = row_to_col(lax.rsqrt(jnp.sum(n.ssq[...], axis=0)[0:1, :] / D + epsilon), 128)
    column = scale[:, 0:1]
    scale = twice(scale)
    hat = h * scale

    first = []
    for m in range(2):
        ps, qs = getattr(n, f"p{m}_s"), getattr(n, f"q{m}_s")
        part = slice(64 * m, 64 * m + 64)

        def scaled(k):
            return n.raw[k, part, :] * column[part] + n.look[k, part, :].astype(f32)

        def to_x(k):
            p = scaled(k)
            for b in range(4):
                ps[b, k] = p[16 * b : 16 * b + 16].astype(bf16)

        def to_y(k):
            p = scaled(k + 4)
            for b in range(4):
                rows = [p[16 * a + 4 * b : 16 * a + 4 * b + 4] for a in range(4)]
                qs[b, k] = jnp.concatenate(rows, axis=0).astype(bf16)

        loop(0, 4, to_x)
        red_p = reduce("x", f"p{m}", rows_half(2))
        loop(0, 4, to_y)
        first.append((red_p, reduce("y", f"q{m}", rows_half(2))))
    normed_f = hat * gain
    n.nb[at.x, at.y] = normed_f.astype(bf16)
    for b in range(16):
        n.ns[at.z, at.c, b] = fold(normed_f[8 * b : 8 * b + 8], 2)
    norm_z = RingGather(
        out, at, "z",
        lambda i, hf: n.ns.at[i, at.c, span(hf, 16)],
        lambda k: n.ns.at[pl.ds(0, k), at.c],
        n.nz_m,
    )
    norm_y = RingGather(
        out, at, "y",
        lambda i, hf: n.nb.at[at.x, i, span(hf, 128)],
        lambda k: n.nb.at[at.x, pl.ds(0, k)],
        n.ny_m,
    )

    masks = head_masks(128)
    allowed = step_mask()
    held = [Named(), Named()]

    def wcat(c):
        return jnp.concatenate([n.wb[a, c] for a in range(4)], axis=0)

    def half_of(m, name):
        return getattr(n, name + str(m))

    def chain(m):
        mine = held[m]
        red_p, red_q = first[m]
        red_p.forward()
        red_q.forward()
        yield
        for red, to, axis in ((red_p, "pp", "y"), (red_q, "qq", "x")):
            red.finish()
            total = [red.total(lambda ref: ref[k]) for k in range(4)]
            for b in range(4):
                rows = [total[k][4 * b : 4 * b + 4] for k in range(4)]
                getattr(n, f"{to}{m}_s")[b] = jnp.concatenate(rows, axis=0).astype(bf16)
            if axis == "y":
                red_pp = direct("y", f"pp{m}")
            else:
                red_qq = direct("x", f"qq{m}")
        yield
        red_pp.finish()
        red_qq.finish()
        di = jnp.concatenate([red_pp.total(), red_qq.total()], axis=0)
        mine.dscale = lax.rsqrt(jnp.mean(di * di, axis=1, keepdims=True) + epsilon)
        mine.dhat = di * mine.dscale
        n.dob[0, m, at.y] = (mine.dhat * dgain).astype(bf16)
        got = y_same(n.dob.at[0, m], half_of(m, "dn_m"))
        yield
        got.wait_recv()
        dnv = n.dob[0, m].reshape(128, DD)
        for c in range(3):
            n.qkv[m, c] = dot(dnv, wcat(c), NT).astype(bf16)
        q, k, v = n.qkv[m, 0], n.qkv[m, 1], n.qkv[m, 2]
        mixed = jnp.zeros((128, 256), f32)
        for hd in range(4):
            qh = jnp.where(masks[hd], q, jnp.zeros_like(q))
            exact = attention(qh, k, allowed)
            n.ex[m, hd] = exact
            mixed = jnp.where(masks[hd], dot(exact.astype(bf16), v), mixed)
        n.tri[m, 3] = mixed.astype(bf16)
        terms = dot(n.tri[m, 3], wcat(3))
        for b in range(4):
            getattr(n, f"h{m}_s")[b] = terms[32 * b : 32 * b + 32].astype(bf16)
        red_h = direct("y", f"h{m}")
        yield
        red_h.finish()
        src, dst = half_of(m, "a1s"), half_of(m, "a1r")
        for k, block in enumerate(by_step(di + red_h.total())):
            src[k] = block
        got = seq_all(src, dst, half_of(m, "a1_m"))
        dst[at.s] = src[at.s]
        yield
        got.wait_recv()
        n.ob[m, at.y] = from_steps(dst).astype(bf16)
        got = y_same(n.ob.at[m], half_of(m, "ob_m"))
        yield
        got.wait_recv()
        rows = n.ob[m].reshape(128, DD)
        tab = n.tab[...].reshape(512, DD)
        logits = capped(dot(tab, rows, NT))
        hot = mine.hot == lax.broadcasted_iota(jnp.int32, (512, 128), 0)
        sums = jnp.sum(jnp.exp(logits - soft_cap), axis=0, keepdims=True)
        chosen = jnp.sum(jnp.where(hot, logits, 0.0), axis=0, keepdims=True)
        e = half_of(m, "e")
        e[at.y] = jnp.concatenate([sums, chosen, jnp.zeros((6, 128), f32)], axis=0)
        got = y_same(e, half_of(m, "e_m"))
        yield
        got.wait_recv()
        total = jnp.sum(e[...], axis=0)
        lse_row = soft_cap + jnp.log(total[0:1, :])
        grad = (jnp.exp(logits - lse_row) - jnp.where(hot, 1.0, 0.0)) * cap_slope(logits)
        n.gr[m] = grad.astype(bf16)
        terms = dot(grad.T.astype(bf16), tab)
        for b in range(4):
            getattr(n, f"v{m}_s")[b] = terms[32 * b : 32 * b + 32].astype(bf16)
        red_v = direct("y", f"v{m}")
        loss = row_to_col(lse_row - total[1:2, :], 128)
        for g in range(8):
            rows = [loss[32 * b + 4 * g : 32 * b + 4 * g + 4] for b in range(4)]
            n.lc[g, m] = jnp.concatenate(rows, axis=0)
        yield
        red_v.finish()
        src, dst = half_of(m, "a2s"), half_of(m, "a2r")
        for k, block in enumerate(by_step(red_v.total())):
            src[k] = block
        got = seq_all(src, dst, half_of(m, "a2_m"))
        dst[at.s] = src[at.s]
        yield
        got.wait_recv()
        output_back = from_steps(dst)
        n.dob[1, m, at.y] = output_back.astype(bf16)
        got = y_same(n.dob.at[1, m], half_of(m, "obb_m"))
        yield
        got.wait_recv()
        g = dot(n.dob[1, m].reshape(128, DD), wcat(3), NT).astype(bf16)
        q, k, v = n.qkv[m, 0], n.qkv[m, 1], n.qkv[m, 2]
        dq = jnp.zeros((128, 256), f32)
        dk = jnp.zeros((128, 256), f32)
        dv = jnp.zeros((128, 256), f32)
        for hd in range(4):
            gh = jnp.where(masks[hd], g, jnp.zeros_like(g))
            exact = n.ex[m, hd]
            dw = dot(gh, v, NT).astype(bf16).astype(f32)
            ds = exact * (dw - jnp.sum(dw * exact, axis=1, keepdims=True)) / math.sqrt(HEAD)
            dv = jnp.where(masks[hd], dot(exact.T.astype(bf16), g), dv)
            dq = jnp.where(masks[hd], dot(ds.astype(bf16), k), dq)
            dk = jnp.where(masks[hd], dot(ds.T.astype(bf16), q), dk)
        n.tri[m, 0] = dq.astype(bf16)
        n.tri[m, 1] = dk.astype(bf16)
        n.tri[m, 2] = dv.astype(bf16)
        terms = dot(n.tri[m, 0], wcat(0)) + dot(n.tri[m, 1], wcat(1)) + dot(n.tri[m, 2], wcat(2))
        for b in range(4):
            getattr(n, f"c{m}_s")[b] = terms[32 * b : 32 * b + 32].astype(bf16)
        red_c = direct("y", f"c{m}")
        yield
        red_c.finish()
        nback = red_c.total()
        mine.gain_term = jnp.sum(nback * mine.dhat, axis=0, keepdims=True)
        hback = nback * dgain
        inner = jnp.mean(hback * mine.dhat, axis=1, keepdims=True)
        ib = output_back + mine.dscale * (hback - mine.dhat * inner)
        src, dst = half_of(m, "a3s"), half_of(m, "a3r")
        for k, block in enumerate(by_step(ib)):
            src[k] = block
        got = seq_all(src, dst, half_of(m, "a3_m"))
        dst[at.s] = src[at.s]
        yield
        got.wait_recv()
        n.ib[m, at.x, at.y] = from_steps(dst).astype(bf16)

        def part(axis, where, sems):
            return RingGather(out, at, axis, where, lambda k: where(pl.ds(0, k), None), sems)

        def spread(axis, mine_is, where, sems):
            src = where(mine_is)
            return out.spread(axis, 4, lambda to: src, src, sems, None, where(pl.ds(0, 3)))

        low, high = pl.ds(0, 16), pl.ds(16, 16)
        ib = n.ib.at[m]
        if m == 0:
            one = [spread("x", at.x, lambda i: ib.at[i, at.y], n.i0x_m)]
        else:
            one = [
                spread("x", at.x, lambda i: ib.at[i, at.y, low], n.iax_m),
                spread("y", at.y, lambda i: ib.at[at.x, i, high], n.iby_m),
            ]
        yield
        one[0].wait_recv()
        if m == 0:
            two = [part("y", lambda i, hf: ib.at[:, i, :, span(hf, DD)], n.i0y_m)]
        else:
            two = [part("y", lambda i, hf: ib.at[:, i, low, span(hf, DD)], n.iay_m)]
            one[1].wait_recv()
            two.append(part("x", lambda i, hf: ib.at[i, :, high, span(hf, DD)], n.ibx_m))
        yield
        for ring in two:
            ring.forward()
        yield
        for ring in two:
            ring.finish()
        yield

    run = [chain(0), chain(1)]

    def step(m):
        next(run[m])

    def text_piece(i):
        feats = jnp.concatenate([n.nb[i // 2, 2 * (i % 2) + b] for b in range(2)], axis=1)
        part = dot(n.tt[:, 512 * i : 512 * i + 512], feats, NT)
        if i == 0:
            n.tl[...] = part
        else:
            n.tl[...] += part

    def text_back(a):
        part = dot(n.tgr[...], n.tt[:, 1024 * a : 1024 * a + 1024])
        for b in range(4):
            n.t_s[a, b] = part[:, 256 * b : 256 * b + 256].astype(bf16)

    weights.forward()
    step(0)
    step(1)
    norm_y.forward()
    weights.finish()
    weights_z = RingGather(
        out, at, "z",
        lambda i, hf: n.wb.at[span(hf, 4), i, mine],
        lambda k: n.wb.at[:, pl.ds(0, k), mine],
        n.wz_m,
    )
    step(0)
    norm_z.forward()
    norm_y.finish()
    norm_x = RingGather(
        out, at, "x", lambda i, hf: n.nb.at[i, span(hf, 4)], lambda k: n.nb.at[pl.ds(0, k)], n.nx_m
    )
    step(1)
    weights_z.forward()
    step(0)
    n.tab[at.x] = n.au[at.s]
    tab_x = RingGather(
        out, at, "x", lambda i, hf: n.tab.at[i, span(hf, 128)], lambda k: n.tab.at[pl.ds(0, k)], n.tab_m
    )
    step(1)
    norm_z.finish()
    share = n.ns.at[:, at.c]
    wait_n = out.one(share, share, n.nc_m, at.sibling)
    weights_z.finish()
    for other in (weights.right, at.peer("x", 2)[0], weights.left):
        part = n.wb.at[other, :, mine]
        out.go(part, part, n.wc_m.at[0], n.wc_m.at[1], at.sibling)
    out.sent_later(n.wb.at[pl.ds(0, 3), :, mine], n.wc_m.at[0])
    wait_w = out.bytes_of(n.wb.at[pl.ds(0, 3), :, mine], n.wc_m.at[1])
    got_ids.wait_recv()
    i = lax.broadcasted_iota(jnp.int32, (128, 1024), 0)
    j = lax.broadcasted_iota(jnp.int32, (128, 1024), 1)
    same = ((i >> 6) == (j >> 9)) & (((i >> 2) & 15) == ((j >> 5) & 15)) & ((i & 3) == (j & 3))
    group = lax.broadcasted_iota(jnp.int32, (8, 1024), 0)
    j = lax.broadcasted_iota(jnp.int32, (8, 1024), 1)
    book = [at.s, jnp.maximum(at.s - 1, 0)]
    ids2 = [jnp.concatenate([n.idb[g, pl.ds(k, 1), :] for g in range(8)], axis=0) for k in book]
    spread = lax.dot_general(
        jnp.concatenate(ids2, axis=0).astype(f32), jnp.where(same, 1.0, 0.0), NN,
        precision=lax.Precision.HIGHEST, preferred_element_type=f32,
    )
    for i in range(2):
        own = jnp.where(((j >> 2) & 7) == group, spread[8 * i : 8 * i + 8], 0.0)
        n.idr[i] = jnp.sum(own, axis=0, keepdims=True).astype(jnp.int32)
    norm_x.forward()
    wait_w.wait_recv()
    step(0)
    step(1)
    wait_n.wait_recv()
    def transposed(b):
        rows = []
        for t in range(4):
            for s in range(8):
                index = 8 * lax.div(b, 4) + 2 * lax.rem(b, 4) + t // 2
                tile = unfold(n.ns[s // 2, s % 2, index], 2)
                rows.append(tile[4 * (t % 2) : 4 * (t % 2) + 4])
        cols = pl.ds(pl.multiple_of(128 * b, 128), 128)
        n.nt[:, cols] = jnp.concatenate(rows, axis=0).T.astype(bf16)

    loop(0, 8, transposed)
    step(0)
    tab_x.forward()
    step(1)
    norm_x.finish()
    loads[2].wait()
    text_piece(0)
    step(0)
    text_piece(1)
    step(1)

    def two_blocks(to):
        return n.nb.at[lax.div(to, 2), pl.ds(2 * lax.rem(to, 2), 2)]

    n.ndst[at.s] = two_blocks(at.s)[...]
    got_nd = out.spread("s", 8, two_blocks, n.ndst.at[at.s], n.nd_m, n.ndst)
    for m in range(2):
        row = n.idr[0, :, pl.ds(pl.multiple_of(at.x * 128 + 512 * m, 128), 128)]
        held[m].hot = jnp.where(((row >> 7) & 3) == at.y, ((row >> 9) << 7) | (row & 127), -1)
    tab_x.finish()
    text_piece(2)
    step(0)
    step(1)
    text_piece(3)
    step(0)
    text_piece(4)
    step(1)
    text_piece(5)
    step(0)
    text_piece(6)
    step(1)
    text_piece(7)
    tl = capped(n.tl[...])
    n.tl[...] = tl
    text_hot = lax.broadcasted_iota(jnp.int32, (VOCAB, 128), 0) == n.tid[...] - at.t * VOCAB
    tsum = jnp.sum(jnp.exp(tl - soft_cap), axis=0, keepdims=True)
    tchosen = jnp.sum(jnp.where(text_hot, tl, 0.0), axis=0, keepdims=True)
    n.ty[at.y] = jnp.concatenate([tsum, tchosen, jnp.zeros((6, 128), f32)], axis=0)
    got_ty = y_same(n.ty, n.ty_m)
    step(0)
    step(1)
    got_ty.wait_recv()
    n.tx[at.x] = jnp.sum(n.ty[...], axis=0)
    got_tx = x_same(n.tx, n.tx_m)
    got_lc = seq_all(n.lc, n.lr, n.lc_m)
    n.lr[at.s] = n.lc[at.s]
    grads = jnp.concatenate([n.gr[0], n.gr[1]], axis=1)

    def vocab_grad(b):
        cols = pl.ds(pl.multiple_of(256 * b, 256), 256)
        g = dot(grads, n.ob[:, :, :, cols].reshape(256, 256))
        for a in range(4):
            n.g_s[a, :, cols] = g[128 * a : 128 * a + 128].astype(bf16)

    loop(0, 4, vocab_grad)
    red_g = reduce("x", "g", rows_half(64))
    step(0)
    got_tx.wait_recv()
    ttotal = jnp.sum(n.tx[...], axis=0)
    tlse_row = soft_cap + jnp.log(ttotal[0:1, :])
    n.tlr[...] = tlse_row - ttotal[1:2, :]
    tl = n.tl[...]
    tgrad = (jnp.exp(tl - tlse_row) - jnp.where(text_hot, 1.0, 0.0)) * cap_slope(tl)
    padded = jnp.concatenate([tgrad, jnp.zeros((1024 - VOCAB, 128), f32)], axis=0)
    n.tg[at.z, at.c] = padded.astype(bf16)
    tg_z = RingGather(
        out, at, "z",
        lambda i, hf: n.tg.at[i, at.c, span(hf, 1024)],
        lambda k: n.tg.at[pl.ds(0, k), at.c],
        n.tgz_m,
    )
    n.tgr[...] = padded.T[:, 0:VOCAB].astype(bf16)
    step(1)
    red_g.forward()
    text_back(0)
    step(0)
    text_back(1)
    step(1)
    text_back(2)
    step(0)
    text_back(3)
    red_t = reduce("x", "t", rows_half(2))
    step(1)

    for c in range(4):
        n.trt[c] = n.tri[:, c].reshape(256, 256).astype(f32).T.astype(bf16)

    def weight_grad(zz):
        cols = pl.ds(pl.multiple_of(256 * zz, 256), 256)
        to = pl.ds(pl.multiple_of(128 * zz, 128), 128)
        g = dot(n.trt[0:3].reshape(768, 256), n.dob[0, :, :, :, cols].reshape(256, 256))
        last = dot(n.trt[3], n.dob[1, :, :, :, cols].reshape(256, 256))
        for core in range(2):
            for a in range(4):
                for c in range(4):
                    rows = last[64 * a : 64 * a + 64] if c == 3 else g[256 * c + 64 * a : 256 * c + 64 * a + 64]
                    n.gas[core, a, c, :, to] = rows[:, 128 * core : 128 * core + 128].astype(bf16)

    step(0)
    tg_z.forward()
    red_g.finish()
    g = red_g.total()
    for b in range(8):
        n.gts[b] = g[:, 128 * b : 128 * b + 128].astype(bf16)
    got_gt = seq_all(n.gts, n.gtr, n.gt_m)
    n.gtr[at.s] = n.gts[at.s]
    step(1)
    loop(0, 2, weight_grad)
    step(0)
    loop(2, 4, weight_grad)
    step(1)
    theirs = n.gas.at[1 - at.c]
    wait_gar = out.one(theirs, n.gar, n.gar_m, at.sibling)
    red_t.forward()
    term = held[0].gain_term + held[1].gain_term
    n.dgs[at.s] = jnp.concatenate([term[:, 128 * b : 128 * b + 128] for b in range(8)], axis=0)
    got_dgs = seq_same(n.dgs, n.dgs_m)
    got_lc.wait_recv()
    lane = lax.broadcasted_iota(jnp.int32, (16, 128), 1)
    for m in range(2):
        losses = jnp.zeros((16, 128), f32)
        for k in range(8):
            losses = jnp.where(lane == 1 + k, n.lr[k, m], losses)
        n.lx[at.x, m] = losses
    got_lx = x_same(n.lx, n.lx_m)
    tg_z.finish()
    share_t = n.tg.at[:, at.c]
    wait_t = out.one(share_t, share_t, n.tgc_m, at.sibling)
    step(0)

    def features(m):
        block = dot(n.ib[m].reshape(512, DD), n.pj[at.s], NT)
        for a in range(4):
            for s in range(8):
                lo = 128 * a + 4 * s
                rows = [block[lo + 32 * b : lo + 32 * b + 4] for b in range(4)]
                rows = jnp.concatenate(rows, axis=0).astype(bf16)
                n.sf[s % 2, s // 2, 64 * m + 16 * a : 64 * m + 16 * a + 16, :] = rows

    def hot_before(m):
        prev = jnp.where(at.s > 0, n.idr[1, :, 512 * m : 512 * m + 512] - at.t * 128, -1)
        entry = lax.broadcasted_iota(jnp.int32, (128, 512), 0)
        return jnp.where(prev == entry, 1.0, 0.0).astype(bf16)

    features(0)
    red_t.finish()
    for b in range(4):
        n.t2_s[b] = red_t.total(lambda ref: ref[b]).astype(bf16)
    red_t2 = reduce("y", "t2", rows_half(64))
    wait_gar.wait_recv()
    for a in range(4):
        n.ga_s[a] = (n.gas[at.c, a].astype(f32) + n.gar[a].astype(f32)).astype(bf16)
    red_ga = reduce("x", "ga", rows_half(2))
    left0 = jnp.concatenate([n.nt[:, 0:512], hot_before(0)], axis=0)

    def first_half(b):
        cols = pl.ds(pl.multiple_of(256 * b, 256), 256)
        g = dot(left0, n.ib[0, :, :, :, cols].reshape(512, 256))
        for i in range(3):
            n.raw[i, :, cols] = g[128 * i : 128 * i + 128]

    loop(0, 4, first_half)
    red_t2.forward()
    step(1)
    features(1)
    wait_sf = out.one(n.sf.at[1 - at.c], n.sfr, n.sfr_m, at.sibling)

    left1 = jnp.concatenate([n.nt[:, 512:1024], hot_before(1)], axis=0)

    def proj_grad(d):
        to = lax.rem(at.z + d, 4)
        cols = pl.ds(pl.multiple_of(to * 256, 256), 256)
        g = dot(left1, n.ib[1, :, :, :, cols].reshape(512, 256))
        g = g + jnp.concatenate([n.raw[i, :, cols] for i in range(3)], axis=0)
        g = jnp.concatenate([g[0:256], g[256:384] * embed_scale], axis=0)
        n.gas_all[2 * to, 0:384, :] = g[:, 0:128].astype(bf16)
        n.gas_all[2 * to + 1, 0:384, :] = g[:, 128:256].astype(bf16)

    def send_proj(d):
        proj_grad(d)
        to = lax.rem(at.z + d, 4)
        for core in range(2):
            src = n.gas_all.at[2 * to + core]
            out.go(src, n.gar_all.at[at.s], n.gall_m.at[0], n.gall_m.at[1], (to, core, at.x, at.y))

    (right, to_right), (far, _), (left, to_left) = [at.peer("z", d) for d in (1, 2, 3)]
    low, high = pl.ds(0, 192), pl.ds(192, 192)
    proj_grad(2)
    wait_sf.wait_recv()
    for b in range(4):
        n.f_s[b] = (n.sf[at.c, b].astype(f32) + n.sfr[b].astype(f32)).astype(bf16)
    red_f = direct("z", "f")
    for core in range(2):
        src = n.gas_all.at[2 * far + core]
        out.go(src.at[low], n.rel.at[0, core], n.rel_m.at[0], n.rel_m.at[1], to_right)
        out.go(src.at[high], n.rel.at[1, core], n.rel_m.at[0], n.rel_m.at[2], to_left)
    red_t2.finish()
    send_proj(1)
    send_proj(3)
    out.bytes_of(n.rel.at[0], n.rel_m.at[1]).wait_recv()
    out.bytes_of(n.rel.at[1], n.rel_m.at[2]).wait_recv()
    for core in range(2):
        there = n.gar_all.at[2 * left + at.c, low]
        out.go(n.rel.at[0, core], there, n.gall_m.at[0], n.gall_m.at[1], (right, core, at.x, at.y))
        there = n.gar_all.at[2 * right + at.c, high]
        out.go(n.rel.at[1, core], there, n.gall_m.at[0], n.gall_m.at[1], (left, core, at.x, at.y))
    out.sent_later(n.rel, n.rel_m.at[0])
    proj_grad(0)
    n.gar_all[at.s] = n.gas_all[at.s]
    theirs = 2 * at.z + 1 - at.c
    out.go(n.gas_all.at[theirs], n.gar_all.at[at.s], n.gall_m.at[0], n.gall_m.at[1], at.sibling)
    out.sent_later(n.gas_all.at[pl.ds(0, 7)], n.gall_m.at[0])
    got_all = out.bytes_of(n.gar_all.at[pl.ds(0, 7)], n.gall_m.at[1])
    red_f.finish()
    fb = red_t2.total() + red_f.total()
    gback = fb * gain
    inner = jnp.sum(gback * hat, axis=1, keepdims=True)
    n.rd[at.t] = jnp.broadcast_to(inner, (128, 128)).T[0:8, :]
    got_rd = plane_same(n.rd, n.rd_m)
    n.tgn[at.s] = jnp.broadcast_to(jnp.sum(fb * hat, axis=0, keepdims=True), (8, 256))
    got_tgn = seq_same(n.tgn, n.tgn_m)
    red_ga.forward()
    got_dgs.wait_recv()
    n.dgy[at.y] = jnp.sum(n.dgs[...], axis=0)
    got_dgy = y_same(n.dgy, n.dgy_m)

    wait_t.wait_recv()
    got_nd.wait_recv()

    def table_grad(a):
        part = pl.ds(pl.multiple_of(512 * a, 512), 512)
        left = jnp.concatenate([n.tg[g // 2, g % 2, part, :] for g in range(8)], axis=1)
        for b in range(2):
            right = n.ndst[:, b].reshape(1024, 256)
            n.o_gtt[part, 256 * b : 256 * b + 256] = dot(left, right).astype(bf16)

    loop(0, 2, table_grad)
    got_dgy.wait_recv()
    n.dgx[at.x] = jnp.sum(n.dgy[...], axis=0)
    got_dgx = x_same(n.dgx, n.dgx_m)
    red_ga.finish()
    for b in range(4):
        n.gz_s[b] = red_ga.total(lambda ref: ref[:, :, 128 * b : 128 * b + 128]).astype(bf16)
    red_gz = direct("z", "gz")
    got_rd.wait_recv()
    dots = twice(row_to_col(jnp.sum(n.rd[...], axis=0)[0:1, :], 128))
    n.o_gh[...] = scale * (gback - hat * (dots / D))
    got_tgn.wait_recv()
    n.o_tgain[...] = jnp.sum(n.tgn[...], axis=0)[0:1, :]
    got_lx.wait_recv()
    losses = jnp.concatenate([n.lx[a, m] for m in range(2) for a in range(4)], axis=0).T
    n.o_loss[...] = jnp.concatenate([n.tlr[...], losses[1:9]], axis=0)
    got_dgx.wait_recv()
    n.o_dg[...] = jnp.sum(n.dgx[...], axis=0)
    got_gt.wait_recv()
    got_all.wait_recv()
    n.o_gp[...] = n.gar_all[:, 0:256, :]
    for k in range(8):
        g = n.gtr[k].astype(f32)
        if k < 7:
            g = g + n.gar_all[k + 1, 256:384, :].astype(f32)
        n.o_gtab[k] = g
    red_gz.finish()
    ga = red_gz.total()
    n.o_gqkv[...] = ga[0:3]
    n.o_gout[...] = ga[3]
    out.finish()


def write_kernel(*refs):
    count = len(refs) // 2
    for src, dst in zip(refs[:count], refs[count:]):
        dst[...] = src[...].astype(f32)


def write_outputs(results):
    shapes = [r.shape for r in results]
    shapes[3] = (VOCAB, 512)
    blocks = {1: (64, 256), 3: (512, 512), 4: (4, 256, 128), 5: (4, 128, 128)}

    def spec(i):
        block = blocks.get(i, shapes[i])
        moves = i in blocks
        return pl.BlockSpec(block, lambda g: (g if moves else 0,) + (0,) * (len(block) - 1))

    return pl.pallas_call(
        write_kernel,
        out_shape=[jax.ShapeDtypeStruct(shape, f32) for shape in shapes],
        grid=(2,),
        in_specs=[spec(i) for i in range(9)],
        out_specs=[spec(i) for i in range(9)],
        name="write",
    )(*results)


def on_device(
    hidden, text_gain, text_table, proj, audio_table, depth_gain, attn_qkv, attn_out, text_ids, audio_ids
):
    vmem = pl.BlockSpec(memory_space=pltpu.VMEM)
    hbm = pl.BlockSpec(memory_space=pl.ANY)
    outs = [
        ((9, 128), f32), ((128, 256), f32), ((1, 256), f32), ((1024, 512), bf16), ((8, 256, 128), bf16),
        ((8, 128, 128), f32), ((8, 128), f32), ((3, 64, 128), f32), ((64, 128), f32),
    ]
    results = pl.pallas_call(
        kernel,
        out_shape=[jax.ShapeDtypeStruct(shape, dtype) for shape, dtype in outs],
        in_specs=[vmem, vmem, hbm, hbm, hbm, vmem, vmem, vmem, vmem, vmem],
        out_specs=[vmem] * len(outs),
        scratch_shapes=[scratch_shape(entry) for entry in SCRATCH],
        name="head",
        compiler_params=pltpu.CompilerParams(
            collective_id=1, has_side_effects=True, vmem_limit_bytes=VMEM_LIMIT
        ),
    )(
        hidden, text_gain, text_table, proj, audio_table, depth_gain,
        jnp.transpose(attn_qkv, (1, 2, 0)), attn_out, text_ids[None, :], audio_ids.T,
    )
    losses, gh, tgain, gtt, gp, gtab, dg, gqkv, gout = write_outputs(results)
    return losses.T, gh, tgain[0], gtt.T, gp, gtab, dg.reshape(DD), jnp.transpose(gqkv, (2, 0, 1)), gout


def solution(mesh):
    fine = Mesh(mesh.devices.reshape(4, 2, 4, 4), ("z", "core", "x", "y"))
    seq = ("z", "core")
    tp = ("x", "y")
    in_specs = (
        P(seq, tp), P(tp), P(tp, None), P(None, tp, None), P(None, tp, None),
        P(), P(None, None, tp), P(tp, None), P(seq), P(seq, None),
    )
    out_specs = (
        P(seq, None), P(seq, tp), P(tp), P(seq, tp), P(None, tp, seq),
        P(None, tp, seq), P(), P(seq, None, tp), P(tp, seq),
    )
    return jax.shard_map(
        on_device, mesh=fine, in_specs=in_specs, out_specs=out_specs, check_vma=False
    )
```
